128 devices in a mesh: dp: 8 (over y, core), tp: 16 (over z, x).
Axes of the slice: x: 4, y: 4, z: 4, core: 2. Of those that a mesh axis runs over, the one named last changes fastest.
Arguments:
- old_cache: bfloat16 [256, 3072, 576], P('dp', 'tp'), may hold values from -8 to 8, as said below
- lengths: int32 [256], replicated, may hold values from 384 to 3070, as said below
- new_slot: int32 [256], replicated, may hold values from 0 to 255, as said below
- queries: bfloat16 [2, 256, 128, 576], P(None, ('dp', 'tp')), may hold values from -100 to 100
- new_latent: bfloat16 [2, 256, 576], P(None, ('dp', 'tp')), may hold values from -6 to 6
- hidden: bfloat16 [2, 256, 7168], P(None, None, 'dp'), may hold values from -6 to 6
- value_up_weight: bfloat16 [128, 512, 128], P('tp'), may hold values from -1 to 1
- w_out: bfloat16 [16384, 7168], P('tp', 'dp'), may hold values from -0.046875 to 0.046875
- norm_gain: bfloat16 [7168], P('dp'), may hold values from 0.099609375 to 1.8984375
- w_gate: bfloat16 [7168, 18432], P('dp', 'tp'), may hold values from -0.0625 to 0.0625
- w_up: bfloat16 [7168, 18432], P('dp', 'tp'), may hold values from -0.0625 to 0.0625
- w_down: bfloat16 [18432, 7168], P('tp', 'dp'), may hold values from -0.046875 to 0.046875
Outputs:
- new_cache: bfloat16 [256, 3072, 576], P(('dp', 'tp'))
- layer_out: bfloat16 [2, 256, 7168], P(None, None, 'dp')
The draws below stay inside these ranges and needn't reach their ends.
Inputs may be any that keep to these rules, and one draw needn't show every extreme that they name: A permutation. Request r moves to device new_slot[r] // 2 (dp slowest) in new group new_slot[r] // 32; exactly 4 requests of each old group go to each new group, and they take that group's slots from (r // 32) * 4 to (r // 32) * 4 + 3. `lengths`: the largest is exactly 3070. `old_cache`: rows at or past a request's length carry no meaning.
All inputs are finite; a program needn't handle non-finite values.
Results may differ from the reference program's by a relative error of at most 0.0075.
Values may be sent and summed in bfloat16 or wider, within the bound.
A program may use at most 128 MiB of HBM per device.

```python
import jax
import jax.numpy as jnp
from jax import lax

D = 7168
FF = 18432
HEADS = 128
KV_RANK = 512
V_DIM = 128
CTX = 3072
STEPS = 2
R = 256
GROUP_REQ = 32
MOVE = 4
LATENT_WIDTH = 576
N_DP = 8


def request_layout(key):
    sub_key = jax.random.fold_in(key, 101)
    dest_key, order_key, length_key, longest_key = jax.random.split(sub_key, 4)
    pattern = jnp.arange(GROUP_REQ, dtype=jnp.int32) % N_DP
    group_keys = jax.random.split(dest_key, N_DP)
    dest_group = jax.vmap(lambda one_key: jax.random.permutation(one_key, pattern))(group_keys).reshape(R)
    old_group = jnp.arange(R, dtype=jnp.int32) // GROUP_REQ
    priority = jax.random.permutation(order_key, R).astype(jnp.int32)
    before = (dest_group[None, :] == dest_group[:, None]) & (old_group[None, :] == old_group[:, None]) & (priority[None, :] < priority[:, None])
    pair_index = jnp.sum(before.astype(jnp.int32), axis=1)
    slots = (dest_group * GROUP_REQ + old_group * MOVE + pair_index).astype(jnp.int32)
    spans = jax.random.randint(length_key, (R,), CTX // 8, CTX - STEPS + 1)
    longest = jax.random.randint(longest_key, (), 0, R)
    spans = jnp.where(jnp.arange(R) == longest, CTX - STEPS, spans).astype(jnp.int32)
    return (slots, spans)


def cache_row(cache_key, index):
    return jax.random.normal(jax.random.fold_in(cache_key, index), (LATENT_WIDTH,), jnp.float32)


def draw_new_slot(key, part):
    return request_layout(key)[0]


def draw_lengths(key, part):
    return request_layout(key)[1]


def draw_old_cache(key, part):
    cache_key = jax.random.fold_in(key, 202)
    indices = jnp.arange(R * CTX, dtype=jnp.int32)
    cached_row_list = jax.vmap(lambda index: cache_row(cache_key, index))(indices)
    return cached_row_list.reshape(R, CTX, LATENT_WIDTH).astype(jnp.bfloat16)


def draw_queries(key, part):
    own_key = jax.random.fold_in(key, 303)
    noise_key = jax.random.fold_in(own_key, 0)
    base = jax.random.normal(noise_key, (STEPS, R, HEADS, LATENT_WIDTH), jnp.float32)
    return base.astype(jnp.bfloat16)


def block_scale(key, shape, cuts, smallest, top_value):
    factor_of = 1.0
    for position, blocks in cuts:
        draws = jax.random.uniform(jax.random.fold_in(jax.random.fold_in(key, 6), position), (blocks,), jnp.float32, smallest / len(cuts), top_value / len(cuts))
        factor_of = factor_of * jnp.repeat(jnp.exp(draws), shape[position] // blocks).reshape((-1,) + (1,) * (len(shape) - 1 - position))
    return factor_of


def noise(stream_key, shape, scale, bound, cuts=(), kind=jnp.bfloat16):
    values = scale * jax.random.normal(stream_key, shape, jnp.float32)
    if cuts:
        values = values * block_scale(stream_key, shape, cuts, -0.22, 0.18)
    return jnp.clip(values, -bound, bound).astype(kind)


def setup_inputs(seed: int = 0) -> dict:
    keys = jax.random.split(jax.random.key(seed), 13)
    return {
        "old_cache": draw_old_cache(jax.random.fold_in(keys[12], 71), 0),
        "lengths": draw_lengths(jax.random.fold_in(keys[12], 71), 0),
        "new_slot": draw_new_slot(jax.random.fold_in(keys[12], 71), 0),
        "queries": draw_queries(jax.random.fold_in(keys[12], 71), 0),
        "new_latent": noise(keys[4], (STEPS, R, LATENT_WIDTH), 1.0, 6.0, ((1, 128),)),
        "hidden": noise(keys[5], (STEPS, R, D), 1.0, 6.0, ((2, 8),)),
        "value_up_weight": noise(keys[6], (HEADS, KV_RANK, V_DIM), (KV_RANK // 16) ** -0.5, 1.0, ((0, 16),)),
        "w_out": noise(keys[7], (HEADS * V_DIM, D), (HEADS * V_DIM) ** -0.5, 0.046875, ((0, 16), (1, 8))),
        "norm_gain": jnp.clip(1.0 + 0.18 * jax.random.normal(keys[8], (D,), jnp.float32), 0.099609375, 1.8984375).astype(jnp.bfloat16),
        "w_gate": noise(keys[9], (D, FF), D ** -0.5, 0.0625, ((0, 8), (1, 16))),
        "w_up": noise(keys[10], (D, FF), D ** -0.5, 0.0625, ((0, 8), (1, 16))),
        "w_down": noise(keys[11], (FF, D), FF ** -0.5, 0.046875, ((0, 16), (1, 8))),
    }


score_scale = 0.07216878364870323
norm_eps = 1e-06

def attend_one(query_row, key_rows, last_pos):
    raw_scores = jnp.dot(query_row, key_rows.T, preferred_element_type=jnp.float32) * score_scale
    positions = jnp.arange(key_rows.shape[0], dtype=jnp.int32)
    masked = jnp.where(positions[None, :] <= last_pos, raw_scores, -jnp.inf)
    row_max = lax.optimization_barrier(jnp.max(masked, axis=1, keepdims=True))
    exponent = jnp.exp(masked - row_max)
    row_total = lax.optimization_barrier(jnp.sum(exponent, axis=1, keepdims=True))
    weights = (exponent / row_total).astype(jnp.bfloat16)
    return jnp.dot(weights, key_rows[:, :KV_RANK], preferred_element_type=jnp.float32).astype(jnp.bfloat16)

def reference(old_cache, lengths, new_slot, queries, new_latent, hidden, value_up_weight, w_out, norm_gain, w_gate, w_up, w_down):
    everyone = jnp.arange(R, dtype=jnp.int32)
    source = jnp.zeros((R,), jnp.int32).at[new_slot].set(everyone)
    kv_cache = old_cache[source]
    new_len = lengths[source]
    for step_no in range(STEPS):
        kv_cache = kv_cache.at[everyone, new_len + step_no].set(new_latent[step_no])
    positions = jnp.arange(CTX, dtype=jnp.int32)
    new_cache = jnp.where(positions[None, :, None] < (new_len + STEPS)[:, None, None], kv_cache, jnp.zeros((), jnp.bfloat16))
    results = []
    gain = norm_gain.astype(jnp.float32)
    for step_no in range(STEPS):
        latent_vectors = lax.map(lambda item: attend_one(item[0], item[1], item[2]), (queries[step_no], new_cache, new_len + step_no))
        expanded_values = jnp.einsum('fty,typ->ftp', latent_vectors.astype(jnp.float32), value_up_weight.astype(jnp.float32))
        expanded_values = expanded_values.astype(jnp.bfloat16).reshape(R, HEADS * V_DIM)
        after_attn = hidden[step_no].astype(jnp.float32) + jnp.dot(expanded_values, w_out, preferred_element_type=jnp.float32)
        squares = lax.optimization_barrier(jnp.sum(after_attn * after_attn, axis=1))
        normed = (after_attn / jnp.sqrt(squares / D + norm_eps)[:, None] * gain).astype(jnp.bfloat16)
        gate_part = jnp.dot(normed, w_gate, preferred_element_type=jnp.float32)
        up_part = jnp.dot(normed, w_up, preferred_element_type=jnp.float32)
        hidden_act = (jax.nn.silu(gate_part) * up_part).astype(jnp.bfloat16)
        ffn_out = jnp.dot(hidden_act, w_down, preferred_element_type=jnp.float32)
        results.append((after_attn + ffn_out).astype(jnp.bfloat16))
    return (new_cache, jnp.stack(results))
```

```python
import functools

import jax
import jax.numpy as jnp
from jax import lax
from jax.experimental import pallas as pl
from jax.experimental.pallas import tpu as pltpu
from jax.sharding import PartitionSpec as P

D = 7168


MESH = pl.DeviceIdType.MESH


def loop(low, high, action):
    def body(i, carry):
        action(i)
        return carry

    lax.fori_loop(low, high, body, 0)


def move_kernel(n_dp, n_tp, chunks, picked, cache, out, loaded, stage, mid, load_sem, own_sem, send1, recv1, send2, recv2):
    group_req, piece, _ = loaded.shape
    per_pair = group_req // n_dp
    per_dev = group_req // n_tp
    rows = piece // chunks
    g = lax.axis_index("dp")
    c = lax.axis_index("tp")
    load = pltpu.make_async_copy(cache, loaded, load_sem)
    load.start()
    barrier = pltpu.get_barrier_semaphore()

    def greet_dp(i):
        pl.semaphore_signal(barrier, 1, device_id=(lax.rem(g + i, n_dp), c), device_id_type=MESH)

    def greet_tp(i):
        pl.semaphore_signal(barrier, 1, device_id=(g, lax.rem(c + i, n_tp)), device_id_type=MESH)

    loop(1, n_dp, greet_dp)
    loop(1, n_tp, greet_tp)
    pl.semaphore_wait(barrier, n_dp + n_tp - 2)
    load.wait()

    def sort(i):
        stage[i] = loaded[picked[i]]

    loop(0, group_req, sort)

    def keep(i):
        mid[per_pair * g + i] = stage[per_pair * g + i]

    loop(0, per_pair, keep)

    def over_dp(q, i, from_group):
        to_group = lax.rem(g + i, n_dp)
        part = pl.ds(q * rows, rows)
        return pltpu.make_async_remote_copy(
            src_ref=stage.at[pl.ds(per_pair * to_group, per_pair), part],
            dst_ref=mid.at[pl.ds(per_pair * from_group, per_pair), part],
            send_sem=send1.at[q, to_group],
            recv_sem=recv1.at[q, from_group],
            device_id=(to_group, c),
            device_id_type=MESH,
        )

    def over_tp(q, i, from_column):
        to_column = lax.rem(c + i, n_tp)
        return pltpu.make_async_remote_copy(
            src_ref=mid.at[pl.ds(per_dev * to_column, per_dev), pl.ds(q * rows, rows)],
            dst_ref=out.at[:, pl.ds(from_column * piece + q * rows, rows)],
            send_sem=send2.at[q, to_column],
            recv_sem=recv2.at[q, from_column],
            device_id=(g, to_column),
            device_id_type=MESH,
        )

    def own(q):
        return pltpu.make_async_copy(
            mid.at[pl.ds(per_dev * c, per_dev), pl.ds(q * rows, rows)],
            out.at[:, pl.ds(c * piece + q * rows, rows)],
            own_sem.at[q],
        )

    ahead = 2
    for q in range(chunks + 1):
        if q < chunks:
            if q >= ahead:
                loop(1, n_dp, lambda i: over_dp(q - ahead, i, g).wait_send())
            loop(1, n_dp, lambda i: over_dp(q, i, g).start())
        if q >= 1:
            loop(1, n_dp, lambda i: over_dp(q - 1, i, lax.rem(g + n_dp - i, n_dp)).wait_recv())
            loop(1, n_tp, lambda i: over_tp(q - 1, i, c).start())
            own(q - 1).start()
    for q in range(chunks):
        if q >= chunks - ahead:
            loop(1, n_dp, lambda i: over_dp(q, i, g).wait_send())
        loop(1, n_tp, lambda i: over_tp(q, i, c).wait_send())
        loop(1, n_tp, lambda i: over_tp(q, i, lax.rem(c + n_tp - i, n_tp)).wait_recv())
        own(q).wait()


def move(picked, old_cache, n_dp, n_tp):
    group_req, piece, width = old_cache.shape
    chunks = 12
    sems = pltpu.SemaphoreType.DMA
    return pl.pallas_call(
        functools.partial(move_kernel, n_dp, n_tp, chunks),
        out_shape=jax.ShapeDtypeStruct((group_req // n_tp, piece * n_tp, width), old_cache.dtype),
        in_specs=[pl.BlockSpec(memory_space=pltpu.SMEM), pl.BlockSpec(memory_space=pl.ANY)],
        out_specs=pl.BlockSpec(memory_space=pl.ANY),
        scratch_shapes=[
            pltpu.VMEM(old_cache.shape, old_cache.dtype),
            pltpu.VMEM(old_cache.shape, old_cache.dtype),
            pltpu.VMEM(old_cache.shape, old_cache.dtype),
            sems,
            sems((chunks,)),
            sems((chunks, n_dp)),
            sems((chunks, n_dp)),
            sems((chunks, n_tp)),
            sems((chunks, n_tp)),
        ],
        compiler_params=pltpu.CompilerParams(collective_id=0, has_side_effects=True, vmem_limit_bytes=48 * 2**20),
    )(picked, old_cache)


score_scale = 0.07216878364870323
norm_eps = 1e-06


def attend_blocks(query_row, key_rows, last_pos, kv_rank):
    context = key_rows.shape[0]
    raw_all = (
        jnp.einsum("hc,pc->hp", query_row, key_rows, preferred_element_type=jnp.float32)
        * score_scale
    )
    offsets = jnp.arange(context, dtype=jnp.int32)
    masked = jnp.where(offsets[None, :] <= last_pos, raw_all, -jnp.inf)
    row_max = jnp.max(masked, axis=1, keepdims=True)
    exponent = jnp.exp(masked - row_max)
    row_total = jnp.sum(exponent, axis=1, keepdims=True)
    weights = (exponent / row_total).astype(jnp.bfloat16)
    accum = jnp.dot(weights, key_rows[:, :kv_rank], preferred_element_type=jnp.float32)
    return accum.astype(jnp.bfloat16)


def normalize(rows_in, gain):
    squares = lax.psum(jnp.sum(rows_in * rows_in, axis=1), "dp")
    return (rows_in / jnp.sqrt(squares / D + norm_eps)[:, None] * gain).astype(jnp.bfloat16)


def feed_forward(normed, w_gate, w_up, w_down):
    gate_local = jnp.dot(normed, w_gate, preferred_element_type=jnp.float32)
    up_local = jnp.dot(normed, w_up, preferred_element_type=jnp.float32)
    gate_part, up_part = lax.psum((gate_local, up_local), "dp")
    hidden_act = (jax.nn.silu(gate_part) * up_part).astype(jnp.bfloat16)
    return jnp.dot(hidden_act, w_down, preferred_element_type=jnp.float32)


def tp_whole(terms):
    return lax.psum(terms, "tp")


def shards(
    old_cache,
    lengths,
    new_slot,
    queries,
    new_latent,
    hidden,
    value_up_weight,
    w_out,
    norm_gain,
    w_gate,
    w_up,
    w_down,
):
    dp_count = lax.axis_size("dp")
    tp_count = lax.axis_size("tp")
    my_group = lax.axis_index("dp")
    my_column = lax.axis_index("tp")
    group_req, piece_len, lat_width = old_cache.shape
    per_pair = group_req // dp_count
    step_count = queries.shape[0]
    req_dev = queries.shape[1]
    req_total = new_slot.shape[0]
    context = piece_len * tp_count
    kv_rank = value_up_weight.shape[1]
    everyone = jnp.arange(req_total, dtype=jnp.int32)
    new_group = new_slot // group_req
    pair_rank = new_slot % group_req - everyone // group_req * per_pair
    my_targets = lax.dynamic_slice_in_dim(
        new_group * per_pair + pair_rank, my_group * group_req, group_req
    )
    target_places = jnp.arange(group_req, dtype=jnp.int32)
    picked = jnp.sum(
        jnp.where(my_targets[None, :] == target_places[:, None], target_places[None, :], 0), axis=1
    )
    arrived = move(picked, old_cache, dp_count, tp_count)
    source = jnp.sum(
        jnp.where(new_slot[None, :] == everyone[:, None], everyone[None, :], 0), axis=1
    )
    my_slots = (my_group * tp_count + my_column) * req_dev + jnp.arange(req_dev, dtype=jnp.int32)
    my_lengths = jnp.take(lengths, jnp.take(source, my_slots))
    positions = jnp.arange(context, dtype=jnp.int32)
    kv_cache = arrived
    for step_no in range(step_count):
        kv_cache = jnp.where(
            positions[None, :, None] == (my_lengths + step_no)[:, None, None],
            new_latent[step_no][:, None, :],
            kv_cache,
        )
    new_cache = jnp.where(
        positions[None, :, None] < (my_lengths + step_count)[:, None, None],
        kv_cache,
        jnp.zeros((), jnp.bfloat16),
    )
    gain = norm_gain.astype(jnp.float32)
    results = []
    for step_no in range(step_count):
        latent_vectors = jnp.stack(
            [
                attend_blocks(
                    queries[step_no, item], kv_cache[item], my_lengths[item] + step_no, kv_rank
                )
                for item in range(req_dev)
            ]
        )
        spread_rows = lax.all_to_all(latent_vectors, "tp", split_axis=1, concat_axis=0, tiled=True)
        expanded_values = jnp.einsum(
            "fty,typ->ftp", spread_rows, value_up_weight, preferred_element_type=jnp.float32
        )
        expanded_values = expanded_values.astype(jnp.bfloat16).reshape(group_req, -1)
        head_terms = jnp.dot(
            lax.all_gather(expanded_values, "dp", axis=0, tiled=True),
            w_out,
            preferred_element_type=jnp.float32,
        )
        residual = hidden[step_no].astype(jnp.float32)
        after_attn = residual + tp_whole(head_terms)
        normed = normalize(after_attn, gain)
        ffn_out = tp_whole(feed_forward(normed, w_gate, w_up, w_down))
        layer_row_block = (after_attn + ffn_out).astype(jnp.bfloat16)
        results.append(layer_row_block)
    return (new_cache, jnp.stack(results))


def solution(mesh):
    in_specs = (
        P("dp", "tp", None),
        P(),
        P(),
        P(None, ("dp", "tp"), None, None),
        P(None, ("dp", "tp"), None),
        P(None, None, "dp"),
        P("tp", None, None),
        P("tp", "dp"),
        P("dp"),
        P("dp", "tp"),
        P("dp", "tp"),
        P("tp", "dp"),
    )
    out_specs = (P(("dp", "tp"), None, None), P(None, None, "dp"))
    return jax.shard_map(shards, mesh=mesh, in_specs=in_specs, out_specs=out_specs, check_vma=False)
```

```python
import functools

import jax
import jax.numpy as jnp
from jax import lax
from jax.experimental import pallas as pl
from jax.experimental.pallas import tpu as pltpu
from jax.sharding import PartitionSpec as P

D = 7168


MESH = pl.DeviceIdType.MESH


def loop(low, high, action):
    def body(i, carry):
        action(i)
        return carry

    lax.fori_loop(low, high, body, 0)


def move_kernel(n_dp, n_tp, chunks, picked, cache, out, loaded, stage, mid, load_sem, own_sem, send1, recv1, send2, recv2):
    group_req, piece, _ = loaded.shape
    per_pair = group_req // n_dp
    per_dev = group_req // n_tp
    rows = piece // chunks
    g = lax.axis_index("dp")
    c = lax.axis_index("tp")
    load = pltpu.make_async_copy(cache, loaded, load_sem)
    load.start()
    barrier = pltpu.get_barrier_semaphore()

    def greet_dp(i):
        pl.semaphore_signal(barrier, 1, device_id=(lax.rem(g + i, n_dp), c), device_id_type=MESH)

    def greet_tp(i):
        pl.semaphore_signal(barrier, 1, device_id=(g, lax.rem(c + i, n_tp)), device_id_type=MESH)

    loop(1, n_dp, greet_dp)
    loop(1, n_tp, greet_tp)
    pl.semaphore_wait(barrier, n_dp + n_tp - 2)
    load.wait()

    def sort(i):
        stage[i] = loaded[picked[i]]

    loop(0, group_req, sort)

    def keep(i):
        mid[per_pair * g + i] = stage[per_pair * g + i]

    loop(0, per_pair, keep)

    def over_dp(q, i, from_group):
        to_group = lax.rem(g + i, n_dp)
        part = pl.ds(q * rows, rows)
        return pltpu.make_async_remote_copy(
            src_ref=stage.at[pl.ds(per_pair * to_group, per_pair), part],
            dst_ref=mid.at[pl.ds(per_pair * from_group, per_pair), part],
            send_sem=send1.at[q, to_group],
            recv_sem=recv1.at[q, from_group],
            device_id=(to_group, c),
            device_id_type=MESH,
        )

    def over_tp(q, i, from_column):
        to_column = lax.rem(c + i, n_tp)
        return pltpu.make_async_remote_copy(
            src_ref=mid.at[pl.ds(per_dev * to_column, per_dev), pl.ds(q * rows, rows)],
            dst_ref=out.at[:, pl.ds(from_column * piece + q * rows, rows)],
            send_sem=send2.at[q, to_column],
            recv_sem=recv2.at[q, from_column],
            device_id=(g, to_column),
            device_id_type=MESH,
        )

    def own(q):
        return pltpu.make_async_copy(
            mid.at[pl.ds(per_dev * c, per_dev), pl.ds(q * rows, rows)],
            out.at[:, pl.ds(c * piece + q * rows, rows)],
            own_sem.at[q],
        )

    ahead = 2
    for q in range(chunks + 1):
        if q < chunks:
            if q >= ahead:
                loop(1, n_dp, lambda i: over_dp(q - ahead, i, g).wait_send())
            loop(1, n_dp, lambda i: over_dp(q, i, g).start())
        if q >= 1:
            loop(1, n_dp, lambda i: over_dp(q - 1, i, lax.rem(g + n_dp - i, n_dp)).wait_recv())
            loop(1, n_tp, lambda i: over_tp(q - 1, i, c).start())
            own(q - 1).start()
    for q in range(chunks):
        if q >= chunks - ahead:
            loop(1, n_dp, lambda i: over_dp(q, i, g).wait_send())
        loop(1, n_tp, lambda i: over_tp(q, i, c).wait_send())
        loop(1, n_tp, lambda i: over_tp(q, i, lax.rem(c + n_tp - i, n_tp)).wait_recv())
        own(q).wait()


def move(picked, old_cache, n_dp, n_tp):
    group_req, piece, width = old_cache.shape
    chunks = 12
    sems = pltpu.SemaphoreType.DMA
    return pl.pallas_call(
        functools.partial(move_kernel, n_dp, n_tp, chunks),
        out_shape=jax.ShapeDtypeStruct((group_req // n_tp, piece * n_tp, width), old_cache.dtype),
        in_specs=[pl.BlockSpec(memory_space=pltpu.SMEM), pl.BlockSpec(memory_space=pl.ANY)],
        out_specs=pl.BlockSpec(memory_space=pl.ANY),
        scratch_shapes=[
            pltpu.VMEM(old_cache.shape, old_cache.dtype),
            pltpu.VMEM(old_cache.shape, old_cache.dtype),
            pltpu.VMEM(old_cache.shape, old_cache.dtype),
            sems,
            sems((chunks,)),
            sems((chunks, n_dp)),
            sems((chunks, n_dp)),
            sems((chunks, n_tp)),
            sems((chunks, n_tp)),
        ],
        compiler_params=pltpu.CompilerParams(collective_id=0, has_side_effects=True, vmem_limit_bytes=48 * 2**20),
    )(picked, old_cache)


score_scale = 0.07216878364870323
norm_eps = 1e-06


def attend_blocks(query_row, key_rows, last_pos, kv_rank):
    context = key_rows.shape[0]
    raw_all = (
        jnp.einsum("hc,pc->hp", query_row, key_rows, preferred_element_type=jnp.float32)
        * score_scale
    )
    offsets = jnp.arange(context, dtype=jnp.int32)
    masked = jnp.where(offsets[None, :] <= last_pos, raw_all, -jnp.inf)
    row_max = jnp.max(masked, axis=1, keepdims=True)
    exponent = jnp.exp(masked - row_max)
    row_total = jnp.sum(exponent, axis=1, keepdims=True)
    weights = (exponent / row_total).astype(jnp.bfloat16)
    accum = jnp.dot(weights, key_rows[:, :kv_rank], preferred_element_type=jnp.float32)
    return accum.astype(jnp.bfloat16)


def dense_kernel(
    lat,
    value_up,
    hidden,
    gain,
    w_out,
    w_gate,
    w_up,
    w_down,
    out,
    vup_v,
    wout_v,
    wgate_v,
    wup_v,
    wdown_v,
    latr,
    perm,
    xbuf,
    s3,
    r3,
    after,
    ybuf,
    gu,
    keep,
    pair_s,
    pair_r,
    ring_s,
    ring_r,
    hbuf,
    wsem,
    lat_ss,
    lat_rs,
    x_ss,
    x_rs,
    s3_ss,
    s3_rs,
    y_ss,
    y_rs,
    pair_ss,
    pair_rs,
    ring_ss,
    ring_rs,
    h_ss,
    h_rs,
    s7_ss,
    s7_rs,
    o_ss,
    o_rs,
):
    f32, bf16 = jnp.float32, jnp.bfloat16
    g = lax.axis_index("dp")
    c = lax.axis_index("tp")
    y, k = g // 2, lax.rem(g, 2)
    z, x = c // 4, lax.rem(c, 4)
    sib = g + 1 - 2 * k
    ff = wgate_v.shape[1]
    width = 2 * ff

    def owner(block):
        return 4 * lax.rem(block, 4) + lax.rem(lax.rem(block, 4) + block // 4, 4)

    mine = 4 * lax.rem(x - z + 4, 4) + z

    loads = []
    for n, (src, dst) in enumerate(
        ((value_up, vup_v), (w_out, wout_v), (w_gate, wgate_v), (w_up, wup_v), (w_down, wdown_v))
    ):
        loads.append(pltpu.make_async_copy(src, dst, wsem.at[n]))
        loads[-1].start()

    def remote(src, dst, send_sem, recv_sem, dp, tp):
        return pltpu.make_async_remote_copy(
            src_ref=src, dst_ref=dst, send_sem=send_sem, recv_sem=recv_sem, device_id=(dp, tp), device_id_type=MESH
        )

    barrier = pltpu.get_barrier_semaphore()
    loop(1, 16, lambda i: pl.semaphore_signal(barrier, 1, device_id=(g, lax.rem(c + i, 16)), device_id_type=MESH))
    loop(1, 4, lambda i: pl.semaphore_signal(barrier, 1, device_id=(lax.rem(g + 2 * i, 8), c), device_id_type=MESH))
    pl.semaphore_signal(barrier, 1, device_id=(sib, c), device_id_type=MESH)
    pl.semaphore_wait(barrier, 19)

    def lat_copy(i, source):
        to = lax.rem(c + i, 16)
        return remote(lat.at[to], latr.at[source], lat_ss.at[to], lat_rs.at[source], g, to)

    loop(1, 16, lambda i: lat_copy(i, c).start())
    latr[c] = lat[c]
    row = lax.broadcasted_iota(jnp.int32, (512, 512), 0)
    col = lax.broadcasted_iota(jnp.int32, (512, 512), 1)
    wanted = ((row & 31) >> 1) * 32 + (row & 1) * 16 + ((row >> 5) & 1) * 8 + (row >> 6)
    perm[...] = jnp.where(col == wanted, 1.0, 0.0).astype(bf16)
    loop(1, 16, lambda i: lat_copy(i, lax.rem(c + 16 - i, 16)).wait_recv())
    ordered = jnp.dot(perm[...], latr[...].reshape(512, 512), preferred_element_type=f32).astype(bf16)
    loads[0].wait()
    for head in range(8):
        part = jnp.dot(ordered[64 * head : 64 * head + 64], vup_v[head], preferred_element_type=f32)
        xbuf[g, :, 128 * head : 128 * head + 128] = part.astype(bf16)

    def gather_ring(buf, ss, rs, i, source):
        to = lax.rem(g + 2 * i, 8)
        return remote(buf.at[g], buf.at[source], ss.at[i], rs.at[source], to, c)

    def gather_pair(buf, ss, rs, i, sent, got):
        return remote(buf.at[sent], buf.at[got], ss.at[4 + i], rs.at[got], sib, c)

    def gather_start(buf, ss, rs):
        loop(1, 4, lambda i: gather_ring(buf, ss, rs, i, g).start())
        gather_pair(buf, ss, rs, 0, g, g).start()

    def gather_step(buf, ss, rs, i):
        src = lax.rem(g + 8 - 2 * i, 8)
        other = src + 1 - 2 * k

        @pl.when(i > 0)
        def _():
            gather_ring(buf, ss, rs, i, src).wait_recv()
            gather_pair(buf, ss, rs, i, src, src).start()

        gather_pair(buf, ss, rs, i, src, other).wait_recv()
        return src // 2

    def gather_end(buf, ss, rs):
        loop(1, 4, lambda i: gather_ring(buf, ss, rs, i, g).wait_send())
        loop(0, 4, lambda i: gather_pair(buf, ss, rs, i, g, g).wait_send())

    def scatter_copy(ss, rs, block, source):
        return remote(s3.at[block], r3.at[source], ss.at[block], rs.at[source], g, owner(block))

    def scatter(value, chunk, ss, rs):
        for j in range(4):
            s3[4 * chunk + j] = value[32 * j : 32 * j + 32].astype(bf16)
        for j in range(4):
            block = 4 * chunk + j

            @pl.when(block != mine)
            def _():
                scatter_copy(ss, rs, block, c).start()

    def scatter_sum(ss, rs, first):
        total = first
        loop(1, 16, lambda i: scatter_copy(ss, rs, mine, lax.rem(c + 16 - i, 16)).wait_recv())
        r3[c] = s3[mine]
        total = total + jnp.sum(r3[...].astype(f32), axis=0)
        def sent(i):
            @pl.when(i != mine)
            def _():
                scatter_copy(ss, rs, i, c).wait_send()
        loop(0, 16, sent)
        return total

    gather_start(xbuf, x_ss, x_rs)
    loads[1].wait()

    def out_step(i):
        chunk = gather_step(xbuf, x_ss, x_rs, i)
        rows = xbuf[pl.ds(2 * chunk, 2)].reshape(128, 1024)
        scatter(jnp.dot(rows, wout_v[...], preferred_element_type=f32), chunk, s3_ss, s3_rs)

    loop(0, 4, out_step)
    residual = hidden[lax.rem(mine, 2), mine // 2].astype(f32)
    after[...] = scatter_sum(s3_ss, s3_rs, residual)
    gather_end(xbuf, x_ss, x_rs)

    ybuf[mine] = after[...].astype(bf16)

    def spread(buf_at, ss, rs, i, block):
        to = lax.rem(c + i, 16)
        return remote(buf_at(mine), buf_at(block), ss.at[to], rs.at[block], g, to)

    def y_at(block):
        return ybuf.at[block]

    loop(1, 16, lambda i: spread(y_at, y_ss, y_rs, i, mine).start())
    loads[2].wait()
    loads[3].wait()
    lane = lax.broadcasted_iota(jnp.int32, (64, 128), 1)

    def two_part(total):
        high = total.astype(bf16)
        low = (total - high.astype(f32)).astype(bf16)
        return jnp.where(lane < 64, high.astype(f32), low.astype(f32)).astype(bf16)

    def one_part(pair):
        return pair[:, 0:1].astype(f32) + pair[:, 64:65].astype(f32)

    def pair_copy(chunk):
        return remote(pair_s.at[chunk], pair_r.at[chunk], pair_ss.at[chunk], pair_rs.at[chunk], sib, c)

    def ring_copy(chunk, source):
        return remote(ring_s.at[chunk], ring_r.at[source], ring_ss.at[chunk], ring_rs.at[source], 2 * chunk + k, c)

    def gate_step(i):
        chunk = lax.rem(y + 1 + i, 4)
        for j in range(4):
            block = 4 * chunk + j

            @pl.when(block != mine)
            def _():
                spread(y_at, y_ss, y_rs, 1, block).wait_recv()

        rows = ybuf[pl.ds(4 * chunk, 4)].reshape(128, ybuf.shape[2]).astype(f32)
        squares = jnp.sum(rows * rows, axis=1, keepdims=True)
        scaled = (rows * gain[...]).astype(bf16)
        gu[:, :, 0:ff] = jnp.dot(scaled, wgate_v[...], preferred_element_type=f32).reshape(2, 64, ff)
        gu[:, :, ff:width] = jnp.dot(scaled, wup_v[...], preferred_element_type=f32).reshape(2, 64, ff)
        gu[:, :, width : width + 128] = jnp.broadcast_to(squares, (128, 128)).reshape(2, 64, 128)
        pair_s[chunk, :, 0:width] = gu[1 - k, :, 0:width].astype(bf16)
        pair_s[chunk, :, width : width + 128] = two_part(gu[1 - k, :, width : width + 128])
        pair_copy(chunk).start()
        keep[chunk] = gu[k]

    def merge_step(i):
        chunk = lax.rem(y + 1 + i, 4)
        pair_copy(chunk).wait_recv()
        keep[chunk, :, 0:width] += pair_r[chunk, :, 0:width].astype(f32)
        keep[chunk, :, width : width + 128] += one_part(pair_r[chunk, :, width : width + 128])

        @pl.when(chunk != y)
        def _():
            ring_s[chunk, :, 0:width] = keep[chunk, :, 0:width].astype(bf16)
            ring_s[chunk, :, width : width + 128] = two_part(keep[chunk, :, width : width + 128])
            ring_copy(chunk, y).start()

    def gate_loop(i):
        @pl.when(i < 4)
        def _():
            gate_step(i)

        @pl.when(i > 0)
        def _():
            merge_step(i - 1)

    loop(0, 5, gate_loop)

    def ring_add(i):
        source = lax.rem(y + i, 4)
        ring_copy(source, source).wait_recv()
        keep[y, :, 0:width] += ring_r[source, :, 0:width].astype(f32)
        keep[y, :, width : width + 128] += one_part(ring_r[source, :, width : width + 128])

    loop(1, 4, ring_add)
    squares = keep[y, :, width : width + 1]
    scale = 1.0 / jnp.sqrt(squares / D + norm_eps)
    gate = keep[y, :, 0:ff] * scale
    up = keep[y, :, ff:width] * scale
    hbuf[g] = (jax.nn.silu(gate) * up).astype(bf16)
    gather_start(hbuf, h_ss, h_rs)
    loads[4].wait()

    def down_step(i):
        chunk = gather_step(hbuf, h_ss, h_rs, i)
        rows = hbuf[pl.ds(2 * chunk, 2)].reshape(128, ff)
        scatter(jnp.dot(rows, wdown_v[...], preferred_element_type=f32), chunk, s7_ss, s7_rs)

    loop(0, 4, down_step)
    result = scatter_sum(s7_ss, s7_rs, after[...])
    step, group = lax.rem(mine, 2), mine // 2
    out[step, group] = result.astype(bf16)

    def o_at(block):
        return out.at[lax.rem(block, 2), block // 2]

    loop(1, 16, lambda i: spread(o_at, o_ss, o_rs, i, mine).start())
    gather_end(hbuf, h_ss, h_rs)
    loop(1, 16, lambda i: lat_copy(i, c).wait_send())
    loop(1, 16, lambda i: spread(y_at, y_ss, y_rs, i, mine).wait_send())
    loop(0, 4, lambda i: pair_copy(i).wait_send())
    loop(1, 4, lambda i: ring_copy(lax.rem(y + i, 4), y).wait_send())

    def finish(block):
        @pl.when(block != mine)
        def _():
            spread(o_at, o_ss, o_rs, 1, block).wait_recv()

    loop(0, 16, finish)
    loop(1, 16, lambda i: spread(o_at, o_ss, o_rs, i, mine).wait_send())


def dense(lat, value_up, hidden, gain, w_out, w_gate, w_up, w_down):
    steps, total, cols = hidden.shape
    ff = w_gate.shape[1]
    bf16, f32 = jnp.bfloat16, jnp.float32
    vmem, sems = pltpu.VMEM, pltpu.SemaphoreType.DMA
    in_vmem, anywhere = pl.BlockSpec(memory_space=pltpu.VMEM), pl.BlockSpec(memory_space=pl.ANY)
    result = pl.pallas_call(
        dense_kernel,
        out_shape=jax.ShapeDtypeStruct((steps, 8, 32, cols), bf16),
        in_specs=[in_vmem, anywhere, in_vmem, in_vmem, anywhere, anywhere, anywhere, anywhere],
        out_specs=in_vmem,
        scratch_shapes=[
            vmem(value_up.shape, bf16),
            vmem(w_out.shape, bf16),
            vmem(w_gate.shape, bf16),
            vmem(w_up.shape, bf16),
            vmem(w_down.shape, bf16),
            vmem(lat.shape, bf16),
            vmem((512, 512), bf16),
            vmem((8, 64, w_out.shape[0]), bf16),
            vmem((16, 32, cols), bf16),
            vmem((16, 32, cols), bf16),
            vmem((32, cols), f32),
            vmem((16, 32, cols), bf16),
            vmem((2, 64, 2 * ff + 128), f32),
            vmem((4, 64, 2 * ff + 128), f32),
            vmem((4, 64, 2 * ff + 128), bf16),
            vmem((4, 64, 2 * ff + 128), bf16),
            vmem((4, 64, 2 * ff + 128), bf16),
            vmem((4, 64, 2 * ff + 128), bf16),
            vmem((8, 64, ff), bf16),
            sems((5,)),
            sems((16,)),
            sems((16,)),
            sems((8,)),
            sems((8,)),
            sems((16,)),
            sems((16,)),
            sems((16,)),
            sems((16,)),
            sems((4,)),
            sems((4,)),
            sems((4,)),
            sems((4,)),
            sems((8,)),
            sems((8,)),
            sems((16,)),
            sems((16,)),
            sems((16,)),
            sems((16,)),
        ],
        compiler_params=pltpu.CompilerParams(collective_id=1, has_side_effects=True, vmem_limit_bytes=52 * 2**20),
    )(lat, value_up, hidden.reshape(steps, 8, 32, cols), gain, w_out, w_gate, w_up, w_down)
    return result.reshape(steps, total, cols)


def shards(
    old_cache,
    lengths,
    new_slot,
    queries,
    new_latent,
    hidden,
    value_up_weight,
    w_out,
    norm_gain,
    w_gate,
    w_up,
    w_down,
):
    dp_count = lax.axis_size("dp")
    tp_count = lax.axis_size("tp")
    my_group = lax.axis_index("dp")
    my_column = lax.axis_index("tp")
    group_req, piece_len, lat_width = old_cache.shape
    per_pair = group_req // dp_count
    step_count = queries.shape[0]
    req_dev = queries.shape[1]
    req_total = new_slot.shape[0]
    context = piece_len * tp_count
    kv_rank = value_up_weight.shape[1]
    everyone = jnp.arange(req_total, dtype=jnp.int32)
    new_group = new_slot // group_req
    pair_rank = new_slot % group_req - everyone // group_req * per_pair
    my_targets = lax.dynamic_slice_in_dim(
        new_group * per_pair + pair_rank, my_group * group_req, group_req
    )
    target_places = jnp.arange(group_req, dtype=jnp.int32)
    picked = jnp.sum(
        jnp.where(my_targets[None, :] == target_places[:, None], target_places[None, :], 0), axis=1
    )
    arrived = move(picked, old_cache, dp_count, tp_count)
    source = jnp.sum(
        jnp.where(new_slot[None, :] == everyone[:, None], everyone[None, :], 0), axis=1
    )
    my_slots = (my_group * tp_count + my_column) * req_dev + jnp.arange(req_dev, dtype=jnp.int32)
    my_lengths = jnp.take(lengths, jnp.take(source, my_slots))
    positions = jnp.arange(context, dtype=jnp.int32)
    kv_cache = arrived
    for step_no in range(step_count):
        kv_cache = jnp.where(
            positions[None, :, None] == (my_lengths + step_no)[:, None, None],
            new_latent[step_no][:, None, :],
            kv_cache,
        )
    new_cache = jnp.where(
        positions[None, :, None] < (my_lengths + step_count)[:, None, None],
        kv_cache,
        jnp.zeros((), jnp.bfloat16),
    )
    latents = jnp.stack(
        [
            jnp.stack(
                [
                    attend_blocks(
                        queries[step_no, item], kv_cache[item], my_lengths[item] + step_no, kv_rank
                    )
                    for step_no in range(step_count)
                ]
            )
            for item in range(req_dev)
        ]
    )
    latents = latents.reshape(req_dev, step_count, tp_count, -1, kv_rank).transpose(2, 0, 1, 3, 4)
    latents = latents.reshape(tp_count, -1, kv_rank)
    gain = norm_gain.astype(jnp.float32)[None, :]
    layer_out = dense(latents, value_up_weight, hidden, gain, w_out, w_gate, w_up, w_down)
    return (new_cache, layer_out)


def solution(mesh):
    in_specs = (
        P("dp", "tp", None),
        P(),
        P(),
        P(None, ("dp", "tp"), None, None),
        P(None, ("dp", "tp"), None),
        P(None, None, "dp"),
        P("tp", None, None),
        P("tp", "dp"),
        P("dp"),
        P("dp", "tp"),
        P("dp", "tp"),
        P("tp", "dp"),
    )
    out_specs = (P(("dp", "tp"), None, None), P(None, None, "dp"))
    return jax.shard_map(shards, mesh=mesh, in_specs=in_specs, out_specs=out_specs, check_vma=False)
```

```python
import functools

import jax
import jax.numpy as jnp
from jax import lax
from jax.experimental import pallas as pl
from jax.experimental.pallas import tpu as pltpu
from jax.sharding import PartitionSpec as P

D = 7168


MESH = pl.DeviceIdType.MESH


def loop(low, high, action):
    def body(i, carry):
        action(i)
        return carry

    lax.fori_loop(low, high, body, 0)


def move_kernel(n_dp, n_tp, chunks, picked, cache, out, loaded, stage, mid, load_sem, own_sem, send1, recv1, send2, recv2):
    group_req, piece, _ = loaded.shape
    per_pair = group_req // n_dp
    per_dev = group_req // n_tp
    rows = piece // chunks
    g = lax.axis_index("dp")
    c = lax.axis_index("tp")
    load = pltpu.make_async_copy(cache, loaded, load_sem)
    load.start()
    barrier = pltpu.get_barrier_semaphore()

    def greet_dp(i):
        pl.semaphore_signal(barrier, 1, device_id=(lax.rem(g + i, n_dp), c), device_id_type=MESH)

    def greet_tp(i):
        pl.semaphore_signal(barrier, 1, device_id=(g, lax.rem(c + i, n_tp)), device_id_type=MESH)

    loop(1, n_dp, greet_dp)
    loop(1, n_tp, greet_tp)
    pl.semaphore_wait(barrier, n_dp + n_tp - 2)
    load.wait()

    def sort(i):
        stage[i] = loaded[picked[i]]

    loop(0, group_req, sort)

    def keep(i):
        mid[per_pair * g + i] = stage[per_pair * g + i]

    loop(0, per_pair, keep)

    def over_dp(q, i, from_group):
        to_group = lax.rem(g + i, n_dp)
        part = pl.ds(q * rows, rows)
        return pltpu.make_async_remote_copy(
            src_ref=stage.at[pl.ds(per_pair * to_group, per_pair), part],
            dst_ref=mid.at[pl.ds(per_pair * from_group, per_pair), part],
            send_sem=send1.at[q, to_group],
            recv_sem=recv1.at[q, from_group],
            device_id=(to_group, c),
            device_id_type=MESH,
        )

    def over_tp(q, i, from_column):
        to_column = lax.rem(c + i, n_tp)
        return pltpu.make_async_remote_copy(
            src_ref=mid.at[pl.ds(per_dev * to_column, per_dev), pl.ds(q * rows, rows)],
            dst_ref=out.at[:, pl.ds(from_column * piece + q * rows, rows)],
            send_sem=send2.at[q, to_column],
            recv_sem=recv2.at[q, from_column],
            device_id=(g, to_column),
            device_id_type=MESH,
        )

    def own(q):
        return pltpu.make_async_copy(
            mid.at[pl.ds(per_dev * c, per_dev), pl.ds(q * rows, rows)],
            out.at[:, pl.ds(c * piece + q * rows, rows)],
            own_sem.at[q],
        )

    ahead = 2
    for q in range(chunks + 1):
        if q < chunks:
            if q >= ahead:
                loop(1, n_dp, lambda i: over_dp(q - ahead, i, g).wait_send())
            loop(1, n_dp, lambda i: over_dp(q, i, g).start())
        if q >= 1:
            loop(1, n_dp, lambda i: over_dp(q - 1, i, lax.rem(g + n_dp - i, n_dp)).wait_recv())
            loop(1, n_tp, lambda i: over_tp(q - 1, i, c).start())
            own(q - 1).start()
    for q in range(chunks):
        if q >= chunks - ahead:
            loop(1, n_dp, lambda i: over_dp(q, i, g).wait_send())
        loop(1, n_tp, lambda i: over_tp(q, i, c).wait_send())
        loop(1, n_tp, lambda i: over_tp(q, i, lax.rem(c + n_tp - i, n_tp)).wait_recv())
        own(q).wait()


def move(picked, old_cache, n_dp, n_tp):
    group_req, piece, width = old_cache.shape
    chunks = 12
    sems = pltpu.SemaphoreType.DMA
    return pl.pallas_call(
        functools.partial(move_kernel, n_dp, n_tp, chunks),
        out_shape=jax.ShapeDtypeStruct((group_req // n_tp, piece * n_tp, width), old_cache.dtype),
        in_specs=[pl.BlockSpec(memory_space=pltpu.SMEM), pl.BlockSpec(memory_space=pl.ANY)],
        out_specs=pl.BlockSpec(memory_space=pl.ANY),
        scratch_shapes=[
            pltpu.VMEM(old_cache.shape, old_cache.dtype),
            pltpu.VMEM(old_cache.shape, old_cache.dtype),
            pltpu.VMEM(old_cache.shape, old_cache.dtype),
            sems,
            sems((chunks,)),
            sems((chunks, n_dp)),
            sems((chunks, n_dp)),
            sems((chunks, n_tp)),
            sems((chunks, n_tp)),
        ],
        compiler_params=pltpu.CompilerParams(collective_id=0, has_side_effects=True, vmem_limit_bytes=48 * 2**20),
    )(picked, old_cache)


score_scale = 0.07216878364870323
norm_eps = 1e-06


def attend_kernel(lens, arrived, queries, new_latent, cache_out, lat, scores):
    f32, bf16 = jnp.float32, jnp.bfloat16
    item = pl.program_id(0)
    length = lens[item]
    context, width = arrived.shape[1:]
    heads = queries.shape[3]
    both = 2 * heads
    kv_rank = lat.shape[2]
    query = jnp.concatenate([queries[0, 0], queries[1, 0]], axis=1)
    first = new_latent[0, item].astype(f32)
    second = new_latent[1, item].astype(f32)
    block = 256
    row = lax.broadcasted_iota(jnp.int32, (block, width), 0)
    place = lax.broadcasted_iota(jnp.int32, (block, both), 0)
    last = length + lax.broadcasted_iota(jnp.int32, (block, both), 1) // heads

    def score(i, top):
        start = pl.multiple_of(i * block, block)
        rows = pl.ds(start, block)
        position = row + start
        keys = arrived[0, rows].astype(f32)
        keys = jnp.where(position < length, keys, jnp.where(position == length, first, jnp.where(position == length + 1, second, 0.0)))
        keys = keys.astype(bf16)
        cache_out[0, :, rows] = keys.T
        raw = jnp.dot(keys, query, preferred_element_type=f32) * score_scale
        raw = jnp.where(place + start <= last, raw, -jnp.inf)
        scores[rows] = raw
        return jnp.maximum(top, jnp.max(raw, axis=0, keepdims=True))

    top = lax.fori_loop(0, context // block, score, jnp.full((1, both), -jnp.inf, f32))
    exponent = jnp.exp(scores[...] - top)
    total = jnp.sum(exponent, axis=0, keepdims=True)
    mixed_t = jnp.dot(cache_out[0, :kv_rank], exponent.astype(bf16), preferred_element_type=f32)
    mixed = (mixed_t / total).T
    mixed = mixed.reshape(2, lat.shape[0], -1, kv_rank)
    mixed = jnp.concatenate([mixed[0], mixed[1]], axis=1).astype(bf16)
    lat[:, pl.ds(pl.multiple_of(item * 16, 16), 16)] = mixed


def attend(my_lengths, arrived, queries, new_latent, n_tp, kv_rank):
    items, context, width = arrived.shape
    steps, _, heads, _ = queries.shape
    bf16 = jnp.bfloat16
    flipped, latents = pl.pallas_call(
        attend_kernel,
        grid=(items,),
        out_shape=(
            jax.ShapeDtypeStruct((items, width, context), bf16),
            jax.ShapeDtypeStruct((n_tp, items * steps * heads // n_tp, kv_rank), bf16),
        ),
        in_specs=[
            pl.BlockSpec(memory_space=pltpu.SMEM),
            pl.BlockSpec((1, context, width), lambda i: (i, 0, 0)),
            pl.BlockSpec((steps, 1, width, heads), lambda i: (0, i, 0, 0)),
            pl.BlockSpec((steps, items, 1, width), lambda i: (0, 0, 0, 0)),
        ],
        out_specs=(
            pl.BlockSpec((1, width, context), lambda i: (i, 0, 0)),
            pl.BlockSpec((n_tp, items * steps * heads // n_tp, kv_rank), lambda i: (0, 0, 0)),
        ),
        scratch_shapes=[
            pltpu.VMEM((context, steps * heads), jnp.float32),
        ],
        compiler_params=pltpu.CompilerParams(vmem_limit_bytes=40 * 2**20),
    )(my_lengths, arrived, queries.transpose(0, 1, 3, 2), new_latent[:, :, None, :])
    return flipped.transpose(0, 2, 1), latents

def dense_kernel(
    lat,
    value_up,
    hidden,
    gain,
    w_out,
    w_gate,
    w_up,
    w_down,
    out,
    vup_v,
    wout_v,
    wgate_v,
    wup_v,
    wdown_v,
    latr,
    perm,
    xbuf,
    s3,
    r3,
    after,
    ybuf,
    gu,
    keep,
    pair_s,
    pair_r,
    ring_s,
    ring_r,
    hbuf,
    wsem,
    lat_ss,
    lat_rs,
    x_ss,
    x_rs,
    s3_ss,
    s3_rs,
    y_ss,
    y_rs,
    pair_ss,
    pair_rs,
    ring_ss,
    ring_rs,
    h_ss,
    h_rs,
    s7_ss,
    s7_rs,
    o_ss,
    o_rs,
):
    f32, bf16 = jnp.float32, jnp.bfloat16
    g = lax.axis_index("dp")
    c = lax.axis_index("tp")
    y, k = g // 2, lax.rem(g, 2)
    z, x = c // 4, lax.rem(c, 4)
    sib = g + 1 - 2 * k
    ff = wgate_v.shape[1]
    width = 2 * ff

    def owner(block):
        return 4 * lax.rem(block, 4) + lax.rem(lax.rem(block, 4) + block // 4, 4)

    mine = 4 * lax.rem(x - z + 4, 4) + z

    loads = []
    for n, (src, dst) in enumerate(
        ((value_up, vup_v), (w_out, wout_v), (w_gate, wgate_v), (w_up, wup_v), (w_down, wdown_v))
    ):
        loads.append(pltpu.make_async_copy(src, dst, wsem.at[n]))
        loads[-1].start()

    def remote(src, dst, send_sem, recv_sem, dp, tp):
        return pltpu.make_async_remote_copy(
            src_ref=src, dst_ref=dst, send_sem=send_sem, recv_sem=recv_sem, device_id=(dp, tp), device_id_type=MESH
        )

    barrier = pltpu.get_barrier_semaphore()
    loop(1, 16, lambda i: pl.semaphore_signal(barrier, 1, device_id=(g, lax.rem(c + i, 16)), device_id_type=MESH))
    loop(1, 4, lambda i: pl.semaphore_signal(barrier, 1, device_id=(lax.rem(g + 2 * i, 8), c), device_id_type=MESH))
    pl.semaphore_signal(barrier, 1, device_id=(sib, c), device_id_type=MESH)
    pl.semaphore_wait(barrier, 19)

    def lat_copy(i, source):
        to = lax.rem(c + i, 16)
        return remote(lat.at[to], latr.at[source], lat_ss.at[to], lat_rs.at[source], g, to)

    loop(1, 16, lambda i: lat_copy(i, c).start())
    latr[c] = lat[c]
    row = lax.broadcasted_iota(jnp.int32, (512, 512), 0)
    col = lax.broadcasted_iota(jnp.int32, (512, 512), 1)
    wanted = ((row & 31) >> 1) * 32 + (row & 1) * 16 + ((row >> 5) & 1) * 8 + (row >> 6)
    perm[...] = jnp.where(col == wanted, 1.0, 0.0).astype(bf16)
    loop(1, 16, lambda i: lat_copy(i, lax.rem(c + 16 - i, 16)).wait_recv())
    ordered = jnp.dot(perm[...], latr[...].reshape(512, 512), preferred_element_type=f32).astype(bf16)
    loads[0].wait()
    for head in range(8):
        part = jnp.dot(ordered[64 * head : 64 * head + 64], vup_v[head], preferred_element_type=f32)
        xbuf[g, :, 128 * head : 128 * head + 128] = part.astype(bf16)

    def gather_ring(buf, ss, rs, i, source):
        to = lax.rem(g + 2 * i, 8)
        return remote(buf.at[g], buf.at[source], ss.at[i], rs.at[source], to, c)

    def gather_pair(buf, ss, rs, i, sent, got):
        return remote(buf.at[sent], buf.at[got], ss.at[4 + i], rs.at[got], sib, c)

    def gather_start(buf, ss, rs):
        loop(1, 4, lambda i: gather_ring(buf, ss, rs, i, g).start())
        gather_pair(buf, ss, rs, 0, g, g).start()

    def gather_step(buf, ss, rs, i):
        src = lax.rem(g + 8 - 2 * i, 8)
        other = src + 1 - 2 * k

        @pl.when(i > 0)
        def _():
            gather_ring(buf, ss, rs, i, src).wait_recv()
            gather_pair(buf, ss, rs, i, src, src).start()

        gather_pair(buf, ss, rs, i, src, other).wait_recv()
        return src // 2

    def gather_end(buf, ss, rs):
        loop(1, 4, lambda i: gather_ring(buf, ss, rs, i, g).wait_send())
        loop(0, 4, lambda i: gather_pair(buf, ss, rs, i, g, g).wait_send())

    def scatter_copy(ss, rs, block, source):
        return remote(s3.at[block], r3.at[source], ss.at[block], rs.at[source], g, owner(block))

    def scatter(value, chunk, ss, rs):
        for j in range(4):
            s3[4 * chunk + j] = value[32 * j : 32 * j + 32].astype(bf16)
        for j in range(4):
            block = 4 * chunk + j

            @pl.when(block != mine)
            def _():
                scatter_copy(ss, rs, block, c).start()

    def scatter_sum(ss, rs, first):
        total = first
        loop(1, 16, lambda i: scatter_copy(ss, rs, mine, lax.rem(c + 16 - i, 16)).wait_recv())
        r3[c] = s3[mine]
        total = total + jnp.sum(r3[...].astype(f32), axis=0)
        def sent(i):
            @pl.when(i != mine)
            def _():
                scatter_copy(ss, rs, i, c).wait_send()
        loop(0, 16, sent)
        return total

    gather_start(xbuf, x_ss, x_rs)
    loads[1].wait()

    def out_step(i):
        chunk = gather_step(xbuf, x_ss, x_rs, i)
        rows = xbuf[pl.ds(2 * chunk, 2)].reshape(128, 1024)
        scatter(jnp.dot(rows, wout_v[...], preferred_element_type=f32), chunk, s3_ss, s3_rs)

    loop(0, 4, out_step)
    residual = hidden[lax.rem(mine, 2), mine // 2].astype(f32)
    after[...] = scatter_sum(s3_ss, s3_rs, residual)
    gather_end(xbuf, x_ss, x_rs)

    ybuf[mine] = after[...].astype(bf16)

    def spread(buf_at, ss, rs, i, block):
        to = lax.rem(c + i, 16)
        return remote(buf_at(mine), buf_at(block), ss.at[to], rs.at[block], g, to)

    def y_at(block):
        return ybuf.at[block]

    loop(1, 16, lambda i: spread(y_at, y_ss, y_rs, i, mine).start())
    loads[2].wait()
    loads[3].wait()
    lane = lax.broadcasted_iota(jnp.int32, (64, 128), 1)

    def two_part(total):
        high = total.astype(bf16)
        low = (total - high.astype(f32)).astype(bf16)
        return jnp.where(lane < 64, high.astype(f32), low.astype(f32)).astype(bf16)

    def one_part(pair):
        return pair[:, 0:1].astype(f32) + pair[:, 64:65].astype(f32)

    def pair_copy(chunk):
        return remote(pair_s.at[chunk], pair_r.at[chunk], pair_ss.at[chunk], pair_rs.at[chunk], sib, c)

    def ring_copy(chunk, source):
        return remote(ring_s.at[chunk], ring_r.at[source], ring_ss.at[chunk], ring_rs.at[source], 2 * chunk + k, c)

    def gate_step(i):
        chunk = lax.rem(y + 1 + i, 4)
        for j in range(4):
            block = 4 * chunk + j

            @pl.when(block != mine)
            def _():
                spread(y_at, y_ss, y_rs, 1, block).wait_recv()

        rows = ybuf[pl.ds(4 * chunk, 4)].reshape(128, ybuf.shape[2]).astype(f32)
        squares = jnp.sum(rows * rows, axis=1, keepdims=True)
        scaled = (rows * gain[...]).astype(bf16)
        gu[:, :, 0:ff] = jnp.dot(scaled, wgate_v[...], preferred_element_type=f32).reshape(2, 64, ff)
        gu[:, :, ff:width] = jnp.dot(scaled, wup_v[...], preferred_element_type=f32).reshape(2, 64, ff)
        gu[:, :, width : width + 128] = jnp.broadcast_to(squares, (128, 128)).reshape(2, 64, 128)
        pair_s[chunk, :, 0:width] = gu[1 - k, :, 0:width].astype(bf16)
        pair_s[chunk, :, width : width + 128] = two_part(gu[1 - k, :, width : width + 128])
        pair_copy(chunk).start()
        keep[chunk] = gu[k]

    def merge_step(i):
        chunk = lax.rem(y + 1 + i, 4)
        pair_copy(chunk).wait_recv()
        keep[chunk, :, 0:width] += pair_r[chunk, :, 0:width].astype(f32)
        keep[chunk, :, width : width + 128] += one_part(pair_r[chunk, :, width : width + 128])

        @pl.when(chunk != y)
        def _():
            ring_s[chunk, :, 0:width] = keep[chunk, :, 0:width].astype(bf16)
            ring_s[chunk, :, width : width + 128] = two_part(keep[chunk, :, width : width + 128])
            ring_copy(chunk, y).start()

    def gate_loop(i):
        @pl.when(i < 4)
        def _():
            gate_step(i)

        @pl.when(i > 0)
        def _():
            merge_step(i - 1)

    loop(0, 5, gate_loop)

    def ring_add(i):
        source = lax.rem(y + i, 4)
        ring_copy(source, source).wait_recv()
        keep[y, :, 0:width] += ring_r[source, :, 0:width].astype(f32)
        keep[y, :, width : width + 128] += one_part(ring_r[source, :, width : width + 128])

    loop(1, 4, ring_add)
    squares = keep[y, :, width : width + 1]
    scale = 1.0 / jnp.sqrt(squares / D + norm_eps)
    gate = keep[y, :, 0:ff] * scale
    up = keep[y, :, ff:width] * scale
    hbuf[g] = (jax.nn.silu(gate) * up).astype(bf16)
    gather_start(hbuf, h_ss, h_rs)
    loads[4].wait()

    def down_step(i):
        chunk = gather_step(hbuf, h_ss, h_rs, i)
        rows = hbuf[pl.ds(2 * chunk, 2)].reshape(128, ff)
        scatter(jnp.dot(rows, wdown_v[...], preferred_element_type=f32), chunk, s7_ss, s7_rs)

    loop(0, 4, down_step)
    result = scatter_sum(s7_ss, s7_rs, after[...])
    step, group = lax.rem(mine, 2), mine // 2
    out[step, group] = result.astype(bf16)

    def o_at(block):
        return out.at[lax.rem(block, 2), block // 2]

    loop(1, 16, lambda i: spread(o_at, o_ss, o_rs, i, mine).start())
    gather_end(hbuf, h_ss, h_rs)
    loop(1, 16, lambda i: lat_copy(i, c).wait_send())
    loop(1, 16, lambda i: spread(y_at, y_ss, y_rs, i, mine).wait_send())
    loop(0, 4, lambda i: pair_copy(i).wait_send())
    loop(1, 4, lambda i: ring_copy(lax.rem(y + i, 4), y).wait_send())

    def finish(block):
        @pl.when(block != mine)
        def _():
            spread(o_at, o_ss, o_rs, 1, block).wait_recv()

    loop(0, 16, finish)
    loop(1, 16, lambda i: spread(o_at, o_ss, o_rs, i, mine).wait_send())


def dense(lat, value_up, hidden, gain, w_out, w_gate, w_up, w_down):
    steps, total, cols = hidden.shape
    ff = w_gate.shape[1]
    bf16, f32 = jnp.bfloat16, jnp.float32
    vmem, sems = pltpu.VMEM, pltpu.SemaphoreType.DMA
    in_vmem, anywhere = pl.BlockSpec(memory_space=pltpu.VMEM), pl.BlockSpec(memory_space=pl.ANY)
    result = pl.pallas_call(
        dense_kernel,
        out_shape=jax.ShapeDtypeStruct((steps, 8, 32, cols), bf16),
        in_specs=[in_vmem, anywhere, in_vmem, in_vmem, anywhere, anywhere, anywhere, anywhere],
        out_specs=in_vmem,
        scratch_shapes=[
            vmem(value_up.shape, bf16),
            vmem(w_out.shape, bf16),
            vmem(w_gate.shape, bf16),
            vmem(w_up.shape, bf16),
            vmem(w_down.shape, bf16),
            vmem(lat.shape, bf16),
            vmem((512, 512), bf16),
            vmem((8, 64, w_out.shape[0]), bf16),
            vmem((16, 32, cols), bf16),
            vmem((16, 32, cols), bf16),
            vmem((32, cols), f32),
            vmem((16, 32, cols), bf16),
            vmem((2, 64, 2 * ff + 128), f32),
            vmem((4, 64, 2 * ff + 128), f32),
            vmem((4, 64, 2 * ff + 128), bf16),
            vmem((4, 64, 2 * ff + 128), bf16),
            vmem((4, 64, 2 * ff + 128), bf16),
            vmem((4, 64, 2 * ff + 128), bf16),
            vmem((8, 64, ff), bf16),
            sems((5,)),
            sems((16,)),
            sems((16,)),
            sems((8,)),
            sems((8,)),
            sems((16,)),
            sems((16,)),
            sems((16,)),
            sems((16,)),
            sems((4,)),
            sems((4,)),
            sems((4,)),
            sems((4,)),
            sems((8,)),
            sems((8,)),
            sems((16,)),
            sems((16,)),
            sems((16,)),
            sems((16,)),
        ],
        compiler_params=pltpu.CompilerParams(collective_id=1, has_side_effects=True, vmem_limit_bytes=52 * 2**20),
    )(lat, value_up, hidden.reshape(steps, 8, 32, cols), gain, w_out, w_gate, w_up, w_down)
    return result.reshape(steps, total, cols)


def shards(
    old_cache,
    lengths,
    new_slot,
    queries,
    new_latent,
    hidden,
    value_up_weight,
    w_out,
    norm_gain,
    w_gate,
    w_up,
    w_down,
):
    dp_count = lax.axis_size("dp")
    tp_count = lax.axis_size("tp")
    my_group = lax.axis_index("dp")
    my_column = lax.axis_index("tp")
    group_req = old_cache.shape[0]
    per_pair = group_req // dp_count
    req_dev = queries.shape[1]
    req_total = new_slot.shape[0]
    kv_rank = value_up_weight.shape[1]
    everyone = jnp.arange(req_total, dtype=jnp.int32)
    new_group = new_slot // group_req
    pair_rank = new_slot % group_req - everyone // group_req * per_pair
    my_targets = lax.dynamic_slice_in_dim(
        new_group * per_pair + pair_rank, my_group * group_req, group_req
    )
    target_places = jnp.arange(group_req, dtype=jnp.int32)
    picked = jnp.sum(
        jnp.where(my_targets[None, :] == target_places[:, None], target_places[None, :], 0), axis=1
    )
    arrived = move(picked, old_cache, dp_count, tp_count)
    source = jnp.sum(
        jnp.where(new_slot[None, :] == everyone[:, None], everyone[None, :], 0), axis=1
    )
    my_slots = (my_group * tp_count + my_column) * req_dev + jnp.arange(req_dev, dtype=jnp.int32)
    my_lengths = jnp.take(lengths, jnp.take(source, my_slots))
    new_cache, latents = attend(my_lengths, arrived, queries, new_latent, tp_count, kv_rank)
    gain = norm_gain.astype(jnp.float32)[None, :]
    layer_out = dense(latents, value_up_weight, hidden, gain, w_out, w_gate, w_up, w_down)
    return (new_cache, layer_out)


def solution(mesh):
    in_specs = (
        P("dp", "tp", None),
        P(),
        P(),
        P(None, ("dp", "tp"), None, None),
        P(None, ("dp", "tp"), None),
        P(None, None, "dp"),
        P("tp", None, None),
        P("tp", "dp"),
        P("dp"),
        P("dp", "tp"),
        P("dp", "tp"),
        P("tp", "dp"),
    )
    out_specs = (P(("dp", "tp"), None, None), P(None, None, "dp"))
    return jax.shard_map(shards, mesh=mesh, in_specs=in_specs, out_specs=out_specs, check_vma=False)
```

```python
import functools

import jax
import jax.numpy as jnp
from jax import lax
from jax.experimental import pallas as pl
from jax.experimental.pallas import tpu as pltpu
from jax.sharding import PartitionSpec as P

D = 7168


MESH = pl.DeviceIdType.MESH


def loop(low, high, action):
    def body(i, carry):
        action(i)
        return carry

    lax.fori_loop(low, high, body, 0)


def move_kernel(n_dp, n_tp, chunks, picked, cache, out, loaded, stage, mid, load_sem, own_sem, send1, recv1, send2, recv2):
    group_req, piece, _ = loaded.shape
    per_pair = group_req // n_dp
    per_dev = group_req // n_tp
    rows = piece // chunks
    g = lax.axis_index("dp")
    c = lax.axis_index("tp")
    load = pltpu.make_async_copy(cache, loaded, load_sem)
    load.start()
    barrier = pltpu.get_barrier_semaphore()

    def greet_dp(i):
        pl.semaphore_signal(barrier, 1, device_id=(lax.rem(g + i, n_dp), c), device_id_type=MESH)

    def greet_tp(i):
        pl.semaphore_signal(barrier, 1, device_id=(g, lax.rem(c + i, n_tp)), device_id_type=MESH)

    loop(1, n_dp, greet_dp)
    loop(1, n_tp, greet_tp)
    pl.semaphore_wait(barrier, n_dp + n_tp - 2)
    load.wait()

    def sort(i):
        stage[i] = loaded[picked[i]]

    loop(0, group_req, sort)

    def keep(i):
        mid[per_pair * g + i] = stage[per_pair * g + i]

    loop(0, per_pair, keep)

    def over_dp(q, i, from_group):
        to_group = lax.rem(g + i, n_dp)
        part = pl.ds(q * rows, rows)
        return pltpu.make_async_remote_copy(
            src_ref=stage.at[pl.ds(per_pair * to_group, per_pair), part],
            dst_ref=mid.at[pl.ds(per_pair * from_group, per_pair), part],
            send_sem=send1.at[q, to_group],
            recv_sem=recv1.at[q, from_group],
            device_id=(to_group, c),
            device_id_type=MESH,
        )

    def over_tp(q, i, from_column):
        to_column = lax.rem(c + i, n_tp)
        return pltpu.make_async_remote_copy(
            src_ref=mid.at[pl.ds(per_dev * to_column, per_dev), pl.ds(q * rows, rows)],
            dst_ref=out.at[:, pl.ds(from_column * piece + q * rows, rows)],
            send_sem=send2.at[q, to_column],
            recv_sem=recv2.at[q, from_column],
            device_id=(g, to_column),
            device_id_type=MESH,
        )

    def own(q):
        return pltpu.make_async_copy(
            mid.at[pl.ds(per_dev * c, per_dev), pl.ds(q * rows, rows)],
            out.at[:, pl.ds(c * piece + q * rows, rows)],
            own_sem.at[q],
        )

    ahead = 2
    for q in range(chunks + 1):
        if q < chunks:
            if q >= ahead:
                loop(1, n_dp, lambda i: over_dp(q - ahead, i, g).wait_send())
            loop(1, n_dp, lambda i: over_dp(q, i, g).start())
        if q >= 1:
            loop(1, n_dp, lambda i: over_dp(q - 1, i, lax.rem(g + n_dp - i, n_dp)).wait_recv())
            loop(1, n_tp, lambda i: over_tp(q - 1, i, c).start())
            own(q - 1).start()
    for q in range(chunks):
        if q >= chunks - ahead:
            loop(1, n_dp, lambda i: over_dp(q, i, g).wait_send())
        loop(1, n_tp, lambda i: over_tp(q, i, c).wait_send())
        loop(1, n_tp, lambda i: over_tp(q, i, lax.rem(c + n_tp - i, n_tp)).wait_recv())
        own(q).wait()


def move(picked, old_cache, n_dp, n_tp):
    group_req, piece, width = old_cache.shape
    chunks = 12
    sems = pltpu.SemaphoreType.DMA
    return pl.pallas_call(
        functools.partial(move_kernel, n_dp, n_tp, chunks),
        out_shape=jax.ShapeDtypeStruct((group_req // n_tp, piece * n_tp, width), old_cache.dtype),
        in_specs=[pl.BlockSpec(memory_space=pltpu.SMEM), pl.BlockSpec(memory_space=pl.ANY)],
        out_specs=pl.BlockSpec(memory_space=pl.ANY),
        scratch_shapes=[
            pltpu.VMEM(old_cache.shape, old_cache.dtype),
            pltpu.VMEM(old_cache.shape, old_cache.dtype),
            pltpu.VMEM(old_cache.shape, old_cache.dtype),
            sems,
            sems((chunks,)),
            sems((chunks, n_dp)),
            sems((chunks, n_dp)),
            sems((chunks, n_tp)),
            sems((chunks, n_tp)),
        ],
        compiler_params=pltpu.CompilerParams(collective_id=0, has_side_effects=True, vmem_limit_bytes=48 * 2**20),
    )(picked, old_cache)


score_scale = 0.07216878364870323
norm_eps = 1e-06


def attend_kernel(lens, arrived, queries, new_latent, cache_out, lat, scores):
    f32, bf16 = jnp.float32, jnp.bfloat16
    item = pl.program_id(0)
    length = lens[item]
    context, width = arrived.shape[1:]
    heads = queries.shape[3]
    both = 2 * heads
    kv_rank = lat.shape[2]
    query = jnp.concatenate([queries[0, 0], queries[1, 0]], axis=1)
    first = new_latent[0, item].astype(f32)
    second = new_latent[1, item].astype(f32)
    block = 256
    row = lax.broadcasted_iota(jnp.int32, (block, width), 0)
    place = lax.broadcasted_iota(jnp.int32, (block, both), 0)
    last = length + lax.broadcasted_iota(jnp.int32, (block, both), 1) // heads

    def score(i, top):
        start = pl.multiple_of(i * block, block)
        rows = pl.ds(start, block)
        position = row + start
        keys = arrived[0, rows].astype(f32)
        keys = jnp.where(position < length, keys, jnp.where(position == length, first, jnp.where(position == length + 1, second, 0.0)))
        keys = keys.astype(bf16)
        cache_out[0, :, rows] = keys.T
        raw = jnp.dot(keys, query, preferred_element_type=f32) * score_scale
        raw = jnp.where(place + start <= last, raw, -jnp.inf)
        scores[rows] = raw
        return jnp.maximum(top, jnp.max(raw, axis=0, keepdims=True))

    top = lax.fori_loop(0, context // block, score, jnp.full((1, both), -jnp.inf, f32))
    exponent = jnp.exp(scores[...] - top)
    total = jnp.sum(exponent, axis=0, keepdims=True)
    mixed_t = jnp.dot(cache_out[0, :kv_rank], exponent.astype(bf16), preferred_element_type=f32)
    mixed = (mixed_t / total).T
    mixed = mixed.reshape(2, lat.shape[0], -1, kv_rank)
    mixed = jnp.concatenate([mixed[0], mixed[1]], axis=1).astype(bf16)
    lat[:, pl.ds(pl.multiple_of(item * 16, 16), 16)] = mixed


def attend(my_lengths, arrived, queries, new_latent, n_tp, kv_rank):
    items, context, width = arrived.shape
    steps, _, heads, _ = queries.shape
    bf16 = jnp.bfloat16
    flipped, latents = pl.pallas_call(
        attend_kernel,
        grid=(items,),
        out_shape=(
            jax.ShapeDtypeStruct((items, width, context), bf16),
            jax.ShapeDtypeStruct((n_tp, items * steps * heads // n_tp, kv_rank), bf16),
        ),
        in_specs=[
            pl.BlockSpec(memory_space=pltpu.SMEM),
            pl.BlockSpec((1, context, width), lambda i: (i, 0, 0)),
            pl.BlockSpec((steps, 1, width, heads), lambda i: (0, i, 0, 0)),
            pl.BlockSpec((steps, items, 1, width), lambda i: (0, 0, 0, 0)),
        ],
        out_specs=(
            pl.BlockSpec((1, width, context), lambda i: (i, 0, 0)),
            pl.BlockSpec((n_tp, items * steps * heads // n_tp, kv_rank), lambda i: (0, 0, 0)),
        ),
        scratch_shapes=[
            pltpu.VMEM((context, steps * heads), jnp.float32),
        ],
        compiler_params=pltpu.CompilerParams(vmem_limit_bytes=40 * 2**20),
    )(my_lengths, arrived, queries.transpose(0, 1, 3, 2), new_latent[:, :, None, :])
    return flipped.transpose(0, 2, 1), latents

def dense_kernel(
    lat,
    value_up,
    hidden,
    gain,
    w_out,
    w_gate,
    w_up,
    w_down,
    out,
    vup_v,
    wout_v,
    wgate_v,
    wup_v,
    wdown_v,
    latr,
    perm,
    xbuf,
    s3,
    r3,
    after,
    ybuf,
    gu,
    pair_s,
    pair_r,
    ring_s,
    ring_r,
    hbuf,
    wsem,
    lat_ss,
    lat_rs,
    x_ss,
    x_rs,
    s3_ss,
    s3_rs,
    y_ss,
    y_rs,
    pair_ss,
    pair_rs,
    ring_ss,
    ring_rs,
    h_ss,
    h_rs,
    s7_ss,
    s7_rs,
    o_ss,
    o_rs,
):
    f32, bf16 = jnp.float32, jnp.bfloat16
    g = lax.axis_index("dp")
    c = lax.axis_index("tp")
    y, k = g // 2, lax.rem(g, 2)
    z, x = c // 4, lax.rem(c, 4)
    sib = g + 1 - 2 * k
    ff = wgate_v.shape[1]
    width = 2 * ff

    def block_of(column):
        down = column // 4
        return 4 * lax.rem(lax.rem(column, 4) - down + 4, 4) + down

    mine = block_of(c)

    loads = []
    for n, (src, dst) in enumerate(
        ((value_up, vup_v), (w_out, wout_v), (w_gate, wgate_v), (w_up, wup_v), (w_down, wdown_v))
    ):
        loads.append(pltpu.make_async_copy(src, dst, wsem.at[n]))
        loads[-1].start()

    def remote(src, dst, send_sem, recv_sem, dp, tp):
        return pltpu.make_async_remote_copy(
            src_ref=src, dst_ref=dst, send_sem=send_sem, recv_sem=recv_sem, device_id=(dp, tp), device_id_type=MESH
        )

    barrier = pltpu.get_barrier_semaphore()
    loop(1, 16, lambda i: pl.semaphore_signal(barrier, 1, device_id=(g, lax.rem(c + i, 16)), device_id_type=MESH))
    loop(1, 4, lambda i: pl.semaphore_signal(barrier, 1, device_id=(lax.rem(g + 2 * i, 8), c), device_id_type=MESH))
    pl.semaphore_signal(barrier, 1, device_id=(sib, c), device_id_type=MESH)
    pl.semaphore_wait(barrier, 19)

    def lat_copy(i, source):
        to = lax.rem(c + i, 16)
        return remote(lat.at[to], latr.at[source], lat_ss.at[to], lat_rs.at[source], g, to)

    loop(1, 16, lambda i: lat_copy(i, c).start())
    latr[c] = lat[c]
    row = lax.broadcasted_iota(jnp.int32, (512, 512), 0)
    col = lax.broadcasted_iota(jnp.int32, (512, 512), 1)
    wanted = ((row & 31) >> 1) * 32 + (row & 1) * 16 + ((row >> 5) & 1) * 8 + (row >> 6)
    perm[...] = jnp.where(col == wanted, 1.0, 0.0).astype(bf16)
    loop(1, 16, lambda i: lat_copy(i, lax.rem(c + 16 - i, 16)).wait_recv())
    ordered = jnp.dot(perm[...], latr[...].reshape(512, 512), preferred_element_type=f32).astype(bf16)
    loads[0].wait()
    for head in range(8):
        part = jnp.dot(ordered[64 * head : 64 * head + 64], vup_v[head], preferred_element_type=f32)
        xbuf[0, g, :, 128 * head : 128 * head + 128] = part[:32].astype(bf16)
        xbuf[1, g, :, 128 * head : 128 * head + 128] = part[32:].astype(bf16)

    def gather_ring(buf, ss, rs, s, i, source):
        to = lax.rem(g + 2 * i, 8)
        return remote(buf.at[s, g], buf.at[s, source], ss.at[s, i], rs.at[s, source], to, c)

    def gather_pair(buf, ss, rs, s, i, sent, got):
        return remote(buf.at[s, sent], buf.at[s, got], ss.at[s, 4 + i], rs.at[s, got], sib, c)

    def gather_start(buf, ss, rs, s):
        loop(1, 4, lambda i: gather_ring(buf, ss, rs, s, i, g).start())
        gather_pair(buf, ss, rs, s, 0, g, g).start()

    def gather_rest(buf, ss, rs, s):
        def forward(i):
            src = lax.rem(g + 8 - 2 * i, 8)
            gather_ring(buf, ss, rs, s, i, src).wait_recv()
            gather_pair(buf, ss, rs, s, i, src, src).start()

        loop(1, 4, forward)
        loop(0, 4, lambda i: gather_pair(buf, ss, rs, s, i, g, lax.rem(sib + 8 - 2 * i, 8)).wait_recv())

    def gather_end(buf, ss, rs, s):
        loop(1, 4, lambda i: gather_ring(buf, ss, rs, s, i, g).wait_send())
        loop(0, 4, lambda i: gather_pair(buf, ss, rs, s, i, g, g).wait_send())

    def scatter_copy(ss, rs, s, i, source):
        to = lax.rem(c + i, 16)
        return remote(s3.at[s, block_of(to)], r3.at[s, source], ss.at[s, to], rs.at[s, source], g, to)

    def scatter(value, ss, rs, s):
        s3[s] = value.reshape(16, 16, value.shape[1]).astype(bf16)
        loop(1, 16, lambda i: scatter_copy(ss, rs, s, i, c).start())

    def scatter_sum(ss, rs, s, first):
        r3[s, c] = s3[s, mine]
        loop(1, 16, lambda i: scatter_copy(ss, rs, s, i, lax.rem(c + 16 - i, 16)).wait_recv())
        total = first + jnp.sum(r3[s].astype(f32), axis=0)
        loop(1, 16, lambda i: scatter_copy(ss, rs, s, i, c).wait_send())
        return total

    def spread(buf, ss, rs, s, i, source):
        to = lax.rem(c + i, 16)
        return remote(buf.at[s, mine], buf.at[s, block_of(source)], ss.at[s, to], rs.at[s, source], g, to)

    def spread_start(buf, ss, rs, s):
        loop(1, 16, lambda i: spread(buf, ss, rs, s, i, c).start())

    def spread_wait(buf, ss, rs, s):
        loop(1, 16, lambda i: spread(buf, ss, rs, s, i, lax.rem(c + 16 - i, 16)).wait_recv())

    def spread_end(buf, ss, rs, s):
        loop(1, 16, lambda i: spread(buf, ss, rs, s, i, c).wait_send())

    loop(0, 2, lambda s: gather_start(xbuf, x_ss, x_rs, s))
    loads[1].wait()

    def out_stage(s):
        gather_rest(xbuf, x_ss, x_rs, s)
        rows = xbuf[s].reshape(256, xbuf.shape[3])
        scatter(jnp.dot(rows, wout_v[...], preferred_element_type=f32), s3_ss, s3_rs, s)

    loop(0, 2, out_stage)

    def after_stage(s):
        after[s] = scatter_sum(s3_ss, s3_rs, s, hidden[s, mine].astype(f32))
        ybuf[s, mine] = after[s].astype(bf16)
        spread_start(ybuf, y_ss, y_rs, s)

    loop(0, 2, after_stage)
    loads[2].wait()
    loads[3].wait()
    lane = lax.broadcasted_iota(jnp.int32, (32, 128), 1)

    def two_part(total):
        high = total.astype(bf16)
        low = (total - high.astype(f32)).astype(bf16)
        return jnp.where(lane < 64, high.astype(f32), low.astype(f32)).astype(bf16)

    def one_part(pair):
        return pair[:, 0:1].astype(f32) + pair[:, 64:65].astype(f32)

    def pair_copy(s, chunk):
        return remote(pair_s.at[s, chunk], pair_r.at[s, chunk], pair_ss.at[s, chunk], pair_rs.at[s, chunk], sib, c)

    def ring_copy(s, chunk, source):
        return remote(
            ring_s.at[s, chunk], ring_r.at[s, source], ring_ss.at[s, chunk], ring_rs.at[s, source], 2 * chunk + k, c
        )

    def gate_stage(s):
        spread_wait(ybuf, y_ss, y_rs, s)
        rows = ybuf[s].reshape(256, ybuf.shape[3]).astype(f32)
        squares = jnp.sum(rows * rows, axis=1, keepdims=True)
        scaled = (rows * gain[...]).astype(bf16)
        gu[s, :, :, :, width : width + 128] = jnp.broadcast_to(squares, (256, 128)).reshape(4, 2, 32, 128)
        gu[s, :, :, :, 0:ff] = jnp.dot(scaled, wgate_v[...], preferred_element_type=f32).reshape(4, 2, 32, ff)
        gu[s, :, :, :, ff:width] = jnp.dot(scaled, wup_v[...], preferred_element_type=f32).reshape(4, 2, 32, ff)

        def give(i):
            chunk = lax.rem(y + 1 + i, 4)
            pair_s[s, chunk, :, 0:width] = gu[s, chunk, 1 - k, :, 0:width].astype(bf16)
            pair_s[s, chunk, :, width : width + 128] = two_part(gu[s, chunk, 1 - k, :, width : width + 128])
            pair_copy(s, chunk).start()

        loop(0, 4, give)

        def merge(i):
            chunk = lax.rem(y + 1 + i, 4)
            pair_copy(s, chunk).wait_recv()
            total = gu[s, chunk, k, :, 0:width] + pair_r[s, chunk, :, 0:width].astype(f32)
            squares = gu[s, chunk, k, :, width : width + 128] + one_part(pair_r[s, chunk, :, width : width + 128])
            gu[s, chunk, k, :, 0:width] = total
            gu[s, chunk, k, :, width : width + 128] = squares

            @pl.when(chunk != y)
            def _():
                ring_s[s, chunk, :, 0:width] = total.astype(bf16)
                ring_s[s, chunk, :, width : width + 128] = two_part(squares)
                ring_copy(s, chunk, y).start()

        loop(0, 4, merge)

    loop(0, 2, gate_stage)

    def act_stage(s):
        def ring_add(i):
            source = lax.rem(y + i, 4)
            ring_copy(s, source, source).wait_recv()
            gu[s, y, k, :, 0:width] += ring_r[s, source, :, 0:width].astype(f32)
            gu[s, y, k, :, width : width + 128] += one_part(ring_r[s, source, :, width : width + 128])

        loop(1, 4, ring_add)
        scale = 1.0 / jnp.sqrt(gu[s, y, k, :, width : width + 1] / D + norm_eps)
        gate = gu[s, y, k, :, 0:ff] * scale
        up = gu[s, y, k, :, ff:width] * scale
        hbuf[s, g] = (jax.nn.silu(gate) * up).astype(bf16)
        gather_start(hbuf, h_ss, h_rs, s)

    loop(0, 2, act_stage)
    loads[4].wait()

    def down_stage(s):
        gather_rest(hbuf, h_ss, h_rs, s)
        rows = hbuf[s].reshape(256, ff)
        scatter(jnp.dot(rows, wdown_v[...], preferred_element_type=f32), s7_ss, s7_rs, s)

    loop(0, 2, down_stage)

    def result_stage(s):
        out[s, mine] = scatter_sum(s7_ss, s7_rs, s, after[s]).astype(bf16)
        spread_start(out, o_ss, o_rs, s)

    loop(0, 2, result_stage)
    loop(1, 16, lambda i: lat_copy(i, c).wait_send())

    def end_stage(s):
        gather_end(xbuf, x_ss, x_rs, s)
        spread_end(ybuf, y_ss, y_rs, s)
        loop(0, 4, lambda i: pair_copy(s, i).wait_send())
        loop(1, 4, lambda i: ring_copy(s, lax.rem(y + i, 4), y).wait_send())
        gather_end(hbuf, h_ss, h_rs, s)
        spread_end(out, o_ss, o_rs, s)
        spread_wait(out, o_ss, o_rs, s)

    loop(0, 2, end_stage)


def dense(lat, value_up, hidden, gain, w_out, w_gate, w_up, w_down):
    steps, total, cols = hidden.shape
    ff = w_gate.shape[1]
    bf16, f32 = jnp.bfloat16, jnp.float32
    vmem, sems = pltpu.VMEM, pltpu.SemaphoreType.DMA
    in_vmem, anywhere = pl.BlockSpec(memory_space=pltpu.VMEM), pl.BlockSpec(memory_space=pl.ANY)
    result = pl.pallas_call(
        dense_kernel,
        out_shape=jax.ShapeDtypeStruct((steps, 16, 16, cols), bf16),
        in_specs=[in_vmem, anywhere, in_vmem, in_vmem, anywhere, anywhere, anywhere, anywhere],
        out_specs=in_vmem,
        scratch_shapes=[
            vmem(value_up.shape, bf16),
            vmem(w_out.shape, bf16),
            vmem(w_gate.shape, bf16),
            vmem(w_up.shape, bf16),
            vmem(w_down.shape, bf16),
            vmem(lat.shape, bf16),
            vmem((512, 512), bf16),
            vmem((2, 8, 32, w_out.shape[0]), bf16),
            vmem((2, 16, 16, cols), bf16),
            vmem((2, 16, 16, cols), bf16),
            vmem((2, 16, cols), f32),
            vmem((2, 16, 16, cols), bf16),
            vmem((2, 4, 2, 32, 2 * ff + 128), f32),
            vmem((2, 4, 32, 2 * ff + 128), bf16),
            vmem((2, 4, 32, 2 * ff + 128), bf16),
            vmem((2, 4, 32, 2 * ff + 128), bf16),
            vmem((2, 4, 32, 2 * ff + 128), bf16),
            vmem((2, 8, 32, ff), bf16),
            sems((5,)),
            sems((16,)),
            sems((16,)),
            sems((2, 8)),
            sems((2, 8)),
            sems((2, 16)),
            sems((2, 16)),
            sems((2, 16)),
            sems((2, 16)),
            sems((2, 4)),
            sems((2, 4)),
            sems((2, 4)),
            sems((2, 4)),
            sems((2, 8)),
            sems((2, 8)),
            sems((2, 16)),
            sems((2, 16)),
            sems((2, 16)),
            sems((2, 16)),
        ],
        compiler_params=pltpu.CompilerParams(collective_id=1, has_side_effects=True, vmem_limit_bytes=52 * 2**20),
    )(lat, value_up, hidden.reshape(steps, 16, 16, cols), gain, w_out, w_gate, w_up, w_down)
    return result.reshape(steps, total, cols)


def shards(
    old_cache,
    lengths,
    new_slot,
    queries,
    new_latent,
    hidden,
    value_up_weight,
    w_out,
    norm_gain,
    w_gate,
    w_up,
    w_down,
):
    dp_count = lax.axis_size("dp")
    tp_count = lax.axis_size("tp")
    my_group = lax.axis_index("dp")
    my_column = lax.axis_index("tp")
    group_req = old_cache.shape[0]
    per_pair = group_req // dp_count
    req_dev = queries.shape[1]
    req_total = new_slot.shape[0]
    kv_rank = value_up_weight.shape[1]
    everyone = jnp.arange(req_total, dtype=jnp.int32)
    new_group = new_slot // group_req
    pair_rank = new_slot % group_req - everyone // group_req * per_pair
    my_targets = lax.dynamic_slice_in_dim(
        new_group * per_pair + pair_rank, my_group * group_req, group_req
    )
    target_places = jnp.arange(group_req, dtype=jnp.int32)
    picked = jnp.sum(
        jnp.where(my_targets[None, :] == target_places[:, None], target_places[None, :], 0), axis=1
    )
    arrived = move(picked, old_cache, dp_count, tp_count)
    source = jnp.sum(
        jnp.where(new_slot[None, :] == everyone[:, None], everyone[None, :], 0), axis=1
    )
    my_slots = (my_group * tp_count + my_column) * req_dev + jnp.arange(req_dev, dtype=jnp.int32)
    my_lengths = jnp.take(lengths, jnp.take(source, my_slots))
    new_cache, latents = attend(my_lengths, arrived, queries, new_latent, tp_count, kv_rank)
    gain = norm_gain.astype(jnp.float32)[None, :]
    layer_out = dense(latents, value_up_weight, hidden, gain, w_out, w_gate, w_up, w_down)
    return (new_cache, layer_out)


def solution(mesh):
    in_specs = (
        P("dp", "tp", None),
        P(),
        P(),
        P(None, ("dp", "tp"), None, None),
        P(None, ("dp", "tp"), None),
        P(None, None, "dp"),
        P("tp", None, None),
        P("tp", "dp"),
        P("dp"),
        P("dp", "tp"),
        P("dp", "tp"),
        P("tp", "dp"),
    )
    out_specs = (P(("dp", "tp"), None, None), P(None, None, "dp"))
    return jax.shard_map(shards, mesh=mesh, in_specs=in_specs, out_specs=out_specs, check_vma=False)
```

```python
import functools

import jax
import jax.numpy as jnp
from jax import lax
from jax.experimental import pallas as pl
from jax.experimental.pallas import tpu as pltpu
from jax.sharding import PartitionSpec as P

D = 7168


MESH = pl.DeviceIdType.MESH


def loop(low, high, action):
    def body(i, carry):
        action(i)
        return carry

    lax.fori_loop(low, high, body, 0)


def move_kernel(
    n_dp, n_tp, chunks, ahead, picked, cache, out, loaded, stage, mid, load_sem, own_sem, send1, recv1, send2, recv2
):
    group_req, piece, width = loaded.shape
    rows = piece // chunks
    rank = (stage.shape[2] - 128) // 2
    pairs = n_tp // n_dp
    g = lax.axis_index("dp")
    c = lax.axis_index("tp")

    load = pltpu.make_async_copy(cache, loaded, load_sem)
    load.start()
    barrier = pltpu.get_barrier_semaphore()

    def greet_dp(i):
        pl.semaphore_signal(barrier, 1, device_id=(lax.rem(g + i, n_dp), c), device_id_type=MESH)

    def greet_tp(i):
        pl.semaphore_signal(barrier, 1, device_id=(g, lax.rem(c + i, n_tp)), device_id_type=MESH)

    loop(1, n_dp, greet_dp)
    loop(1, n_tp, greet_tp)
    pl.semaphore_wait(barrier, n_dp + n_tp - 2)
    load.wait()

    def sort(q):
        part = pl.ds(q * rows, rows)

        def one(i):
            first = picked[2 * i]
            second = picked[2 * i + 1]
            stage[i, part, 0:rank] = loaded[first, part, 0:rank]
            stage[i, part, rank : 2 * rank] = loaded[second, part, 0:rank]
            tails = [loaded[first, part, rank:width], loaded[second, part, rank:width]]
            stage[i, part, 2 * rank :] = jnp.concatenate(tails, axis=1)

        loop(0, n_tp, one)
        for n in range(pairs):
            mid[pairs * g + n, part] = stage[pairs * g + n, part]

    def over_dp(q, i, from_group):
        to_group = lax.rem(g + i, n_dp)
        part = pl.ds(q * rows, rows)
        return pltpu.make_async_remote_copy(
            src_ref=stage.at[pl.ds(pairs * to_group, pairs), part],
            dst_ref=mid.at[pl.ds(pairs * from_group, pairs), part],
            send_sem=send1.at[q, to_group],
            recv_sem=recv1.at[q, from_group],
            device_id=(to_group, c),
            device_id_type=MESH,
        )

    def over_tp(q, i, from_column):
        to_column = lax.rem(c + i, n_tp)
        return pltpu.make_async_remote_copy(
            src_ref=mid.at[to_column, pl.ds(q * rows, rows)],
            dst_ref=out.at[pl.ds(from_column * piece + q * rows, rows)],
            send_sem=send2.at[q, to_column],
            recv_sem=recv2.at[q, from_column],
            device_id=(g, to_column),
            device_id_type=MESH,
        )

    def own(q):
        return pltpu.make_async_copy(
            mid.at[c, pl.ds(q * rows, rows)], out.at[pl.ds(c * piece + q * rows, rows)], own_sem.at[q]
        )

    for q in range(chunks + 1):
        if q < chunks:
            sort(q)
            if q >= ahead:
                loop(1, n_dp, lambda i: over_dp(q - ahead, i, g).wait_send())
            loop(1, n_dp, lambda i: over_dp(q, i, g).start())
        if q >= 1:
            loop(1, n_dp, lambda i: over_dp(q - 1, i, lax.rem(g + n_dp - i, n_dp)).wait_recv())
            loop(1, n_tp, lambda i: over_tp(q - 1, i, c).start())
            own(q - 1).start()
    for q in range(chunks):
        if q >= chunks - ahead:
            loop(1, n_dp, lambda i: over_dp(q, i, g).wait_send())
        loop(1, n_tp, lambda i: over_tp(q, i, c).wait_send())
        loop(1, n_tp, lambda i: over_tp(q, i, lax.rem(c + n_tp - i, n_tp)).wait_recv())
        own(q).wait()


def move(picked, old_cache, n_dp, n_tp, chunks=12, ahead=2):
    group_req, piece, width = old_cache.shape
    packed = (n_tp, piece, 2 * width)
    sems = pltpu.SemaphoreType.DMA
    return pl.pallas_call(
        functools.partial(move_kernel, n_dp, n_tp, chunks, ahead),
        out_shape=jax.ShapeDtypeStruct((piece * n_tp, 2 * width), old_cache.dtype),
        in_specs=[pl.BlockSpec(memory_space=pltpu.SMEM), pl.BlockSpec(memory_space=pl.ANY)],
        out_specs=pl.BlockSpec(memory_space=pl.ANY),
        scratch_shapes=[
            pltpu.VMEM(old_cache.shape, old_cache.dtype),
            pltpu.VMEM(packed, old_cache.dtype),
            pltpu.VMEM(packed, old_cache.dtype),
            sems,
            sems((chunks,)),
            sems((chunks, n_dp)),
            sems((chunks, n_dp)),
            sems((chunks, n_tp)),
            sems((chunks, n_tp)),
        ],
        compiler_params=pltpu.CompilerParams(collective_id=0, has_side_effects=True, vmem_limit_bytes=48 * 2**20),
    )(picked, old_cache)


score_scale = 0.07216878364870323
norm_eps = 1e-06


def attend_kernel(lens, main, tail, queries, new_main, new_tail, cache_out, lat, scores, query):
    f32, bf16 = jnp.float32, jnp.bfloat16
    item = pl.program_id(0)
    length = lens[item]
    context, rank = main.shape
    heads = queries.shape[3]
    both = 2 * heads
    query[:rank] = jnp.concatenate([queries[0, 0, :rank], queries[1, 0, :rank]], axis=1)
    query[rank:] = jnp.zeros((128, both), bf16)
    half = pl.multiple_of(rank + item * 64, 64)
    query[pl.ds(half, 64)] = jnp.concatenate([queries[0, 0, rank:], queries[1, 0, rank:]], axis=1)
    block = context // 2
    row = lax.broadcasted_iota(jnp.int32, (block, rank), 0)
    tail_row = lax.broadcasted_iota(jnp.int32, (block, 128), 0)
    tail_length = jnp.where(lax.broadcasted_iota(jnp.int32, (block, 128), 1) < 64, lens[0], lens[1])
    place = lax.broadcasted_iota(jnp.int32, (block, both), 0)
    last = length + lax.broadcasted_iota(jnp.int32, (block, both), 1) // heads

    def fill(old, position, size, first, second):
        new = jnp.where(position == size, first.astype(f32), jnp.where(position == size + 1, second.astype(f32), 0.0))
        return jnp.where(position < size, old.astype(f32), new).astype(bf16)

    def score(i, top):
        start = pl.multiple_of(i * block, block)
        rows = pl.ds(start, block)
        keys = fill(main[rows], row + start, length, new_main[0, item], new_main[1, item])
        tails = fill(tail[rows], tail_row + start, tail_length, new_tail[0], new_tail[1])
        cache_out[0, :rank, rows] = keys.T
        tails_t = tails.T

        @pl.when(item == 0)
        def _():
            cache_out[0, rank:, rows] = tails_t[:64]

        @pl.when(item == 1)
        def _():
            cache_out[0, rank:, rows] = tails_t[64:]

        both_parts = jnp.concatenate([keys, tails], axis=1)
        raw = jnp.dot(both_parts, query[...], preferred_element_type=f32)
        raw = jnp.where(place + start <= last, raw * score_scale, -jnp.inf)
        scores[rows] = raw
        return jnp.maximum(top, jnp.max(raw, axis=0, keepdims=True))

    top = lax.fori_loop(0, context // block, score, jnp.full((1, both), -jnp.inf, f32))
    exponent = jnp.exp(scores[...] - top)
    total = jnp.sum(exponent, axis=0, keepdims=True)
    mixed_t = jnp.dot(cache_out[0, :rank], exponent.astype(bf16), preferred_element_type=f32)
    mixed = (mixed_t / total).T
    mixed = mixed.reshape(2, lat.shape[0], -1, rank)
    mixed = jnp.concatenate([mixed[0], mixed[1]], axis=1).astype(bf16)
    lat[:, pl.ds(pl.multiple_of(item * 16, 16), 16)] = mixed


def attend(my_lengths, arrived, queries, new_latent, n_tp, kv_rank):
    context = arrived.shape[0]
    steps, items, heads, width = queries.shape
    bf16 = jnp.bfloat16
    new_tail = new_latent[:, :, kv_rank:].reshape(steps, 1, -1)
    flipped, latents = pl.pallas_call(
        attend_kernel,
        grid=(items,),
        out_shape=(
            jax.ShapeDtypeStruct((items, width, context), bf16),
            jax.ShapeDtypeStruct((n_tp, items * steps * heads // n_tp, kv_rank), bf16),
        ),
        in_specs=[
            pl.BlockSpec(memory_space=pltpu.SMEM),
            pl.BlockSpec((context, kv_rank), lambda i: (0, i)),
            pl.BlockSpec((context, 128), lambda i: (0, 2 * kv_rank // 128)),
            pl.BlockSpec((steps, 1, width, heads), lambda i: (0, i, 0, 0)),
            pl.BlockSpec((steps, items, 1, kv_rank), lambda i: (0, 0, 0, 0)),
            pl.BlockSpec((steps, 1, 128), lambda i: (0, 0, 0)),
        ],
        out_specs=(
            pl.BlockSpec((1, width, context), lambda i: (i, 0, 0)),
            pl.BlockSpec((n_tp, items * steps * heads // n_tp, kv_rank), lambda i: (0, 0, 0)),
        ),
        scratch_shapes=[
            pltpu.VMEM((context, steps * heads), jnp.float32),
            pltpu.VMEM((kv_rank + 128, steps * heads), bf16),
        ],
        compiler_params=pltpu.CompilerParams(vmem_limit_bytes=40 * 2**20),
    )(my_lengths, arrived, arrived, queries.transpose(0, 1, 3, 2), new_latent[:, :, None, :kv_rank], new_tail)
    return flipped.transpose(0, 2, 1), latents


def dense_kernel(
    lat,
    value_up,
    hidden,
    gain,
    w_out,
    w_gate,
    w_up,
    w_down,
    out,
    vup_v,
    wout_v,
    wgate_v,
    wup_v,
    wdown_v,
    latr,
    perm,
    xbuf,
    s3,
    r3,
    after,
    ybuf,
    gu,
    pair_s,
    pair_r,
    ring_s,
    ring_r,
    hbuf,
    wsem,
    lat_ss,
    lat_rs,
    x_ss,
    x_rs,
    s3_ss,
    s3_rs,
    y_ss,
    y_rs,
    pair_ss,
    pair_rs,
    ring_ss,
    ring_rs,
    h_ss,
    h_rs,
    s7_ss,
    s7_rs,
    o_ss,
    o_rs,
):
    f32, bf16 = jnp.float32, jnp.bfloat16
    g = lax.axis_index("dp")
    c = lax.axis_index("tp")
    y, k = g // 2, lax.rem(g, 2)
    z, x = c // 4, lax.rem(c, 4)
    sib = g + 1 - 2 * k
    ff = wgate_v.shape[1]
    width = 2 * ff

    def block_of(column):
        down = column // 4
        return 4 * lax.rem(lax.rem(column, 4) - down + 4, 4) + down

    mine = block_of(c)

    loads = []
    for n, (src, dst) in enumerate(
        ((value_up, vup_v), (w_out, wout_v), (w_gate, wgate_v), (w_up, wup_v), (w_down, wdown_v))
    ):
        loads.append(pltpu.make_async_copy(src, dst, wsem.at[n]))
        loads[-1].start()

    def remote(src, dst, send_sem, recv_sem, dp, tp):
        return pltpu.make_async_remote_copy(
            src_ref=src, dst_ref=dst, send_sem=send_sem, recv_sem=recv_sem, device_id=(dp, tp), device_id_type=MESH
        )

    barrier = pltpu.get_barrier_semaphore()
    loop(1, 16, lambda i: pl.semaphore_signal(barrier, 1, device_id=(g, lax.rem(c + i, 16)), device_id_type=MESH))
    loop(1, 4, lambda i: pl.semaphore_signal(barrier, 1, device_id=(lax.rem(g + 2 * i, 8), c), device_id_type=MESH))
    pl.semaphore_signal(barrier, 1, device_id=(sib, c), device_id_type=MESH)
    pl.semaphore_wait(barrier, 19)

    def lat_copy(i, source):
        to = lax.rem(c + i, 16)
        return remote(lat.at[to], latr.at[source], lat_ss.at[to], lat_rs.at[source], g, to)

    loop(1, 16, lambda i: lat_copy(i, c).start())
    latr[c] = lat[c]
    row = lax.broadcasted_iota(jnp.int32, (512, 512), 0)
    col = lax.broadcasted_iota(jnp.int32, (512, 512), 1)
    wanted = ((row & 31) >> 1) * 32 + (row & 1) * 16 + ((row >> 5) & 1) * 8 + (row >> 6)
    perm[...] = jnp.where(col == wanted, 1.0, 0.0).astype(bf16)
    loop(1, 16, lambda i: lat_copy(i, lax.rem(c + 16 - i, 16)).wait_recv())
    ordered = jnp.dot(perm[...], latr[...].reshape(512, 512), preferred_element_type=f32).astype(bf16)
    loads[0].wait()
    for head in range(8):
        part = jnp.dot(ordered[64 * head : 64 * head + 64], vup_v[head], preferred_element_type=f32)
        xbuf[0, g, :, 128 * head : 128 * head + 128] = part[:32].astype(bf16)
        xbuf[1, g, :, 128 * head : 128 * head + 128] = part[32:].astype(bf16)

    def gather_ring(buf, ss, rs, s, i, source):
        to = lax.rem(g + 2 * i, 8)
        return remote(buf.at[s, g], buf.at[s, source], ss.at[s, i], rs.at[s, source], to, c)

    def gather_pair(buf, ss, rs, s, i, sent, got):
        return remote(buf.at[s, sent], buf.at[s, got], ss.at[s, 4 + i], rs.at[s, got], sib, c)

    def gather_start(buf, ss, rs, s):
        loop(1, 4, lambda i: gather_ring(buf, ss, rs, s, i, g).start())
        gather_pair(buf, ss, rs, s, 0, g, g).start()

    def gather_rest(buf, ss, rs, s):
        def forward(i):
            src = lax.rem(g + 8 - 2 * i, 8)
            gather_ring(buf, ss, rs, s, i, src).wait_recv()
            gather_pair(buf, ss, rs, s, i, src, src).start()

        loop(1, 4, forward)
        loop(0, 4, lambda i: gather_pair(buf, ss, rs, s, i, g, lax.rem(sib + 8 - 2 * i, 8)).wait_recv())

    def gather_end(buf, ss, rs, s):
        loop(1, 4, lambda i: gather_ring(buf, ss, rs, s, i, g).wait_send())
        loop(0, 4, lambda i: gather_pair(buf, ss, rs, s, i, g, g).wait_send())

    def scatter_copy(ss, rs, s, i, source):
        to = lax.rem(c + i, 16)
        return remote(s3.at[s, block_of(to)], r3.at[s, source], ss.at[s, to], rs.at[s, source], g, to)

    def scatter(value, ss, rs, s):
        s3[s] = value.reshape(16, 16, value.shape[1]).astype(bf16)
        loop(1, 16, lambda i: scatter_copy(ss, rs, s, i, c).start())

    def scatter_sum(ss, rs, s, first):
        r3[s, c] = s3[s, mine]
        loop(1, 16, lambda i: scatter_copy(ss, rs, s, i, lax.rem(c + 16 - i, 16)).wait_recv())
        total = first + jnp.sum(r3[s].astype(f32), axis=0)
        loop(1, 16, lambda i: scatter_copy(ss, rs, s, i, c).wait_send())
        return total

    def spread(buf, ss, rs, s, i, source):
        to = lax.rem(c + i, 16)
        return remote(buf.at[s, mine], buf.at[s, block_of(source)], ss.at[s, to], rs.at[s, source], g, to)

    def spread_start(buf, ss, rs, s):
        loop(1, 16, lambda i: spread(buf, ss, rs, s, i, c).start())

    def spread_wait(buf, ss, rs, s):
        loop(1, 16, lambda i: spread(buf, ss, rs, s, i, lax.rem(c + 16 - i, 16)).wait_recv())

    def spread_end(buf, ss, rs, s):
        loop(1, 16, lambda i: spread(buf, ss, rs, s, i, c).wait_send())

    loop(0, 2, lambda s: gather_start(xbuf, x_ss, x_rs, s))
    loads[1].wait()

    def out_stage(s):
        gather_rest(xbuf, x_ss, x_rs, s)
        rows = xbuf[s].reshape(256, xbuf.shape[3])
        scatter(jnp.dot(rows, wout_v[...], preferred_element_type=f32), s3_ss, s3_rs, s)

    loop(0, 2, out_stage)

    def after_stage(s):
        after[s] = scatter_sum(s3_ss, s3_rs, s, hidden[s, mine].astype(f32))
        ybuf[s, mine] = after[s].astype(bf16)
        spread_start(ybuf, y_ss, y_rs, s)

    loop(0, 2, after_stage)
    loads[2].wait()
    loads[3].wait()
    lane = lax.broadcasted_iota(jnp.int32, (32, 128), 1)

    def two_part(total):
        high = total.astype(bf16)
        low = (total - high.astype(f32)).astype(bf16)
        return jnp.where(lane < 64, high.astype(f32), low.astype(f32)).astype(bf16)

    def one_part(pair):
        return pair[:, 0:1].astype(f32) + pair[:, 64:65].astype(f32)

    def pair_copy(s, chunk):
        return remote(pair_s.at[s, chunk], pair_r.at[s, chunk], pair_ss.at[s, chunk], pair_rs.at[s, chunk], sib, c)

    def ring_copy(s, chunk, source):
        return remote(
            ring_s.at[s, chunk], ring_r.at[s, source], ring_ss.at[s, chunk], ring_rs.at[s, source], 2 * chunk + k, c
        )

    def gate_stage(s):
        spread_wait(ybuf, y_ss, y_rs, s)
        rows = ybuf[s].reshape(256, ybuf.shape[3]).astype(f32)
        squares = jnp.sum(rows * rows, axis=1, keepdims=True)
        scaled = (rows * gain[...]).astype(bf16)
        gu[s, :, :, :, width : width + 128] = jnp.broadcast_to(squares, (256, 128)).reshape(4, 2, 32, 128)
        gu[s, :, :, :, 0:ff] = jnp.dot(scaled, wgate_v[...], preferred_element_type=f32).reshape(4, 2, 32, ff)
        gu[s, :, :, :, ff:width] = jnp.dot(scaled, wup_v[...], preferred_element_type=f32).reshape(4, 2, 32, ff)

        def give(i):
            chunk = lax.rem(y + 1 + i, 4)
            pair_s[s, chunk, :, 0:width] = gu[s, chunk, 1 - k, :, 0:width].astype(bf16)
            pair_s[s, chunk, :, width : width + 128] = two_part(gu[s, chunk, 1 - k, :, width : width + 128])
            pair_copy(s, chunk).start()

        loop(0, 4, give)

        def merge(i):
            chunk = lax.rem(y + 1 + i, 4)
            pair_copy(s, chunk).wait_recv()
            total = gu[s, chunk, k, :, 0:width] + pair_r[s, chunk, :, 0:width].astype(f32)
            squares = gu[s, chunk, k, :, width : width + 128] + one_part(pair_r[s, chunk, :, width : width + 128])
            gu[s, chunk, k, :, 0:width] = total
            gu[s, chunk, k, :, width : width + 128] = squares

            @pl.when(chunk != y)
            def _():
                ring_s[s, chunk, :, 0:width] = total.astype(bf16)
                ring_s[s, chunk, :, width : width + 128] = two_part(squares)
                ring_copy(s, chunk, y).start()

        loop(0, 4, merge)

    loop(0, 2, gate_stage)

    def act_stage(s):
        def ring_add(i):
            source = lax.rem(y + i, 4)
            ring_copy(s, source, source).wait_recv()
            gu[s, y, k, :, 0:width] += ring_r[s, source, :, 0:width].astype(f32)
            gu[s, y, k, :, width : width + 128] += one_part(ring_r[s, source, :, width : width + 128])

        loop(1, 4, ring_add)
        scale = 1.0 / jnp.sqrt(gu[s, y, k, :, width : width + 1] / D + norm_eps)
        gate = gu[s, y, k, :, 0:ff] * scale
        up = gu[s, y, k, :, ff:width] * scale
        hbuf[s, g] = (jax.nn.silu(gate) * up).astype(bf16)
        gather_start(hbuf, h_ss, h_rs, s)

    loop(0, 2, act_stage)
    loads[4].wait()

    def down_stage(s):
        gather_rest(hbuf, h_ss, h_rs, s)
        rows = hbuf[s].reshape(256, ff)
        scatter(jnp.dot(rows, wdown_v[...], preferred_element_type=f32), s7_ss, s7_rs, s)

    loop(0, 2, down_stage)

    def result_stage(s):
        out[s, mine] = scatter_sum(s7_ss, s7_rs, s, after[s]).astype(bf16)
        spread_start(out, o_ss, o_rs, s)

    loop(0, 2, result_stage)
    loop(1, 16, lambda i: lat_copy(i, c).wait_send())

    def end_stage(s):
        gather_end(xbuf, x_ss, x_rs, s)
        spread_end(ybuf, y_ss, y_rs, s)
        loop(0, 4, lambda i: pair_copy(s, i).wait_send())
        loop(1, 4, lambda i: ring_copy(s, lax.rem(y + i, 4), y).wait_send())
        gather_end(hbuf, h_ss, h_rs, s)
        spread_end(out, o_ss, o_rs, s)
        spread_wait(out, o_ss, o_rs, s)

    loop(0, 2, end_stage)


def dense(lat, value_up, hidden, gain, w_out, w_gate, w_up, w_down):
    steps, total, cols = hidden.shape
    ff = w_gate.shape[1]
    bf16, f32 = jnp.bfloat16, jnp.float32
    vmem, sems = pltpu.VMEM, pltpu.SemaphoreType.DMA
    in_vmem, anywhere = pl.BlockSpec(memory_space=pltpu.VMEM), pl.BlockSpec(memory_space=pl.ANY)
    result = pl.pallas_call(
        dense_kernel,
        out_shape=jax.ShapeDtypeStruct((steps, 16, 16, cols), bf16),
        in_specs=[in_vmem, anywhere, in_vmem, in_vmem, anywhere, anywhere, anywhere, anywhere],
        out_specs=in_vmem,
        scratch_shapes=[
            vmem(value_up.shape, bf16),
            vmem(w_out.shape, bf16),
            vmem(w_gate.shape, bf16),
            vmem(w_up.shape, bf16),
            vmem(w_down.shape, bf16),
            vmem(lat.shape, bf16),
            vmem((512, 512), bf16),
            vmem((2, 8, 32, w_out.shape[0]), bf16),
            vmem((2, 16, 16, cols), bf16),
            vmem((2, 16, 16, cols), bf16),
            vmem((2, 16, cols), f32),
            vmem((2, 16, 16, cols), bf16),
            vmem((2, 4, 2, 32, 2 * ff + 128), f32),
            vmem((2, 4, 32, 2 * ff + 128), bf16),
            vmem((2, 4, 32, 2 * ff + 128), bf16),
            vmem((2, 4, 32, 2 * ff + 128), bf16),
            vmem((2, 4, 32, 2 * ff + 128), bf16),
            vmem((2, 8, 32, ff), bf16),
            sems((5,)),
            sems((16,)),
            sems((16,)),
            sems((2, 8)),
            sems((2, 8)),
            sems((2, 16)),
            sems((2, 16)),
            sems((2, 16)),
            sems((2, 16)),
            sems((2, 4)),
            sems((2, 4)),
            sems((2, 4)),
            sems((2, 4)),
            sems((2, 8)),
            sems((2, 8)),
            sems((2, 16)),
            sems((2, 16)),
            sems((2, 16)),
            sems((2, 16)),
        ],
        compiler_params=pltpu.CompilerParams(collective_id=1, has_side_effects=True, vmem_limit_bytes=52 * 2**20),
    )(lat, value_up, hidden.reshape(steps, 16, 16, cols), gain, w_out, w_gate, w_up, w_down)
    return result.reshape(steps, total, cols)


def shards(
    old_cache,
    lengths,
    new_slot,
    queries,
    new_latent,
    hidden,
    value_up_weight,
    w_out,
    norm_gain,
    w_gate,
    w_up,
    w_down,
):
    dp_count = lax.axis_size("dp")
    tp_count = lax.axis_size("tp")
    my_group = lax.axis_index("dp")
    my_column = lax.axis_index("tp")
    group_req = old_cache.shape[0]
    per_pair = group_req // dp_count
    req_dev = queries.shape[1]
    req_total = new_slot.shape[0]
    kv_rank = value_up_weight.shape[1]
    everyone = jnp.arange(req_total, dtype=jnp.int32)
    new_group = new_slot // group_req
    pair_rank = new_slot % group_req - everyone // group_req * per_pair
    my_targets = lax.dynamic_slice_in_dim(
        new_group * per_pair + pair_rank, my_group * group_req, group_req
    )
    target_places = jnp.arange(group_req, dtype=jnp.int32)
    picked = jnp.sum(
        jnp.where(my_targets[None, :] == target_places[:, None], target_places[None, :], 0), axis=1
    )
    arrived = move(picked, old_cache, dp_count, tp_count)
    source = jnp.sum(
        jnp.where(new_slot[None, :] == everyone[:, None], everyone[None, :], 0), axis=1
    )
    my_slots = (my_group * tp_count + my_column) * req_dev + jnp.arange(req_dev, dtype=jnp.int32)
    my_lengths = jnp.take(lengths, jnp.take(source, my_slots))
    new_cache, latents = attend(my_lengths, arrived, queries, new_latent, tp_count, kv_rank)
    gain = norm_gain.astype(jnp.float32)[None, :]
    layer_out = dense(latents, value_up_weight, hidden, gain, w_out, w_gate, w_up, w_down)
    return (new_cache, layer_out)


def solution(mesh):
    in_specs = (
        P("dp", "tp", None),
        P(),
        P(),
        P(None, ("dp", "tp"), None, None),
        P(None, ("dp", "tp"), None),
        P(None, None, "dp"),
        P("tp", None, None),
        P("tp", "dp"),
        P("dp"),
        P("dp", "tp"),
        P("dp", "tp"),
        P("tp", "dp"),
    )
    out_specs = (P(("dp", "tp"), None, None), P(None, None, "dp"))
    return jax.shard_map(shards, mesh=mesh, in_specs=in_specs, out_specs=out_specs, check_vma=False)
```

```python
import functools

import jax
import jax.numpy as jnp
from jax import lax
from jax.experimental import pallas as pl
from jax.experimental.pallas import tpu as pltpu
from jax.sharding import PartitionSpec as P

D = 7168


MESH = pl.DeviceIdType.MESH


def loop(low, high, action):
    def body(i, carry):
        action(i)
        return carry

    lax.fori_loop(low, high, body, 0)


def move_kernel(
    n_dp, n_tp, chunks, ahead, picked, cache, out, loaded, stage, mid, load_sem, own_sem, send1, recv1, send2, recv2
):
    group_req, piece, width = loaded.shape
    rows = piece // chunks
    rank = (stage.shape[2] - 128) // 2
    pairs = n_tp // n_dp
    g = lax.axis_index("dp")
    c = lax.axis_index("tp")

    load = pltpu.make_async_copy(cache, loaded, load_sem)
    load.start()
    barrier = pltpu.get_barrier_semaphore()

    def greet_dp(i):
        pl.semaphore_signal(barrier, 1, device_id=(lax.rem(g + i, n_dp), c), device_id_type=MESH)

    def greet_tp(i):
        pl.semaphore_signal(barrier, 1, device_id=(g, lax.rem(c + i, n_tp)), device_id_type=MESH)

    loop(1, n_dp, greet_dp)
    loop(1, n_tp, greet_tp)
    pl.semaphore_wait(barrier, n_dp + n_tp - 2)
    load.wait()

    def sort(q):
        part = pl.ds(q * rows, rows)

        def one(i):
            first = picked[2 * i]
            second = picked[2 * i + 1]
            stage[i, part, 0:rank] = loaded[first, part, 0:rank]
            stage[i, part, rank : 2 * rank] = loaded[second, part, 0:rank]
            tails = [loaded[first, part, rank:width], loaded[second, part, rank:width]]
            stage[i, part, 2 * rank :] = jnp.concatenate(tails, axis=1)

        loop(0, n_tp, one)
        for n in range(pairs):
            mid[pairs * g + n, part] = stage[pairs * g + n, part]

    def over_dp(q, i, from_group):
        to_group = lax.rem(g + i, n_dp)
        part = pl.ds(q * rows, rows)
        return pltpu.make_async_remote_copy(
            src_ref=stage.at[pl.ds(pairs * to_group, pairs), part],
            dst_ref=mid.at[pl.ds(pairs * from_group, pairs), part],
            send_sem=send1.at[q, to_group],
            recv_sem=recv1.at[q, from_group],
            device_id=(to_group, c),
            device_id_type=MESH,
        )

    def over_tp(q, i, from_column):
        to_column = lax.rem(c + i, n_tp)
        return pltpu.make_async_remote_copy(
            src_ref=mid.at[to_column, pl.ds(q * rows, rows)],
            dst_ref=out.at[pl.ds(from_column * piece + q * rows, rows)],
            send_sem=send2.at[q, to_column],
            recv_sem=recv2.at[q, from_column],
            device_id=(g, to_column),
            device_id_type=MESH,
        )

    def own(q):
        return pltpu.make_async_copy(
            mid.at[c, pl.ds(q * rows, rows)], out.at[pl.ds(c * piece + q * rows, rows)], own_sem.at[q]
        )

    for q in range(chunks + 1):
        if q < chunks:
            sort(q)
            if q >= ahead:
                loop(1, n_dp, lambda i: over_dp(q - ahead, i, g).wait_send())
            loop(1, n_dp, lambda i: over_dp(q, i, g).start())
        if q >= 1:
            loop(1, n_dp, lambda i: over_dp(q - 1, i, lax.rem(g + n_dp - i, n_dp)).wait_recv())
            loop(1, n_tp, lambda i: over_tp(q - 1, i, c).start())
            own(q - 1).start()
    for q in range(chunks):
        if q >= chunks - ahead:
            loop(1, n_dp, lambda i: over_dp(q, i, g).wait_send())
        loop(1, n_tp, lambda i: over_tp(q, i, c).wait_send())
        loop(1, n_tp, lambda i: over_tp(q, i, lax.rem(c + n_tp - i, n_tp)).wait_recv())
        own(q).wait()


def move(picked, old_cache, n_dp, n_tp, chunks=12, ahead=2):
    group_req, piece, width = old_cache.shape
    packed = (n_tp, piece, 2 * width)
    sems = pltpu.SemaphoreType.DMA
    return pl.pallas_call(
        functools.partial(move_kernel, n_dp, n_tp, chunks, ahead),
        out_shape=jax.ShapeDtypeStruct((piece * n_tp, 2 * width), old_cache.dtype),
        in_specs=[pl.BlockSpec(memory_space=pltpu.SMEM), pl.BlockSpec(memory_space=pl.ANY)],
        out_specs=pl.BlockSpec(memory_space=pl.ANY),
        scratch_shapes=[
            pltpu.VMEM(old_cache.shape, old_cache.dtype),
            pltpu.VMEM(packed, old_cache.dtype),
            pltpu.VMEM(packed, old_cache.dtype),
            sems,
            sems((chunks,)),
            sems((chunks, n_dp)),
            sems((chunks, n_dp)),
            sems((chunks, n_tp)),
            sems((chunks, n_tp)),
        ],
        compiler_params=pltpu.CompilerParams(collective_id=0, has_side_effects=True, vmem_limit_bytes=48 * 2**20),
    )(picked, old_cache)


score_scale = 0.07216878364870323
norm_eps = 1e-06


def attend_kernel(lens, main, tail, queries, new_main, new_tail, cache_out, lat, scores, query):
    f32, bf16 = jnp.float32, jnp.bfloat16
    item = pl.program_id(0)
    length = lens[item]
    context, rank = main.shape
    heads = queries.shape[3]
    both = 2 * heads
    query[:rank] = jnp.concatenate([queries[0, 0, :rank], queries[1, 0, :rank]], axis=1)
    query[rank:] = jnp.zeros((128, both), bf16)
    half = pl.multiple_of(rank + item * 64, 64)
    query[pl.ds(half, 64)] = jnp.concatenate([queries[0, 0, rank:], queries[1, 0, rank:]], axis=1)
    block = context // 2
    row = lax.broadcasted_iota(jnp.int32, (block, rank), 0)
    tail_row = lax.broadcasted_iota(jnp.int32, (block, 128), 0)
    tail_length = jnp.where(lax.broadcasted_iota(jnp.int32, (block, 128), 1) < 64, lens[0], lens[1])
    place = lax.broadcasted_iota(jnp.int32, (block, both), 0)
    last = length + lax.broadcasted_iota(jnp.int32, (block, both), 1) // heads

    def fill(old, position, size, first, second):
        new = jnp.where(position == size, first.astype(f32), jnp.where(position == size + 1, second.astype(f32), 0.0))
        return jnp.where(position < size, old.astype(f32), new).astype(bf16)

    def score(i, top):
        start = pl.multiple_of(i * block, block)
        rows = pl.ds(start, block)
        keys = fill(main[rows], row + start, length, new_main[0, item], new_main[1, item])
        tails = fill(tail[rows], tail_row + start, tail_length, new_tail[0], new_tail[1])
        cache_out[0, :rank, rows] = keys.T
        tails_t = tails.T

        @pl.when(item == 0)
        def _():
            cache_out[0, rank:, rows] = tails_t[:64]

        @pl.when(item == 1)
        def _():
            cache_out[0, rank:, rows] = tails_t[64:]

        both_parts = jnp.concatenate([keys, tails], axis=1)
        raw = jnp.dot(both_parts, query[...], preferred_element_type=f32)
        raw = jnp.where(place + start <= last, raw * score_scale, -jnp.inf)
        scores[rows] = raw
        return jnp.maximum(top, jnp.max(raw, axis=0, keepdims=True))

    top = lax.fori_loop(0, context // block, score, jnp.full((1, both), -jnp.inf, f32))
    exponent = jnp.exp(scores[...] - top)
    total = jnp.sum(exponent, axis=0, keepdims=True)
    mixed_t = jnp.dot(cache_out[0, :rank], exponent.astype(bf16), preferred_element_type=f32)
    mixed = (mixed_t / total).T
    mixed = mixed.reshape(2, lat.shape[0], -1, rank)
    mixed = jnp.concatenate([mixed[0], mixed[1]], axis=1).astype(bf16)
    lat[:, pl.ds(pl.multiple_of(item * 16, 16), 16)] = mixed


def attend(my_lengths, arrived, queries, new_latent, n_tp, kv_rank):
    context = arrived.shape[0]
    steps, items, heads, width = queries.shape
    bf16 = jnp.bfloat16
    new_tail = new_latent[:, :, kv_rank:].reshape(steps, 1, -1)
    flipped, latents = pl.pallas_call(
        attend_kernel,
        grid=(items,),
        out_shape=(
            jax.ShapeDtypeStruct((items, width, context), bf16),
            jax.ShapeDtypeStruct((n_tp, items * steps * heads // n_tp, kv_rank), bf16),
        ),
        in_specs=[
            pl.BlockSpec(memory_space=pltpu.SMEM),
            pl.BlockSpec((context, kv_rank), lambda i: (0, i)),
            pl.BlockSpec((context, 128), lambda i: (0, 2 * kv_rank // 128)),
            pl.BlockSpec((steps, 1, width, heads), lambda i: (0, i, 0, 0)),
            pl.BlockSpec((steps, items, 1, kv_rank), lambda i: (0, 0, 0, 0)),
            pl.BlockSpec((steps, 1, 128), lambda i: (0, 0, 0)),
        ],
        out_specs=(
            pl.BlockSpec((1, width, context), lambda i: (i, 0, 0)),
            pl.BlockSpec((n_tp, items * steps * heads // n_tp, kv_rank), lambda i: (0, 0, 0)),
        ),
        scratch_shapes=[
            pltpu.VMEM((context, steps * heads), jnp.float32),
            pltpu.VMEM((kv_rank + 128, steps * heads), bf16),
        ],
        compiler_params=pltpu.CompilerParams(vmem_limit_bytes=58 * 2**20),
    )(my_lengths, arrived, arrived, queries.transpose(0, 1, 3, 2), new_latent[:, :, None, :kv_rank], new_tail)
    return flipped.transpose(0, 2, 1), latents


def dense_kernel(
    lat,
    value_up,
    hidden,
    gain,
    w_out,
    w_gate,
    w_up,
    w_down,
    out,
    vup_v,
    wout_v,
    wgate_v,
    wup_v,
    wdown_v,
    latr,
    perm,
    xbuf,
    s3,
    r3,
    after,
    ybuf,
    gu,
    pair_s,
    pair_r,
    ring_s,
    ring_r,
    hbuf,
    wsem,
    lat_ss,
    lat_rs,
    x_ss,
    x_rs,
    s3_ss,
    s3_rs,
    y_ss,
    y_rs,
    pair_ss,
    pair_rs,
    ring_ss,
    ring_rs,
    h_ss,
    h_rs,
    s7_ss,
    s7_rs,
    o_ss,
    o_rs,
):
    f32, bf16 = jnp.float32, jnp.bfloat16
    g = lax.axis_index("dp")
    c = lax.axis_index("tp")
    y, k = g // 2, lax.rem(g, 2)
    z, x = c // 4, lax.rem(c, 4)
    sib = g + 1 - 2 * k
    ff = wgate_v.shape[1]
    width = 2 * ff

    def block_of(column):
        down = column // 4
        return 4 * lax.rem(lax.rem(column, 4) - down + 4, 4) + down

    mine = block_of(c)

    loads = []
    for n, (src, dst) in enumerate(
        ((value_up, vup_v), (w_out, wout_v), (w_gate, wgate_v), (w_up, wup_v), (w_down, wdown_v))
    ):
        loads.append(pltpu.make_async_copy(src, dst, wsem.at[n]))
        loads[-1].start()

    def remote(src, dst, send_sem, recv_sem, dp, tp):
        return pltpu.make_async_remote_copy(
            src_ref=src, dst_ref=dst, send_sem=send_sem, recv_sem=recv_sem, device_id=(dp, tp), device_id_type=MESH
        )

    barrier = pltpu.get_barrier_semaphore()
    loop(1, 16, lambda i: pl.semaphore_signal(barrier, 1, device_id=(g, lax.rem(c + i, 16)), device_id_type=MESH))
    loop(1, 4, lambda i: pl.semaphore_signal(barrier, 1, device_id=(lax.rem(g + 2 * i, 8), c), device_id_type=MESH))
    pl.semaphore_signal(barrier, 1, device_id=(sib, c), device_id_type=MESH)
    pl.semaphore_wait(barrier, 19)

    def lat_copy(i, source):
        to = lax.rem(c + i, 16)
        return remote(lat.at[to], latr.at[source], lat_ss.at[to], lat_rs.at[source], g, to)

    loop(1, 16, lambda i: lat_copy(i, c).start())
    latr[c] = lat[c]
    row = lax.broadcasted_iota(jnp.int32, (512, 512), 0)
    col = lax.broadcasted_iota(jnp.int32, (512, 512), 1)
    wanted = ((row & 31) >> 1) * 32 + (row & 1) * 16 + ((row >> 5) & 1) * 8 + (row >> 6)
    perm[...] = jnp.where(col == wanted, 1.0, 0.0).astype(bf16)
    loop(1, 16, lambda i: lat_copy(i, lax.rem(c + 16 - i, 16)).wait_recv())
    ordered = jnp.dot(perm[...], latr[...].reshape(512, 512), preferred_element_type=f32).astype(bf16)
    loads[0].wait()
    for head in range(8):
        part = jnp.dot(ordered[64 * head : 64 * head + 64], vup_v[head], preferred_element_type=f32)
        xbuf[0, g, :, 128 * head : 128 * head + 128] = part[:32].astype(bf16)
        xbuf[1, g, :, 128 * head : 128 * head + 128] = part[32:].astype(bf16)

    def gather_ring(buf, ss, rs, s, i, source):
        to = lax.rem(g + 2 * i, 8)
        return remote(buf.at[s, g], buf.at[s, source], ss.at[s, i], rs.at[s, source], to, c)

    def gather_pair(buf, ss, rs, s, i, sent, got):
        return remote(buf.at[s, sent], buf.at[s, got], ss.at[s, 4 + i], rs.at[s, got], sib, c)

    def gather_start(buf, ss, rs, s):
        loop(1, 4, lambda i: gather_ring(buf, ss, rs, s, i, g).start())
        gather_pair(buf, ss, rs, s, 0, g, g).start()

    def gather_rest(buf, ss, rs, s):
        def forward(i):
            src = lax.rem(g + 8 - 2 * i, 8)
            gather_ring(buf, ss, rs, s, i, src).wait_recv()
            gather_pair(buf, ss, rs, s, i, src, src).start()

        loop(1, 4, forward)
        loop(0, 4, lambda i: gather_pair(buf, ss, rs, s, i, g, lax.rem(sib + 8 - 2 * i, 8)).wait_recv())

    def gather_end(buf, ss, rs, s):
        loop(1, 4, lambda i: gather_ring(buf, ss, rs, s, i, g).wait_send())
        loop(0, 4, lambda i: gather_pair(buf, ss, rs, s, i, g, g).wait_send())

    def scatter_copy(ss, rs, s, i, source):
        to = lax.rem(c + i, 16)
        return remote(s3.at[s, block_of(to)], r3.at[s, source], ss.at[s, to], rs.at[s, source], g, to)

    def scatter(value, ss, rs, s):
        s3[s] = value.reshape(16, 16, value.shape[1]).astype(bf16)
        loop(1, 16, lambda i: scatter_copy(ss, rs, s, i, c).start())

    def scatter_sum(ss, rs, s, first):
        r3[s, c] = s3[s, mine]
        loop(1, 16, lambda i: scatter_copy(ss, rs, s, i, lax.rem(c + 16 - i, 16)).wait_recv())
        total = first + jnp.sum(r3[s].astype(f32), axis=0)
        loop(1, 16, lambda i: scatter_copy(ss, rs, s, i, c).wait_send())
        return total

    def spread(buf, ss, rs, s, i, source):
        to = lax.rem(c + i, 16)
        return remote(buf.at[s, mine], buf.at[s, block_of(source)], ss.at[s, to], rs.at[s, source], g, to)

    def spread_start(buf, ss, rs, s):
        loop(1, 16, lambda i: spread(buf, ss, rs, s, i, c).start())

    def spread_wait(buf, ss, rs, s):
        loop(1, 16, lambda i: spread(buf, ss, rs, s, i, lax.rem(c + 16 - i, 16)).wait_recv())

    def spread_end(buf, ss, rs, s):
        loop(1, 16, lambda i: spread(buf, ss, rs, s, i, c).wait_send())

    loop(0, 2, lambda s: gather_start(xbuf, x_ss, x_rs, s))
    loads[1].wait()

    def out_stage(s):
        gather_rest(xbuf, x_ss, x_rs, s)
        rows = xbuf[s].reshape(256, xbuf.shape[3])
        scatter(jnp.dot(rows, wout_v[...], preferred_element_type=f32), s3_ss, s3_rs, s)

    loop(0, 2, out_stage)

    def after_stage(s):
        after[s] = scatter_sum(s3_ss, s3_rs, s, hidden[s, mine].astype(f32))
        ybuf[s, mine] = after[s].astype(bf16)
        spread_start(ybuf, y_ss, y_rs, s)

    loop(0, 2, after_stage)
    loads[2].wait()
    loads[3].wait()
    lane = lax.broadcasted_iota(jnp.int32, (32, 128), 1)

    def two_part(total):
        high = total.astype(bf16)
        low = (total - high.astype(f32)).astype(bf16)
        return jnp.where(lane < 64, high.astype(f32), low.astype(f32)).astype(bf16)

    def one_part(pair):
        return pair[:, 0:1].astype(f32) + pair[:, 64:65].astype(f32)

    def pair_copy(s, chunk):
        return remote(pair_s.at[s, chunk], pair_r.at[s, chunk], pair_ss.at[s, chunk], pair_rs.at[s, chunk], sib, c)

    def ring_copy(s, chunk, source):
        return remote(
            ring_s.at[s, chunk], ring_r.at[s, source], ring_ss.at[s, chunk], ring_rs.at[s, source], 2 * chunk + k, c
        )

    def gate_stage(s):
        spread_wait(ybuf, y_ss, y_rs, s)
        rows = ybuf[s].reshape(256, ybuf.shape[3]).astype(f32)
        squares = jnp.sum(rows * rows, axis=1, keepdims=True)
        scaled = (rows * gain[...]).astype(bf16)
        gu[s, :, :, :, width : width + 128] = jnp.broadcast_to(squares, (256, 128)).reshape(4, 2, 32, 128)
        gu[s, :, :, :, 0:ff] = jnp.dot(scaled, wgate_v[...], preferred_element_type=f32).reshape(4, 2, 32, ff)
        gu[s, :, :, :, ff:width] = jnp.dot(scaled, wup_v[...], preferred_element_type=f32).reshape(4, 2, 32, ff)

        def give(i):
            chunk = lax.rem(y + 1 + i, 4)
            pair_s[s, chunk, :, 0:width] = gu[s, chunk, 1 - k, :, 0:width].astype(bf16)
            pair_s[s, chunk, :, width : width + 128] = two_part(gu[s, chunk, 1 - k, :, width : width + 128])
            pair_copy(s, chunk).start()

        loop(0, 4, give)

        def merge(i):
            chunk = lax.rem(y + 1 + i, 4)
            pair_copy(s, chunk).wait_recv()
            total = gu[s, chunk, k, :, 0:width] + pair_r[s, chunk, :, 0:width].astype(f32)
            squares = gu[s, chunk, k, :, width : width + 128] + one_part(pair_r[s, chunk, :, width : width + 128])
            gu[s, chunk, k, :, 0:width] = total
            gu[s, chunk, k, :, width : width + 128] = squares

            @pl.when(chunk != y)
            def _():
                ring_s[s, chunk, :, 0:width] = total.astype(bf16)
                ring_s[s, chunk, :, width : width + 128] = two_part(squares)
                ring_copy(s, chunk, y).start()

        loop(0, 4, merge)

    loop(0, 2, gate_stage)

    def act_stage(s):
        def ring_add(i):
            source = lax.rem(y + i, 4)
            ring_copy(s, source, source).wait_recv()
            gu[s, y, k, :, 0:width] += ring_r[s, source, :, 0:width].astype(f32)
            gu[s, y, k, :, width : width + 128] += one_part(ring_r[s, source, :, width : width + 128])

        loop(1, 4, ring_add)
        scale = 1.0 / jnp.sqrt(gu[s, y, k, :, width : width + 1] / D + norm_eps)
        gate = gu[s, y, k, :, 0:ff] * scale
        up = gu[s, y, k, :, ff:width] * scale
        hbuf[s, g] = (jax.nn.silu(gate) * up).astype(bf16)
        gather_start(hbuf, h_ss, h_rs, s)

    loop(0, 2, act_stage)
    loads[4].wait()

    def down_stage(s):
        gather_rest(hbuf, h_ss, h_rs, s)
        rows = hbuf[s].reshape(256, ff)
        scatter(jnp.dot(rows, wdown_v[...], preferred_element_type=f32), s7_ss, s7_rs, s)

    loop(0, 2, down_stage)

    def result_stage(s):
        out[s, mine] = scatter_sum(s7_ss, s7_rs, s, after[s]).astype(bf16)
        spread_start(out, o_ss, o_rs, s)

    loop(0, 2, result_stage)
    loop(1, 16, lambda i: lat_copy(i, c).wait_send())

    def end_stage(s):
        gather_end(xbuf, x_ss, x_rs, s)
        spread_end(ybuf, y_ss, y_rs, s)
        loop(0, 4, lambda i: pair_copy(s, i).wait_send())
        loop(1, 4, lambda i: ring_copy(s, lax.rem(y + i, 4), y).wait_send())
        gather_end(hbuf, h_ss, h_rs, s)
        spread_end(out, o_ss, o_rs, s)
        spread_wait(out, o_ss, o_rs, s)

    loop(0, 2, end_stage)


def dense(lat, value_up, hidden, gain, w_out, w_gate, w_up, w_down):
    steps, total, cols = hidden.shape
    ff = w_gate.shape[1]
    bf16, f32 = jnp.bfloat16, jnp.float32
    vmem, sems = pltpu.VMEM, pltpu.SemaphoreType.DMA
    in_vmem, anywhere = pl.BlockSpec(memory_space=pltpu.VMEM), pl.BlockSpec(memory_space=pl.ANY)
    result = pl.pallas_call(
        dense_kernel,
        out_shape=jax.ShapeDtypeStruct((steps, 16, 16, cols), bf16),
        in_specs=[in_vmem, anywhere, in_vmem, in_vmem, anywhere, anywhere, anywhere, anywhere],
        out_specs=in_vmem,
        scratch_shapes=[
            vmem(value_up.shape, bf16),
            vmem(w_out.shape, bf16),
            vmem(w_gate.shape, bf16),
            vmem(w_up.shape, bf16),
            vmem(w_down.shape, bf16),
            vmem(lat.shape, bf16),
            vmem((512, 512), bf16),
            vmem((2, 8, 32, w_out.shape[0]), bf16),
            vmem((2, 16, 16, cols), bf16),
            vmem((2, 16, 16, cols), bf16),
            vmem((2, 16, cols), f32),
            vmem((2, 16, 16, cols), bf16),
            vmem((2, 4, 2, 32, 2 * ff + 128), f32),
            vmem((2, 4, 32, 2 * ff + 128), bf16),
            vmem((2, 4, 32, 2 * ff + 128), bf16),
            vmem((2, 4, 32, 2 * ff + 128), bf16),
            vmem((2, 4, 32, 2 * ff + 128), bf16),
            vmem((2, 8, 32, ff), bf16),
            sems((5,)),
            sems((16,)),
            sems((16,)),
            sems((2, 8)),
            sems((2, 8)),
            sems((2, 16)),
            sems((2, 16)),
            sems((2, 16)),
            sems((2, 16)),
            sems((2, 4)),
            sems((2, 4)),
            sems((2, 4)),
            sems((2, 4)),
            sems((2, 8)),
            sems((2, 8)),
            sems((2, 16)),
            sems((2, 16)),
            sems((2, 16)),
            sems((2, 16)),
        ],
        compiler_params=pltpu.CompilerParams(collective_id=1, has_side_effects=True, vmem_limit_bytes=52 * 2**20),
    )(lat, value_up, hidden.reshape(steps, 16, 16, cols), gain, w_out, w_gate, w_up, w_down)
    return result.reshape(steps, total, cols)


def shards(
    old_cache,
    lengths,
    new_slot,
    queries,
    new_latent,
    hidden,
    value_up_weight,
    w_out,
    norm_gain,
    w_gate,
    w_up,
    w_down,
):
    dp_count = lax.axis_size("dp")
    tp_count = lax.axis_size("tp")
    my_group = lax.axis_index("dp")
    my_column = lax.axis_index("tp")
    group_req = old_cache.shape[0]
    per_pair = group_req // dp_count
    req_dev = queries.shape[1]
    req_total = new_slot.shape[0]
    kv_rank = value_up_weight.shape[1]
    everyone = jnp.arange(req_total, dtype=jnp.int32)
    order = jnp.arange(group_req, dtype=jnp.int32)
    out_slots = order // per_pair * group_req + my_group * per_pair + order % per_pair
    picked = jnp.sum(
        jnp.where(new_slot[None, :] == out_slots[:, None], everyone[None, :] % group_req, 0), axis=1
    )
    arrived = move(picked, old_cache, dp_count, tp_count)
    my_slots = (my_group * tp_count + my_column) * req_dev + jnp.arange(req_dev, dtype=jnp.int32)
    my_lengths = jnp.sum(jnp.where(new_slot[None, :] == my_slots[:, None], lengths[None, :], 0), axis=1)
    new_cache, latents = attend(my_lengths, arrived, queries, new_latent, tp_count, kv_rank)
    gain = norm_gain.astype(jnp.float32)[None, :]
    layer_out = dense(latents, value_up_weight, hidden, gain, w_out, w_gate, w_up, w_down)
    return (new_cache, layer_out)


def solution(mesh):
    in_specs = (
        P("dp", "tp", None),
        P(),
        P(),
        P(None, ("dp", "tp"), None, None),
        P(None, ("dp", "tp"), None),
        P(None, None, "dp"),
        P("tp", None, None),
        P("tp", "dp"),
        P("dp"),
        P("dp", "tp"),
        P("dp", "tp"),
        P("tp", "dp"),
    )
    out_specs = (P(("dp", "tp"), None, None), P(None, None, "dp"))
    return jax.shard_map(shards, mesh=mesh, in_specs=in_specs, out_specs=out_specs, check_vma=False)
```

```python
import functools

import jax
import jax.numpy as jnp
from jax import lax
from jax.experimental import pallas as pl
from jax.experimental.pallas import tpu as pltpu
from jax.sharding import PartitionSpec as P

D = 7168


MESH = pl.DeviceIdType.MESH


def loop(low, high, action):
    def body(i, carry):
        action(i)
        return carry

    lax.fori_loop(low, high, body, 0)


def move_kernel(
    n_dp, n_tp, chunks, ahead, picked, cache, out, loaded, stage, mid, load_sem, own_sem, send1, recv1, send2, recv2
):
    group_req, piece, width = loaded.shape
    rows = piece // chunks
    rank = (stage.shape[2] - 128) // 2
    pairs = n_tp // n_dp
    g = lax.axis_index("dp")
    c = lax.axis_index("tp")

    load = pltpu.make_async_copy(cache, loaded, load_sem)
    load.start()
    barrier = pltpu.get_barrier_semaphore()

    def greet_dp(i):
        pl.semaphore_signal(barrier, 1, device_id=(lax.rem(g + i, n_dp), c), device_id_type=MESH)

    def greet_tp(i):
        pl.semaphore_signal(barrier, 1, device_id=(g, lax.rem(c + i, n_tp)), device_id_type=MESH)

    loop(1, n_dp, greet_dp)
    loop(1, n_tp, greet_tp)
    pl.semaphore_wait(barrier, n_dp + n_tp - 2)
    load.wait()

    def sort(q):
        part = pl.ds(q * rows, rows)

        def one(i):
            first = picked[2 * i]
            second = picked[2 * i + 1]
            stage[i, part, 0:rank] = loaded[first, part, 0:rank]
            stage[i, part, rank : 2 * rank] = loaded[second, part, 0:rank]
            tails = [loaded[first, part, rank:width], loaded[second, part, rank:width]]
            stage[i, part, 2 * rank :] = jnp.concatenate(tails, axis=1)

        loop(0, n_tp, one)
        for n in range(pairs):
            mid[pairs * g + n, part] = stage[pairs * g + n, part]

    def over_dp(q, i, from_group):
        to_group = lax.rem(g + i, n_dp)
        part = pl.ds(q * rows, rows)
        return pltpu.make_async_remote_copy(
            src_ref=stage.at[pl.ds(pairs * to_group, pairs), part],
            dst_ref=mid.at[pl.ds(pairs * from_group, pairs), part],
            send_sem=send1.at[q, to_group],
            recv_sem=recv1.at[q, from_group],
            device_id=(to_group, c),
            device_id_type=MESH,
        )

    def over_tp(q, i, from_column):
        to_column = lax.rem(c + i, n_tp)
        return pltpu.make_async_remote_copy(
            src_ref=mid.at[to_column, pl.ds(q * rows, rows)],
            dst_ref=out.at[pl.ds(from_column * piece + q * rows, rows)],
            send_sem=send2.at[q, to_column],
            recv_sem=recv2.at[q, from_column],
            device_id=(g, to_column),
            device_id_type=MESH,
        )

    def own(q):
        return pltpu.make_async_copy(
            mid.at[c, pl.ds(q * rows, rows)], out.at[pl.ds(c * piece + q * rows, rows)], own_sem.at[q]
        )

    for q in range(chunks + 1):
        if q < chunks:
            sort(q)
            if q >= ahead:
                loop(1, n_dp, lambda i: over_dp(q - ahead, i, g).wait_send())
            loop(1, n_dp, lambda i: over_dp(q, i, g).start())
        if q >= 1:
            loop(1, n_dp, lambda i: over_dp(q - 1, i, lax.rem(g + n_dp - i, n_dp)).wait_recv())
            loop(1, n_tp, lambda i: over_tp(q - 1, i, c).start())
            own(q - 1).start()
    for q in range(chunks):
        if q >= chunks - ahead:
            loop(1, n_dp, lambda i: over_dp(q, i, g).wait_send())
        loop(1, n_tp, lambda i: over_tp(q, i, c).wait_send())
        loop(1, n_tp, lambda i: over_tp(q, i, lax.rem(c + n_tp - i, n_tp)).wait_recv())
        own(q).wait()


def move(picked, old_cache, n_dp, n_tp, chunks=12, ahead=2):
    group_req, piece, width = old_cache.shape
    packed = (n_tp, piece, 2 * width)
    sems = pltpu.SemaphoreType.DMA
    return pl.pallas_call(
        functools.partial(move_kernel, n_dp, n_tp, chunks, ahead),
        out_shape=jax.ShapeDtypeStruct((piece * n_tp, 2 * width), old_cache.dtype),
        in_specs=[pl.BlockSpec(memory_space=pltpu.SMEM), pl.BlockSpec(memory_space=pl.ANY)],
        out_specs=pl.BlockSpec(memory_space=pl.ANY),
        scratch_shapes=[
            pltpu.VMEM(old_cache.shape, old_cache.dtype),
            pltpu.VMEM(packed, old_cache.dtype),
            pltpu.VMEM(packed, old_cache.dtype),
            sems,
            sems((chunks,)),
            sems((chunks, n_dp)),
            sems((chunks, n_dp)),
            sems((chunks, n_tp)),
            sems((chunks, n_tp)),
        ],
        compiler_params=pltpu.CompilerParams(collective_id=0, has_side_effects=True, vmem_limit_bytes=48 * 2**20),
    )(picked, old_cache)


score_scale = 0.07216878364870323
norm_eps = 1e-06


def attend_kernel(lens, main, tail, queries, new_main, new_tail, cache_out, lat, scores, query):
    f32, bf16 = jnp.float32, jnp.bfloat16
    item = pl.program_id(0)
    length = lens[item]
    context, rank = main.shape
    heads = queries.shape[3]
    both = 2 * heads
    query[:rank] = jnp.concatenate([queries[0, 0, :rank], queries[1, 0, :rank]], axis=1)
    query[rank:] = jnp.zeros((128, both), bf16)
    half = pl.multiple_of(rank + item * 64, 64)
    query[pl.ds(half, 64)] = jnp.concatenate([queries[0, 0, rank:], queries[1, 0, rank:]], axis=1)
    block = context // 2
    row = lax.broadcasted_iota(jnp.int32, (block, rank), 0)
    tail_row = lax.broadcasted_iota(jnp.int32, (block, 128), 0)
    tail_length = jnp.where(lax.broadcasted_iota(jnp.int32, (block, 128), 1) < 64, lens[0], lens[1])
    place = lax.broadcasted_iota(jnp.int32, (block, both), 0)
    last = length + lax.broadcasted_iota(jnp.int32, (block, both), 1) // heads

    def fill(old, position, size, first, second):
        new = jnp.where(position == size, first.astype(f32), jnp.where(position == size + 1, second.astype(f32), 0.0))
        return jnp.where(position < size, old.astype(f32), new).astype(bf16)

    def score(i, top):
        start = pl.multiple_of(i * block, block)
        rows = pl.ds(start, block)
        keys = fill(main[rows], row + start, length, new_main[0, item], new_main[1, item])
        tails = fill(tail[rows], tail_row + start, tail_length, new_tail[0], new_tail[1])
        cache_out[0, :rank, rows] = keys.T
        tails_t = tails.T

        @pl.when(item == 0)
        def _():
            cache_out[0, rank:, rows] = tails_t[:64]

        @pl.when(item == 1)
        def _():
            cache_out[0, rank:, rows] = tails_t[64:]

        both_parts = jnp.concatenate([keys, tails], axis=1)
        raw = jnp.dot(both_parts, query[...], preferred_element_type=f32)
        raw = jnp.where(place + start <= last, raw * score_scale, -jnp.inf)
        scores[rows] = raw
        return jnp.maximum(top, jnp.max(raw, axis=0, keepdims=True))

    top = lax.fori_loop(0, context // block, score, jnp.full((1, both), -jnp.inf, f32))
    exponent = jnp.exp(scores[...] - top)
    total = jnp.sum(exponent, axis=0, keepdims=True)
    mixed_t = jnp.dot(cache_out[0, :rank], exponent.astype(bf16), preferred_element_type=f32)
    mixed = (mixed_t / total).T
    mixed = mixed.reshape(2, lat.shape[0], -1, rank)
    mixed = jnp.concatenate([mixed[0], mixed[1]], axis=1).astype(bf16)
    lat[:, pl.ds(pl.multiple_of(item * 16, 16), 16)] = mixed


def attend(my_lengths, arrived, queries, new_latent, n_tp, kv_rank):
    context = arrived.shape[0]
    steps, items, heads, width = queries.shape
    bf16 = jnp.bfloat16
    new_tail = new_latent[:, :, kv_rank:].reshape(steps, 1, -1)
    flipped, latents = pl.pallas_call(
        attend_kernel,
        grid=(items,),
        out_shape=(
            jax.ShapeDtypeStruct((items, width, context), bf16),
            jax.ShapeDtypeStruct((n_tp, items * steps * heads // n_tp, kv_rank), bf16),
        ),
        in_specs=[
            pl.BlockSpec(memory_space=pltpu.SMEM),
            pl.BlockSpec((context, kv_rank), lambda i: (0, i)),
            pl.BlockSpec((context, 128), lambda i: (0, 2 * kv_rank // 128)),
            pl.BlockSpec((steps, 1, width, heads), lambda i: (0, i, 0, 0)),
            pl.BlockSpec((steps, items, 1, kv_rank), lambda i: (0, 0, 0, 0)),
            pl.BlockSpec((steps, 1, 128), lambda i: (0, 0, 0)),
        ],
        out_specs=(
            pl.BlockSpec((1, width, context), lambda i: (i, 0, 0)),
            pl.BlockSpec((n_tp, items * steps * heads // n_tp, kv_rank), lambda i: (0, 0, 0)),
        ),
        scratch_shapes=[
            pltpu.VMEM((context, steps * heads), jnp.float32),
            pltpu.VMEM((kv_rank + 128, steps * heads), bf16),
        ],
        compiler_params=pltpu.CompilerParams(vmem_limit_bytes=40 * 2**20),
    )(my_lengths, arrived, arrived, queries.transpose(0, 1, 3, 2), new_latent[:, :, None, :kv_rank], new_tail)
    return flipped.transpose(0, 2, 1), latents


def dense_kernel(
    lat,
    value_up,
    hidden,
    gain,
    w_out,
    w_gate,
    w_up,
    w_down,
    out,
    vup_v,
    wout_v,
    wgate_v,
    wup_v,
    wdown_v,
    latr,
    perm,
    xbuf,
    s3,
    r3,
    t3,
    after,
    ybuf,
    gu,
    pair_s,
    pair_r,
    ring_s,
    ring_r,
    hbuf,
    wsem,
    lat_ss,
    lat_rs,
    x_ss,
    x_rs,
    s3_ss,
    s3_rs,
    y_ss,
    y_rs,
    pair_ss,
    pair_rs,
    ring_ss,
    ring_rs,
    h_ss,
    h_rs,
    s7_ss,
    s7_rs,
    o_ss,
    o_rs,
):
    f32, bf16 = jnp.float32, jnp.bfloat16
    g = lax.axis_index("dp")
    c = lax.axis_index("tp")
    y, k = g // 2, lax.rem(g, 2)
    z, x = c // 4, lax.rem(c, 4)
    sib = g + 1 - 2 * k
    ff = wgate_v.shape[1]
    width = 2 * ff

    def block_of(column):
        down = column // 4
        return 4 * lax.rem(lax.rem(column, 4) - down + 4, 4) + down

    mine = block_of(c)

    loads = []
    for n, (src, dst) in enumerate(
        ((value_up, vup_v), (w_out, wout_v), (w_gate, wgate_v), (w_up, wup_v), (w_down, wdown_v))
    ):
        loads.append(pltpu.make_async_copy(src, dst, wsem.at[n]))
        loads[-1].start()

    def remote(src, dst, send_sem, recv_sem, dp, tp):
        return pltpu.make_async_remote_copy(
            src_ref=src, dst_ref=dst, send_sem=send_sem, recv_sem=recv_sem, device_id=(dp, tp), device_id_type=MESH
        )

    barrier = pltpu.get_barrier_semaphore()
    loop(1, 16, lambda i: pl.semaphore_signal(barrier, 1, device_id=(g, lax.rem(c + i, 16)), device_id_type=MESH))
    loop(1, 4, lambda i: pl.semaphore_signal(barrier, 1, device_id=(lax.rem(g + 2 * i, 8), c), device_id_type=MESH))
    pl.semaphore_signal(barrier, 1, device_id=(sib, c), device_id_type=MESH)
    pl.semaphore_wait(barrier, 19)

    def lat_copy(i, source):
        to = lax.rem(c + i, 16)
        return remote(lat.at[to], latr.at[source], lat_ss.at[to], lat_rs.at[source], g, to)

    loop(1, 16, lambda i: lat_copy(i, c).start())
    latr[c] = lat[c]
    row = lax.broadcasted_iota(jnp.int32, (512, 512), 0)
    col = lax.broadcasted_iota(jnp.int32, (512, 512), 1)
    wanted = ((row & 31) >> 1) * 32 + (row & 1) * 16 + ((row >> 5) & 1) * 8 + (row >> 6)
    perm[...] = jnp.where(col == wanted, 1.0, 0.0).astype(bf16)
    loop(1, 16, lambda i: lat_copy(i, lax.rem(c + 16 - i, 16)).wait_recv())
    ordered = jnp.dot(perm[...], latr[...].reshape(512, 512), preferred_element_type=f32).astype(bf16)
    loads[0].wait()
    for head in range(8):
        part = jnp.dot(ordered[64 * head : 64 * head + 64], vup_v[head], preferred_element_type=f32)
        xbuf[0, g, :, 128 * head : 128 * head + 128] = part[:32].astype(bf16)
        xbuf[1, g, :, 128 * head : 128 * head + 128] = part[32:].astype(bf16)

    def gather_ring(buf, ss, rs, s, i, source):
        to = lax.rem(g + 2 * i, 8)
        return remote(buf.at[s, g], buf.at[s, source], ss.at[s, i], rs.at[s, source], to, c)

    def gather_pair(buf, ss, rs, s, i, sent, got):
        return remote(buf.at[s, sent], buf.at[s, got], ss.at[s, 4 + i], rs.at[s, got], sib, c)

    def gather_start(buf, ss, rs, s):
        loop(1, 4, lambda i: gather_ring(buf, ss, rs, s, i, g).start())
        gather_pair(buf, ss, rs, s, 0, g, g).start()

    def gather_rest(buf, ss, rs, s):
        def forward(i):
            src = lax.rem(g + 8 - 2 * i, 8)
            gather_ring(buf, ss, rs, s, i, src).wait_recv()
            gather_pair(buf, ss, rs, s, i, src, src).start()

        loop(1, 4, forward)
        loop(0, 4, lambda i: gather_pair(buf, ss, rs, s, i, g, lax.rem(sib + 8 - 2 * i, 8)).wait_recv())

    def gather_end(buf, ss, rs, s):
        loop(1, 4, lambda i: gather_ring(buf, ss, rs, s, i, g).wait_send())
        loop(0, 4, lambda i: gather_pair(buf, ss, rs, s, i, g, g).wait_send())

    def shift(s, one, two):
        over_x, over_z = one + s * (two - one), two + s * (one - two)
        return 4 * lax.rem(z + over_z, 4) + lax.rem(x + over_x, 4)

    def scatter_one(ss, rs, s, one, two):
        return remote(
            s3.at[s, block_of(shift(s, one, two))],
            r3.at[s, 4 * one + two],
            ss.at[s, 4 * one + two],
            rs.at[s, 4 * one + two],
            g,
            shift(s, one, 0),
        )

    def scatter_two(ss, rs, s, two):
        return remote(t3.at[s, two], r3.at[s, two], ss.at[s, two], rs.at[s, two], g, shift(s, 0, two))

    def scatter(value, ss, rs, s):
        s3[s] = value.reshape(16, 16, value.shape[1]).astype(bf16)
        loop(0, 12, lambda n: scatter_one(ss, rs, s, 1 + n // 4, lax.rem(n + 1, 4)).start())

    def first_sum(ss, rs, s, two):
        loop(1, 4, lambda one: scatter_one(ss, rs, s, one, two).wait_recv())
        total = s3[s, block_of(shift(s, 0, two))].astype(f32)
        for one in range(1, 4):
            total = total + r3[s, 4 * one + two].astype(f32)
        return total

    def scatter_mid(ss, rs, s):
        def send(two):
            t3[s, two] = first_sum(ss, rs, s, two).astype(bf16)
            scatter_two(ss, rs, s, two).start()

        loop(1, 4, send)

    def scatter_sum(ss, rs, s, first):
        total = first + first_sum(ss, rs, s, 0)
        loop(1, 4, lambda two: scatter_two(ss, rs, s, two).wait_recv())
        for two in range(1, 4):
            total = total + r3[s, two].astype(f32)
        loop(0, 12, lambda n: scatter_one(ss, rs, s, 1 + n // 4, lax.rem(n, 4)).wait_send())
        loop(1, 4, lambda two: scatter_two(ss, rs, s, two).wait_send())
        return total

    def spread(buf, ss, rs, s, slot, source, to):
        block = block_of(source)
        return remote(buf.at[s, block], buf.at[s, block], ss.at[s, slot], rs.at[s, source], g, to)

    def spread_start(buf, ss, rs, s):
        loop(1, 4, lambda i: spread(buf, ss, rs, s, i, c, shift(s, i, 0)).start())
        loop(1, 4, lambda j: spread(buf, ss, rs, s, 3 + j, c, shift(s, 0, j)).start())

    def spread_mid(buf, ss, rs, s):
        def forward(i):
            source = shift(s, 4 - i, 0)
            spread(buf, ss, rs, s, i, source, source).wait_recv()
            loop(1, 4, lambda j: spread(buf, ss, rs, s, 3 + 3 * i + j, source, shift(s, 0, j)).start())

        loop(1, 4, forward)

    def spread_wait(buf, ss, rs, s):
        def arrive(n):
            source = shift(s, lax.rem(4 - n // 3, 4), 3 - lax.rem(n, 3))
            spread(buf, ss, rs, s, 0, source, source).wait_recv()

        loop(0, 12, arrive)

    def spread_end(buf, ss, rs, s):
        loop(1, 16, lambda slot: spread(buf, ss, rs, s, slot, c, shift(s, 1, 0)).wait_send())

    loop(0, 2, lambda s: gather_start(xbuf, x_ss, x_rs, s))
    loads[1].wait()

    def out_stage(s):
        gather_rest(xbuf, x_ss, x_rs, s)
        rows = xbuf[s].reshape(256, xbuf.shape[3])
        scatter(jnp.dot(rows, wout_v[...], preferred_element_type=f32), s3_ss, s3_rs, s)

    loop(0, 2, out_stage)
    loop(0, 2, lambda s: scatter_mid(s3_ss, s3_rs, s))

    def after_stage(s):
        after[s] = scatter_sum(s3_ss, s3_rs, s, hidden[s, mine].astype(f32))
        ybuf[s, mine] = after[s].astype(bf16)
        spread_start(ybuf, y_ss, y_rs, s)

    loop(0, 2, after_stage)
    loop(0, 2, lambda s: spread_mid(ybuf, y_ss, y_rs, s))
    loads[2].wait()
    loads[3].wait()
    lane = lax.broadcasted_iota(jnp.int32, (32, 128), 1)

    def two_part(total):
        high = total.astype(bf16)
        low = (total - high.astype(f32)).astype(bf16)
        return jnp.where(lane < 64, high.astype(f32), low.astype(f32)).astype(bf16)

    def one_part(pair):
        return pair[:, 0:1].astype(f32) + pair[:, 64:65].astype(f32)

    def pair_copy(s, chunk):
        return remote(pair_s.at[s, chunk], pair_r.at[s, chunk], pair_ss.at[s, chunk], pair_rs.at[s, chunk], sib, c)

    def ring_copy(s, chunk, source):
        return remote(
            ring_s.at[s, chunk], ring_r.at[s, source], ring_ss.at[s, chunk], ring_rs.at[s, source], 2 * chunk + k, c
        )

    def gate_stage(s):
        spread_wait(ybuf, y_ss, y_rs, s)
        rows = ybuf[s].reshape(256, ybuf.shape[3]).astype(f32)
        squares = jnp.sum(rows * rows, axis=1, keepdims=True)
        scaled = (rows * gain[...]).astype(bf16)
        gu[s, :, :, :, width : width + 128] = jnp.broadcast_to(squares, (256, 128)).reshape(4, 2, 32, 128)
        gu[s, :, :, :, 0:ff] = jnp.dot(scaled, wgate_v[...], preferred_element_type=f32).reshape(4, 2, 32, ff)
        gu[s, :, :, :, ff:width] = jnp.dot(scaled, wup_v[...], preferred_element_type=f32).reshape(4, 2, 32, ff)

        def give(i):
            chunk = lax.rem(y + 1 + i, 4)
            pair_s[s, chunk, :, 0:width] = gu[s, chunk, 1 - k, :, 0:width].astype(bf16)
            pair_s[s, chunk, :, width : width + 128] = two_part(gu[s, chunk, 1 - k, :, width : width + 128])
            pair_copy(s, chunk).start()

        loop(0, 4, give)

        def merge(i):
            chunk = lax.rem(y + 1 + i, 4)
            pair_copy(s, chunk).wait_recv()
            total = gu[s, chunk, k, :, 0:width] + pair_r[s, chunk, :, 0:width].astype(f32)
            squares = gu[s, chunk, k, :, width : width + 128] + one_part(pair_r[s, chunk, :, width : width + 128])
            gu[s, chunk, k, :, 0:width] = total
            gu[s, chunk, k, :, width : width + 128] = squares

            @pl.when(chunk != y)
            def _():
                ring_s[s, chunk, :, 0:width] = total.astype(bf16)
                ring_s[s, chunk, :, width : width + 128] = two_part(squares)
                ring_copy(s, chunk, y).start()

        loop(0, 4, merge)

    loop(0, 2, gate_stage)

    def act_stage(s):
        def ring_add(i):
            source = lax.rem(y + i, 4)
            ring_copy(s, source, source).wait_recv()
            gu[s, y, k, :, 0:width] += ring_r[s, source, :, 0:width].astype(f32)
            gu[s, y, k, :, width : width + 128] += one_part(ring_r[s, source, :, width : width + 128])

        loop(1, 4, ring_add)
        scale = 1.0 / jnp.sqrt(gu[s, y, k, :, width : width + 1] / D + norm_eps)
        gate = gu[s, y, k, :, 0:ff] * scale
        up = gu[s, y, k, :, ff:width] * scale
        hbuf[s, g] = (jax.nn.silu(gate) * up).astype(bf16)
        gather_start(hbuf, h_ss, h_rs, s)

    loop(0, 2, act_stage)
    loads[4].wait()

    def down_stage(s):
        gather_rest(hbuf, h_ss, h_rs, s)
        rows = hbuf[s].reshape(256, ff)
        scatter(jnp.dot(rows, wdown_v[...], preferred_element_type=f32), s7_ss, s7_rs, s)

    loop(0, 2, down_stage)
    loop(0, 2, lambda s: scatter_mid(s7_ss, s7_rs, s))

    def result_stage(s):
        out[s, mine] = scatter_sum(s7_ss, s7_rs, s, after[s]).astype(bf16)
        spread_start(out, o_ss, o_rs, s)

    loop(0, 2, result_stage)
    loop(0, 2, lambda s: spread_mid(out, o_ss, o_rs, s))
    loop(1, 16, lambda i: lat_copy(i, c).wait_send())

    def end_stage(s):
        gather_end(xbuf, x_ss, x_rs, s)
        spread_end(ybuf, y_ss, y_rs, s)
        loop(0, 4, lambda i: pair_copy(s, i).wait_send())
        loop(1, 4, lambda i: ring_copy(s, lax.rem(y + i, 4), y).wait_send())
        gather_end(hbuf, h_ss, h_rs, s)
        spread_end(out, o_ss, o_rs, s)
        spread_wait(out, o_ss, o_rs, s)

    loop(0, 2, end_stage)


def dense(lat, value_up, hidden, gain, w_out, w_gate, w_up, w_down):
    steps, total, cols = hidden.shape
    ff = w_gate.shape[1]
    bf16, f32 = jnp.bfloat16, jnp.float32
    vmem, sems = pltpu.VMEM, pltpu.SemaphoreType.DMA
    in_vmem, anywhere = pl.BlockSpec(memory_space=pltpu.VMEM), pl.BlockSpec(memory_space=pl.ANY)
    result = pl.pallas_call(
        dense_kernel,
        out_shape=jax.ShapeDtypeStruct((steps, 16, 16, cols), bf16),
        in_specs=[in_vmem, anywhere, in_vmem, in_vmem, anywhere, anywhere, anywhere, anywhere],
        out_specs=in_vmem,
        scratch_shapes=[
            vmem(value_up.shape, bf16),
            vmem(w_out.shape, bf16),
            vmem(w_gate.shape, bf16),
            vmem(w_up.shape, bf16),
            vmem(w_down.shape, bf16),
            vmem(lat.shape, bf16),
            vmem((512, 512), bf16),
            vmem((2, 8, 32, w_out.shape[0]), bf16),
            vmem((2, 16, 16, cols), bf16),
            vmem((2, 16, 16, cols), bf16),
            vmem((2, 4, 16, cols), bf16),
            vmem((2, 16, cols), f32),
            vmem((2, 16, 16, cols), bf16),
            vmem((2, 4, 2, 32, 2 * ff + 128), f32),
            vmem((2, 4, 32, 2 * ff + 128), bf16),
            vmem((2, 4, 32, 2 * ff + 128), bf16),
            vmem((2, 4, 32, 2 * ff + 128), bf16),
            vmem((2, 4, 32, 2 * ff + 128), bf16),
            vmem((2, 8, 32, ff), bf16),
            sems((5,)),
            sems((16,)),
            sems((16,)),
            sems((2, 8)),
            sems((2, 8)),
            sems((2, 16)),
            sems((2, 16)),
            sems((2, 16)),
            sems((2, 16)),
            sems((2, 4)),
            sems((2, 4)),
            sems((2, 4)),
            sems((2, 4)),
            sems((2, 8)),
            sems((2, 8)),
            sems((2, 16)),
            sems((2, 16)),
            sems((2, 16)),
            sems((2, 16)),
        ],
        compiler_params=pltpu.CompilerParams(collective_id=1, has_side_effects=True, vmem_limit_bytes=52 * 2**20),
    )(lat, value_up, hidden.reshape(steps, 16, 16, cols), gain, w_out, w_gate, w_up, w_down)
    return result.reshape(steps, total, cols)


def shards(
    old_cache,
    lengths,
    new_slot,
    queries,
    new_latent,
    hidden,
    value_up_weight,
    w_out,
    norm_gain,
    w_gate,
    w_up,
    w_down,
):
    dp_count = lax.axis_size("dp")
    tp_count = lax.axis_size("tp")
    my_group = lax.axis_index("dp")
    my_column = lax.axis_index("tp")
    group_req = old_cache.shape[0]
    per_pair = group_req // dp_count
    req_dev = queries.shape[1]
    req_total = new_slot.shape[0]
    kv_rank = value_up_weight.shape[1]
    everyone = jnp.arange(req_total, dtype=jnp.int32)
    order = jnp.arange(group_req, dtype=jnp.int32)
    out_slots = order // per_pair * group_req + my_group * per_pair + order % per_pair
    picked = jnp.sum(
        jnp.where(new_slot[None, :] == out_slots[:, None], everyone[None, :] % group_req, 0), axis=1
    )
    arrived = move(picked, old_cache, dp_count, tp_count)
    my_slots = (my_group * tp_count + my_column) * req_dev + jnp.arange(req_dev, dtype=jnp.int32)
    my_lengths = jnp.sum(jnp.where(new_slot[None, :] == my_slots[:, None], lengths[None, :], 0), axis=1)
    new_cache, latents = attend(my_lengths, arrived, queries, new_latent, tp_count, kv_rank)
    gain = norm_gain.astype(jnp.float32)[None, :]
    layer_out = dense(latents, value_up_weight, hidden, gain, w_out, w_gate, w_up, w_down)
    return (new_cache, layer_out)


def solution(mesh):
    in_specs = (
        P("dp", "tp", None),
        P(),
        P(),
        P(None, ("dp", "tp"), None, None),
        P(None, ("dp", "tp"), None),
        P(None, None, "dp"),
        P("tp", None, None),
        P("tp", "dp"),
        P("dp"),
        P("dp", "tp"),
        P("dp", "tp"),
        P("tp", "dp"),
    )
    out_specs = (P(("dp", "tp"), None, None), P(None, None, "dp"))
    return jax.shard_map(shards, mesh=mesh, in_specs=in_specs, out_specs=out_specs, check_vma=False)
```

```python
import functools

import jax
import jax.numpy as jnp
from jax import lax
from jax.experimental import pallas as pl
from jax.experimental.pallas import tpu as pltpu
from jax.sharding import PartitionSpec as P

D = 7168


MESH = pl.DeviceIdType.MESH


def loop(low, high, action):
    def body(i, carry):
        action(i)
        return carry

    lax.fori_loop(low, high, body, 0)


def move_kernel(
    n_dp, n_tp, chunks, ahead, picked, cache, out, loaded, stage, mid, load_sem, own_sem, send1, recv1, send2, recv2
):
    group_req, piece, width = loaded.shape
    rows = piece // chunks
    rank = (stage.shape[2] - 128) // 2
    pairs = n_tp // n_dp
    g = lax.axis_index("dp")
    c = lax.axis_index("tp")

    load = pltpu.make_async_copy(cache, loaded, load_sem)
    load.start()
    barrier = pltpu.get_barrier_semaphore()

    def greet_dp(i):
        pl.semaphore_signal(barrier, 1, device_id=(lax.rem(g + i, n_dp), c), device_id_type=MESH)

    def greet_tp(i):
        pl.semaphore_signal(barrier, 1, device_id=(g, lax.rem(c + i, n_tp)), device_id_type=MESH)

    loop(1, n_dp, greet_dp)
    loop(1, n_tp, greet_tp)
    pl.semaphore_wait(barrier, n_dp + n_tp - 2)
    load.wait()

    def sort(q):
        part = pl.ds(q * rows, rows)

        def one(i):
            first = picked[2 * i]
            second = picked[2 * i + 1]
            stage[i, part, 0:rank] = loaded[first, part, 0:rank]
            stage[i, part, rank : 2 * rank] = loaded[second, part, 0:rank]
            tails = [loaded[first, part, rank:width], loaded[second, part, rank:width]]
            stage[i, part, 2 * rank :] = jnp.concatenate(tails, axis=1)

        loop(0, n_tp, one)
        for n in range(pairs):
            mid[pairs * g + n, part] = stage[pairs * g + n, part]

    def over_dp(q, i, from_group):
        to_group = lax.rem(g + i, n_dp)
        part = pl.ds(q * rows, rows)
        return pltpu.make_async_remote_copy(
            src_ref=stage.at[pl.ds(pairs * to_group, pairs), part],
            dst_ref=mid.at[pl.ds(pairs * from_group, pairs), part],
            send_sem=send1.at[q, to_group],
            recv_sem=recv1.at[q, from_group],
            device_id=(to_group, c),
            device_id_type=MESH,
        )

    def over_tp(q, i, from_column):
        to_column = lax.rem(c + i, n_tp)
        return pltpu.make_async_remote_copy(
            src_ref=mid.at[to_column, pl.ds(q * rows, rows)],
            dst_ref=out.at[pl.ds(from_column * piece + q * rows, rows)],
            send_sem=send2.at[q, to_column],
            recv_sem=recv2.at[q, from_column],
            device_id=(g, to_column),
            device_id_type=MESH,
        )

    def own(q):
        return pltpu.make_async_copy(
            mid.at[c, pl.ds(q * rows, rows)], out.at[pl.ds(c * piece + q * rows, rows)], own_sem.at[q]
        )

    for q in range(chunks + 1):
        if q < chunks:
            sort(q)
            if q >= ahead:
                loop(1, n_dp, lambda i: over_dp(q - ahead, i, g).wait_send())
            loop(1, n_dp, lambda i: over_dp(q, i, g).start())
        if q >= 1:
            loop(1, n_dp, lambda i: over_dp(q - 1, i, lax.rem(g + n_dp - i, n_dp)).wait_recv())
            loop(1, n_tp, lambda i: over_tp(q - 1, i, c).start())
            own(q - 1).start()
    for q in range(chunks):
        if q >= chunks - ahead:
            loop(1, n_dp, lambda i: over_dp(q, i, g).wait_send())
        loop(1, n_tp, lambda i: over_tp(q, i, c).wait_send())
        loop(1, n_tp, lambda i: over_tp(q, i, lax.rem(c + n_tp - i, n_tp)).wait_recv())
        own(q).wait()


def move(picked, old_cache, n_dp, n_tp, chunks=12, ahead=2):
    group_req, piece, width = old_cache.shape
    packed = (n_tp, piece, 2 * width)
    sems = pltpu.SemaphoreType.DMA
    return pl.pallas_call(
        functools.partial(move_kernel, n_dp, n_tp, chunks, ahead),
        out_shape=jax.ShapeDtypeStruct((piece * n_tp, 2 * width), old_cache.dtype),
        in_specs=[pl.BlockSpec(memory_space=pltpu.SMEM), pl.BlockSpec(memory_space=pl.ANY)],
        out_specs=pl.BlockSpec(memory_space=pl.ANY),
        scratch_shapes=[
            pltpu.VMEM(old_cache.shape, old_cache.dtype),
            pltpu.VMEM(packed, old_cache.dtype),
            pltpu.VMEM(packed, old_cache.dtype),
            sems,
            sems((chunks,)),
            sems((chunks, n_dp)),
            sems((chunks, n_dp)),
            sems((chunks, n_tp)),
            sems((chunks, n_tp)),
        ],
        compiler_params=pltpu.CompilerParams(collective_id=0, has_side_effects=True, vmem_limit_bytes=48 * 2**20),
    )(picked, old_cache)


score_scale = 0.07216878364870323
norm_eps = 1e-06


def attend_kernel(lens, main, tail, queries, new_main, new_tail, cache_out, lat, scores, query):
    f32, bf16 = jnp.float32, jnp.bfloat16
    item = pl.program_id(0)
    length = lens[item]
    context, rank = main.shape
    heads = queries.shape[3]
    both = 2 * heads
    query[:rank] = jnp.concatenate([queries[0, 0, :rank], queries[1, 0, :rank]], axis=1)
    query[rank:] = jnp.zeros((128, both), bf16)
    half = pl.multiple_of(rank + item * 64, 64)
    query[pl.ds(half, 64)] = jnp.concatenate([queries[0, 0, rank:], queries[1, 0, rank:]], axis=1)
    block = context // 2
    row = lax.broadcasted_iota(jnp.int32, (block, rank), 0)
    tail_row = lax.broadcasted_iota(jnp.int32, (block, 128), 0)
    tail_length = jnp.where(lax.broadcasted_iota(jnp.int32, (block, 128), 1) < 64, lens[0], lens[1])
    place = lax.broadcasted_iota(jnp.int32, (block, both), 0)
    last = length + lax.broadcasted_iota(jnp.int32, (block, both), 1) // heads

    def fill(old, position, size, first, second):
        new = jnp.where(position == size, first.astype(f32), jnp.where(position == size + 1, second.astype(f32), 0.0))
        return jnp.where(position < size, old.astype(f32), new).astype(bf16)

    def score(i, top):
        start = pl.multiple_of(i * block, block)
        rows = pl.ds(start, block)
        keys = fill(main[rows], row + start, length, new_main[0, item], new_main[1, item])
        tails = fill(tail[rows], tail_row + start, tail_length, new_tail[0], new_tail[1])
        cache_out[0, :rank, rows] = keys.T
        tails_t = tails.T

        @pl.when(item == 0)
        def _():
            cache_out[0, rank:, rows] = tails_t[:64]

        @pl.when(item == 1)
        def _():
            cache_out[0, rank:, rows] = tails_t[64:]

        both_parts = jnp.concatenate([keys, tails], axis=1)
        raw = jnp.dot(both_parts, query[...], preferred_element_type=f32)
        raw = jnp.where(place + start <= last, raw * score_scale, -jnp.inf)
        scores[rows] = raw
        return jnp.maximum(top, jnp.max(raw, axis=0, keepdims=True))

    top = lax.fori_loop(0, context // block, score, jnp.full((1, both), -jnp.inf, f32))
    exponent = jnp.exp(scores[...] - top)
    total = jnp.sum(exponent, axis=0, keepdims=True)
    mixed_t = jnp.dot(cache_out[0, :rank], exponent.astype(bf16), preferred_element_type=f32)
    mixed = (mixed_t / total).T
    mixed = mixed.reshape(2, lat.shape[0], -1, rank)
    mixed = jnp.concatenate([mixed[0], mixed[1]], axis=1).astype(bf16)
    lat[:, pl.ds(pl.multiple_of(item * 16, 16), 16)] = mixed


def attend(my_lengths, arrived, queries, new_latent, n_tp, kv_rank):
    context = arrived.shape[0]
    steps, items, heads, width = queries.shape
    bf16 = jnp.bfloat16
    new_tail = new_latent[:, :, kv_rank:].reshape(steps, 1, -1)
    flipped, latents = pl.pallas_call(
        attend_kernel,
        grid=(items,),
        out_shape=(
            jax.ShapeDtypeStruct((items, width, context), bf16),
            jax.ShapeDtypeStruct((n_tp, items * steps * heads // n_tp, kv_rank), bf16),
        ),
        in_specs=[
            pl.BlockSpec(memory_space=pltpu.SMEM),
            pl.BlockSpec((context, kv_rank), lambda i: (0, i)),
            pl.BlockSpec((context, 128), lambda i: (0, 2 * kv_rank // 128)),
            pl.BlockSpec((steps, 1, width, heads), lambda i: (0, i, 0, 0)),
            pl.BlockSpec((steps, items, 1, kv_rank), lambda i: (0, 0, 0, 0)),
            pl.BlockSpec((steps, 1, 128), lambda i: (0, 0, 0)),
        ],
        out_specs=(
            pl.BlockSpec((1, width, context), lambda i: (i, 0, 0)),
            pl.BlockSpec((n_tp, items * steps * heads // n_tp, kv_rank), lambda i: (0, 0, 0)),
        ),
        scratch_shapes=[
            pltpu.VMEM((context, steps * heads), jnp.float32),
            pltpu.VMEM((kv_rank + 128, steps * heads), bf16),
        ],
        compiler_params=pltpu.CompilerParams(vmem_limit_bytes=40 * 2**20),
    )(my_lengths, arrived, arrived, queries.transpose(0, 1, 3, 2), new_latent[:, :, None, :kv_rank], new_tail)
    return flipped.transpose(0, 2, 1), latents


def dense_kernel(
    lat,
    value_up,
    hidden,
    gain,
    w_out,
    w_gate,
    w_up,
    w_down,
    out,
    vup_v,
    wout_v,
    wgate_v,
    wup_v,
    wdown_v,
    latr,
    perm,
    xbuf,
    s3,
    r3,
    after,
    ybuf,
    gu,
    pair_s,
    pair_r,
    ring_s,
    ring_r,
    hbuf,
    wsem,
    lat_ss,
    lat_rs,
    x_ss,
    x_rs,
    s3_ss,
    s3_rs,
    y_ss,
    y_rs,
    pair_ss,
    pair_rs,
    ring_ss,
    ring_rs,
    h_ss,
    h_rs,
    s7_ss,
    s7_rs,
    o_ss,
    o_rs,
):
    f32, bf16 = jnp.float32, jnp.bfloat16
    g = lax.axis_index("dp")
    c = lax.axis_index("tp")
    y, k = g // 2, lax.rem(g, 2)
    z, x = c // 4, lax.rem(c, 4)
    sib = g + 1 - 2 * k
    ff = wgate_v.shape[1]
    width = 2 * ff

    def block_of(column):
        down = column // 4
        return 4 * lax.rem(lax.rem(column, 4) - down + 4, 4) + down

    mine = block_of(c)

    loads = []
    for n, (src, dst) in enumerate(
        ((value_up, vup_v), (w_out, wout_v), (w_gate, wgate_v), (w_up, wup_v), (w_down, wdown_v))
    ):
        loads.append(pltpu.make_async_copy(src, dst, wsem.at[n]))
        loads[-1].start()

    def remote(src, dst, send_sem, recv_sem, dp, tp):
        return pltpu.make_async_remote_copy(
            src_ref=src, dst_ref=dst, send_sem=send_sem, recv_sem=recv_sem, device_id=(dp, tp), device_id_type=MESH
        )

    barrier = pltpu.get_barrier_semaphore()
    loop(1, 16, lambda i: pl.semaphore_signal(barrier, 1, device_id=(g, lax.rem(c + i, 16)), device_id_type=MESH))
    loop(1, 4, lambda i: pl.semaphore_signal(barrier, 1, device_id=(lax.rem(g + 2 * i, 8), c), device_id_type=MESH))
    pl.semaphore_signal(barrier, 1, device_id=(sib, c), device_id_type=MESH)
    pl.semaphore_wait(barrier, 19)

    def lat_copy(i, source):
        to = lax.rem(c + i, 16)
        return remote(lat.at[to], latr.at[source], lat_ss, lat_rs, g, to)

    lat_all = remote(lat.at[pl.ds(0, 15)], latr.at[pl.ds(0, 15)], lat_ss, lat_rs, g, lax.rem(c + 1, 16))
    loop(1, 16, lambda i: lat_copy(i, c).start())
    latr[c] = lat[c]
    row = lax.broadcasted_iota(jnp.int32, (512, 512), 0)
    col = lax.broadcasted_iota(jnp.int32, (512, 512), 1)
    wanted = ((row & 31) >> 1) * 32 + (row & 1) * 16 + ((row >> 5) & 1) * 8 + (row >> 6)
    perm[...] = jnp.where(col == wanted, 1.0, 0.0).astype(bf16)
    lat_all.wait_recv()
    ordered = jnp.dot(perm[...], latr[...].reshape(512, 512), preferred_element_type=f32).astype(bf16)
    loads[0].wait()
    for head in range(8):
        part = jnp.dot(ordered[64 * head : 64 * head + 64], vup_v[head], preferred_element_type=f32)
        xbuf[0, g, :, 128 * head : 128 * head + 128] = part[:32].astype(bf16)
        xbuf[1, g, :, 128 * head : 128 * head + 128] = part[32:].astype(bf16)

    def gather_ring(buf, ss, rs, s, i, source):
        to = lax.rem(g + 2 * i, 8)
        return remote(buf.at[s, g], buf.at[s, source], ss.at[s, i], rs.at[s, source], to, c)

    def gather_pair(buf, ss, rs, s, i, sent, got):
        return remote(buf.at[s, sent], buf.at[s, got], ss.at[s, 4 + i], rs.at[s, got], sib, c)

    def gather_start(buf, ss, rs, s):
        loop(1, 4, lambda i: gather_ring(buf, ss, rs, s, i, g).start())
        gather_pair(buf, ss, rs, s, 0, g, g).start()

    def gather_rest(buf, ss, rs, s):
        def forward(i):
            src = lax.rem(g + 8 - 2 * i, 8)
            gather_ring(buf, ss, rs, s, i, src).wait_recv()
            gather_pair(buf, ss, rs, s, i, src, src).start()

        loop(1, 4, forward)
        loop(0, 4, lambda i: gather_pair(buf, ss, rs, s, i, g, lax.rem(sib + 8 - 2 * i, 8)).wait_recv())

    def gather_end(buf, ss, rs, s):
        loop(1, 4, lambda i: gather_ring(buf, ss, rs, s, i, g).wait_send())
        loop(0, 4, lambda i: gather_pair(buf, ss, rs, s, i, g, g).wait_send())

    def scatter_copy(ss, rs, s, i, source):
        to = lax.rem(c + i, 16)
        return remote(s3.at[s, block_of(to)], r3.at[s, source], ss.at[s], rs.at[s], g, to)

    def scatter_all(ss, rs, s):
        part = pl.ds(0, 15)
        return remote(s3.at[s, part], r3.at[s, part], ss.at[s], rs.at[s], g, lax.rem(c + 1, 16))

    def scatter(value, ss, rs, s):
        s3[s] = value.reshape(16, 16, value.shape[1]).astype(bf16)
        loop(1, 16, lambda i: scatter_copy(ss, rs, s, i, c).start())

    def scatter_sum(ss, rs, s, first):
        r3[s, c] = s3[s, mine]
        scatter_all(ss, rs, s).wait_recv()
        total = first + jnp.sum(r3[s].astype(f32), axis=0)
        scatter_all(ss, rs, s).wait_send()
        return total

    def spread(buf, ss, rs, s, i, source):
        to = lax.rem(c + i, 16)
        return remote(buf.at[s, mine], buf.at[s, block_of(source)], ss.at[s], rs.at[s], g, to)

    def spread_all(buf, ss, rs, s):
        part = pl.ds(0, 15)
        return remote(buf.at[s, part], buf.at[s, part], ss.at[s], rs.at[s], g, lax.rem(c + 1, 16))

    def spread_start(buf, ss, rs, s):
        loop(1, 16, lambda i: spread(buf, ss, rs, s, i, c).start())

    def spread_wait(buf, ss, rs, s):
        spread_all(buf, ss, rs, s).wait_recv()

    def spread_end(buf, ss, rs, s):
        spread_all(buf, ss, rs, s).wait_send()

    loop(0, 2, lambda s: gather_start(xbuf, x_ss, x_rs, s))
    loads[1].wait()

    def out_stage(s):
        gather_rest(xbuf, x_ss, x_rs, s)
        rows = xbuf[s].reshape(256, xbuf.shape[3])
        scatter(jnp.dot(rows, wout_v[...], preferred_element_type=f32), s3_ss, s3_rs, s)

    loop(0, 2, out_stage)

    def after_stage(s):
        after[s] = scatter_sum(s3_ss, s3_rs, s, hidden[s, mine].astype(f32))
        ybuf[s, mine] = after[s].astype(bf16)
        spread_start(ybuf, y_ss, y_rs, s)

    loop(0, 2, after_stage)
    loads[2].wait()
    loads[3].wait()
    lane = lax.broadcasted_iota(jnp.int32, (32, 128), 1)

    def two_part(total):
        high = total.astype(bf16)
        low = (total - high.astype(f32)).astype(bf16)
        return jnp.where(lane < 64, high.astype(f32), low.astype(f32)).astype(bf16)

    def one_part(pair):
        return pair[:, 0:1].astype(f32) + pair[:, 64:65].astype(f32)

    def pair_copy(s, chunk):
        return remote(pair_s.at[s, chunk], pair_r.at[s, chunk], pair_ss.at[s, chunk], pair_rs.at[s, chunk], sib, c)

    def ring_copy(s, chunk, source):
        return remote(
            ring_s.at[s, chunk], ring_r.at[s, source], ring_ss.at[s, chunk], ring_rs.at[s, source], 2 * chunk + k, c
        )

    def gate_stage(s):
        spread_wait(ybuf, y_ss, y_rs, s)
        rows = ybuf[s].reshape(256, ybuf.shape[3]).astype(f32)
        squares = jnp.sum(rows * rows, axis=1, keepdims=True)
        scaled = (rows * gain[...]).astype(bf16)
        gu[s, :, :, :, width : width + 128] = jnp.broadcast_to(squares, (256, 128)).reshape(4, 2, 32, 128)
        gu[s, :, :, :, 0:ff] = jnp.dot(scaled, wgate_v[...], preferred_element_type=f32).reshape(4, 2, 32, ff)
        gu[s, :, :, :, ff:width] = jnp.dot(scaled, wup_v[...], preferred_element_type=f32).reshape(4, 2, 32, ff)

        def give(i):
            chunk = lax.rem(y + 1 + i, 4)
            pair_s[s, chunk, :, 0:width] = gu[s, chunk, 1 - k, :, 0:width].astype(bf16)
            pair_s[s, chunk, :, width : width + 128] = two_part(gu[s, chunk, 1 - k, :, width : width + 128])
            pair_copy(s, chunk).start()

        loop(0, 4, give)

        def merge(i):
            chunk = lax.rem(y + 1 + i, 4)
            pair_copy(s, chunk).wait_recv()
            total = gu[s, chunk, k, :, 0:width] + pair_r[s, chunk, :, 0:width].astype(f32)
            squares = gu[s, chunk, k, :, width : width + 128] + one_part(pair_r[s, chunk, :, width : width + 128])
            gu[s, chunk, k, :, 0:width] = total
            gu[s, chunk, k, :, width : width + 128] = squares

            @pl.when(chunk != y)
            def _():
                ring_s[s, chunk, :, 0:width] = total.astype(bf16)
                ring_s[s, chunk, :, width : width + 128] = two_part(squares)
                ring_copy(s, chunk, y).start()

        loop(0, 4, merge)

    loop(0, 2, gate_stage)

    def act_stage(s):
        def ring_add(i):
            source = lax.rem(y + i, 4)
            ring_copy(s, source, source).wait_recv()
            gu[s, y, k, :, 0:width] += ring_r[s, source, :, 0:width].astype(f32)
            gu[s, y, k, :, width : width + 128] += one_part(ring_r[s, source, :, width : width + 128])

        loop(1, 4, ring_add)
        scale = 1.0 / jnp.sqrt(gu[s, y, k, :, width : width + 1] / D + norm_eps)
        gate = gu[s, y, k, :, 0:ff] * scale
        up = gu[s, y, k, :, ff:width] * scale
        hbuf[s, g] = (jax.nn.silu(gate) * up).astype(bf16)
        gather_start(hbuf, h_ss, h_rs, s)

    loop(0, 2, act_stage)
    loads[4].wait()

    def down_stage(s):
        gather_rest(hbuf, h_ss, h_rs, s)
        rows = hbuf[s].reshape(256, ff)
        scatter(jnp.dot(rows, wdown_v[...], preferred_element_type=f32), s7_ss, s7_rs, s)

    loop(0, 2, down_stage)

    def result_stage(s):
        out[s, mine] = scatter_sum(s7_ss, s7_rs, s, after[s]).astype(bf16)
        spread_start(out, o_ss, o_rs, s)

    loop(0, 2, result_stage)
    lat_all.wait_send()

    def end_stage(s):
        gather_end(xbuf, x_ss, x_rs, s)
        spread_end(ybuf, y_ss, y_rs, s)
        loop(0, 4, lambda i: pair_copy(s, i).wait_send())
        loop(1, 4, lambda i: ring_copy(s, lax.rem(y + i, 4), y).wait_send())
        gather_end(hbuf, h_ss, h_rs, s)
        spread_end(out, o_ss, o_rs, s)
        spread_wait(out, o_ss, o_rs, s)

    loop(0, 2, end_stage)


def dense(lat, value_up, hidden, gain, w_out, w_gate, w_up, w_down):
    steps, total, cols = hidden.shape
    ff = w_gate.shape[1]
    bf16, f32 = jnp.bfloat16, jnp.float32
    vmem, sems = pltpu.VMEM, pltpu.SemaphoreType.DMA
    in_vmem, anywhere = pl.BlockSpec(memory_space=pltpu.VMEM), pl.BlockSpec(memory_space=pl.ANY)
    result = pl.pallas_call(
        dense_kernel,
        out_shape=jax.ShapeDtypeStruct((steps, 16, 16, cols), bf16),
        in_specs=[in_vmem, anywhere, in_vmem, in_vmem, anywhere, anywhere, anywhere, anywhere],
        out_specs=in_vmem,
        scratch_shapes=[
            vmem(value_up.shape, bf16),
            vmem(w_out.shape, bf16),
            vmem(w_gate.shape, bf16),
            vmem(w_up.shape, bf16),
            vmem(w_down.shape, bf16),
            vmem(lat.shape, bf16),
            vmem((512, 512), bf16),
            vmem((2, 8, 32, w_out.shape[0]), bf16),
            vmem((2, 16, 16, cols), bf16),
            vmem((2, 16, 16, cols), bf16),
            vmem((2, 16, cols), f32),
            vmem((2, 16, 16, cols), bf16),
            vmem((2, 4, 2, 32, 2 * ff + 128), f32),
            vmem((2, 4, 32, 2 * ff + 128), bf16),
            vmem((2, 4, 32, 2 * ff + 128), bf16),
            vmem((2, 4, 32, 2 * ff + 128), bf16),
            vmem((2, 4, 32, 2 * ff + 128), bf16),
            vmem((2, 8, 32, ff), bf16),
            sems((5,)),
            sems,
            sems,
            sems((2, 8)),
            sems((2, 8)),
            sems((2,)),
            sems((2,)),
            sems((2,)),
            sems((2,)),
            sems((2, 4)),
            sems((2, 4)),
            sems((2, 4)),
            sems((2, 4)),
            sems((2, 8)),
            sems((2, 8)),
            sems((2,)),
            sems((2,)),
            sems((2,)),
            sems((2,)),
        ],
        compiler_params=pltpu.CompilerParams(collective_id=1, has_side_effects=True, vmem_limit_bytes=52 * 2**20),
    )(lat, value_up, hidden.reshape(steps, 16, 16, cols), gain, w_out, w_gate, w_up, w_down)
    return result.reshape(steps, total, cols)


def shards(
    old_cache,
    lengths,
    new_slot,
    queries,
    new_latent,
    hidden,
    value_up_weight,
    w_out,
    norm_gain,
    w_gate,
    w_up,
    w_down,
):
    dp_count = lax.axis_size("dp")
    tp_count = lax.axis_size("tp")
    my_group = lax.axis_index("dp")
    my_column = lax.axis_index("tp")
    group_req = old_cache.shape[0]
    per_pair = group_req // dp_count
    req_dev = queries.shape[1]
    req_total = new_slot.shape[0]
    kv_rank = value_up_weight.shape[1]
    everyone = jnp.arange(req_total, dtype=jnp.int32)
    order = jnp.arange(group_req, dtype=jnp.int32)
    out_slots = order // per_pair * group_req + my_group * per_pair + order % per_pair
    picked = jnp.sum(
        jnp.where(new_slot[None, :] == out_slots[:, None], everyone[None, :] % group_req, 0), axis=1
    )
    arrived = move(picked, old_cache, dp_count, tp_count)
    my_slots = (my_group * tp_count + my_column) * req_dev + jnp.arange(req_dev, dtype=jnp.int32)
    my_lengths = jnp.sum(jnp.where(new_slot[None, :] == my_slots[:, None], lengths[None, :], 0), axis=1)
    new_cache, latents = attend(my_lengths, arrived, queries, new_latent, tp_count, kv_rank)
    gain = norm_gain.astype(jnp.float32)[None, :]
    layer_out = dense(latents, value_up_weight, hidden, gain, w_out, w_gate, w_up, w_down)
    return (new_cache, layer_out)


def solution(mesh):
    in_specs = (
        P("dp", "tp", None),
        P(),
        P(),
        P(None, ("dp", "tp"), None, None),
        P(None, ("dp", "tp"), None),
        P(None, None, "dp"),
        P("tp", None, None),
        P("tp", "dp"),
        P("dp"),
        P("dp", "tp"),
        P("dp", "tp"),
        P("tp", "dp"),
    )
    out_specs = (P(("dp", "tp"), None, None), P(None, None, "dp"))
    return jax.shard_map(shards, mesh=mesh, in_specs=in_specs, out_specs=out_specs, check_vma=False)
```

```python
import functools

import jax
import jax.numpy as jnp
from jax import lax
from jax.experimental import pallas as pl
from jax.experimental.pallas import tpu as pltpu
from jax.sharding import PartitionSpec as P

D = 7168


MESH = pl.DeviceIdType.MESH


def loop(low, high, action):
    def body(i, carry):
        action(i)
        return carry

    lax.fori_loop(low, high, body, 0)


def move_kernel(
    n_dp, n_tp, chunks, ahead, picked, cache, out, loaded, stage, mid, load_sem, own_sem, send1, recv1, send2, recv2
):
    group_req, piece, width = loaded.shape
    rows = piece // chunks
    rank = (stage.shape[2] - 128) // 2
    pairs = n_tp // n_dp
    g = lax.axis_index("dp")
    c = lax.axis_index("tp")

    load = pltpu.make_async_copy(cache, loaded, load_sem)
    load.start()
    barrier = pltpu.get_barrier_semaphore()

    def greet_dp(i):
        pl.semaphore_signal(barrier, 1, device_id=(lax.rem(g + i, n_dp), c), device_id_type=MESH)

    def greet_tp(i):
        pl.semaphore_signal(barrier, 1, device_id=(g, lax.rem(c + i, n_tp)), device_id_type=MESH)

    loop(1, n_dp, greet_dp)
    loop(1, n_tp, greet_tp)
    pl.semaphore_wait(barrier, n_dp + n_tp - 2)
    load.wait()

    def sort(q):
        part = pl.ds(q * rows, rows)

        def one(i):
            first = picked[2 * i]
            second = picked[2 * i + 1]
            stage[i, part, 0:rank] = loaded[first, part, 0:rank]
            stage[i, part, rank : 2 * rank] = loaded[second, part, 0:rank]
            tails = [loaded[first, part, rank:width], loaded[second, part, rank:width]]
            stage[i, part, 2 * rank :] = jnp.concatenate(tails, axis=1)

        loop(0, n_tp, one)
        for n in range(pairs):
            mid[pairs * g + n, part] = stage[pairs * g + n, part]

    def over_dp(q, i, from_group):
        to_group = lax.rem(g + i, n_dp)
        part = pl.ds(q * rows, rows)
        return pltpu.make_async_remote_copy(
            src_ref=stage.at[pl.ds(pairs * to_group, pairs), part],
            dst_ref=mid.at[pl.ds(pairs * from_group, pairs), part],
            send_sem=send1.at[q],
            recv_sem=recv1.at[q],
            device_id=(to_group, c),
            device_id_type=MESH,
        )

    def over_tp(q, i, from_column):
        to_column = lax.rem(c + i, n_tp)
        return pltpu.make_async_remote_copy(
            src_ref=mid.at[to_column, pl.ds(q * rows, rows)],
            dst_ref=out.at[pl.ds(from_column * piece + q * rows, rows)],
            send_sem=send2.at[q],
            recv_sem=recv2.at[q],
            device_id=(g, to_column),
            device_id_type=MESH,
        )

    def all_dp(q):
        part = (pl.ds(0, pairs * (n_dp - 1)), pl.ds(q * rows, rows))
        return pltpu.make_async_remote_copy(
            src_ref=stage.at[part],
            dst_ref=mid.at[part],
            send_sem=send1.at[q],
            recv_sem=recv1.at[q],
            device_id=(lax.rem(g + 1, n_dp), c),
            device_id_type=MESH,
        )

    def all_tp(q):
        part = pl.ds(0, (n_tp - 1) * rows)
        return pltpu.make_async_remote_copy(
            src_ref=out.at[part],
            dst_ref=out.at[part],
            send_sem=send2.at[q],
            recv_sem=recv2.at[q],
            device_id=(g, lax.rem(c + 1, n_tp)),
            device_id_type=MESH,
        )

    def own(q):
        return pltpu.make_async_copy(
            mid.at[c, pl.ds(q * rows, rows)], out.at[pl.ds(c * piece + q * rows, rows)], own_sem.at[q]
        )

    for q in range(chunks + 1):
        if q < chunks:
            sort(q)
            if q >= ahead:
                all_dp(q - ahead).wait_send()
            loop(1, n_dp, lambda i: over_dp(q, i, g).start())
        if q >= 1:
            all_dp(q - 1).wait_recv()
            loop(1, n_tp, lambda i: over_tp(q - 1, i, c).start())
            own(q - 1).start()
    for q in range(chunks):
        if q >= chunks - ahead:
            all_dp(q).wait_send()
        all_tp(q).wait_send()
        all_tp(q).wait_recv()
        own(q).wait()


def move(picked, old_cache, n_dp, n_tp, chunks=12, ahead=2):
    group_req, piece, width = old_cache.shape
    packed = (n_tp, piece, 2 * width)
    sems = pltpu.SemaphoreType.DMA
    return pl.pallas_call(
        functools.partial(move_kernel, n_dp, n_tp, chunks, ahead),
        out_shape=jax.ShapeDtypeStruct((piece * n_tp, 2 * width), old_cache.dtype),
        in_specs=[pl.BlockSpec(memory_space=pltpu.SMEM), pl.BlockSpec(memory_space=pl.ANY)],
        out_specs=pl.BlockSpec(memory_space=pl.ANY),
        scratch_shapes=[
            pltpu.VMEM(old_cache.shape, old_cache.dtype),
            pltpu.VMEM(packed, old_cache.dtype),
            pltpu.VMEM(packed, old_cache.dtype),
            sems,
            sems((chunks,)),
            sems((chunks,)),
            sems((chunks,)),
            sems((chunks,)),
            sems((chunks,)),
        ],
        compiler_params=pltpu.CompilerParams(collective_id=0, has_side_effects=True, vmem_limit_bytes=48 * 2**20),
    )(picked, old_cache)


score_scale = 0.07216878364870323
norm_eps = 1e-06


def attend_kernel(lens, main, tail, queries, new_main, new_tail, cache_out, lat, scores, query):
    f32, bf16 = jnp.float32, jnp.bfloat16
    item = pl.program_id(0)
    length = lens[item]
    context, rank = main.shape
    heads = queries.shape[3]
    both = 2 * heads
    query[:rank] = jnp.concatenate([queries[0, 0, :rank], queries[1, 0, :rank]], axis=1)
    query[rank:] = jnp.zeros((128, both), bf16)
    half = pl.multiple_of(rank + item * 64, 64)
    query[pl.ds(half, 64)] = jnp.concatenate([queries[0, 0, rank:], queries[1, 0, rank:]], axis=1)
    block = context // 2
    row = lax.broadcasted_iota(jnp.int32, (block, rank), 0)
    tail_row = lax.broadcasted_iota(jnp.int32, (block, 128), 0)
    tail_length = jnp.where(lax.broadcasted_iota(jnp.int32, (block, 128), 1) < 64, lens[0], lens[1])
    place = lax.broadcasted_iota(jnp.int32, (block, both), 0)
    last = length + lax.broadcasted_iota(jnp.int32, (block, both), 1) // heads

    def fill(old, position, size, first, second):
        new = jnp.where(position == size, first.astype(f32), jnp.where(position == size + 1, second.astype(f32), 0.0))
        return jnp.where(position < size, old.astype(f32), new).astype(bf16)

    def score(i, top):
        start = pl.multiple_of(i * block, block)
        rows = pl.ds(start, block)
        keys = fill(main[rows], row + start, length, new_main[0, item], new_main[1, item])
        tails = fill(tail[rows], tail_row + start, tail_length, new_tail[0], new_tail[1])
        cache_out[0, :rank, rows] = keys.T
        tails_t = tails.T

        @pl.when(item == 0)
        def _():
            cache_out[0, rank:, rows] = tails_t[:64]

        @pl.when(item == 1)
        def _():
            cache_out[0, rank:, rows] = tails_t[64:]

        both_parts = jnp.concatenate([keys, tails], axis=1)
        raw = jnp.dot(both_parts, query[...], preferred_element_type=f32)
        raw = jnp.where(place + start <= last, raw * score_scale, -jnp.inf)
        scores[rows] = raw
        return jnp.maximum(top, jnp.max(raw, axis=0, keepdims=True))

    top = lax.fori_loop(0, context // block, score, jnp.full((1, both), -jnp.inf, f32))
    exponent = jnp.exp(scores[...] - top)
    total = jnp.sum(exponent, axis=0, keepdims=True)
    mixed_t = jnp.dot(cache_out[0, :rank], exponent.astype(bf16), preferred_element_type=f32)
    mixed = (mixed_t / total).T
    mixed = mixed.reshape(2, lat.shape[0], -1, rank)
    mixed = jnp.concatenate([mixed[0], mixed[1]], axis=1).astype(bf16)
    lat[:, pl.ds(pl.multiple_of(item * 16, 16), 16)] = mixed


def attend(my_lengths, arrived, queries, new_latent, n_tp, kv_rank):
    context = arrived.shape[0]
    steps, items, heads, width = queries.shape
    bf16 = jnp.bfloat16
    new_tail = new_latent[:, :, kv_rank:].reshape(steps, 1, -1)
    flipped, latents = pl.pallas_call(
        attend_kernel,
        grid=(items,),
        out_shape=(
            jax.ShapeDtypeStruct((items, width, context), bf16),
            jax.ShapeDtypeStruct((n_tp, items * steps * heads // n_tp, kv_rank), bf16),
        ),
        in_specs=[
            pl.BlockSpec(memory_space=pltpu.SMEM),
            pl.BlockSpec((context, kv_rank), lambda i: (0, i)),
            pl.BlockSpec((context, 128), lambda i: (0, 2 * kv_rank // 128)),
            pl.BlockSpec((steps, 1, width, heads), lambda i: (0, i, 0, 0)),
            pl.BlockSpec((steps, items, 1, kv_rank), lambda i: (0, 0, 0, 0)),
            pl.BlockSpec((steps, 1, 128), lambda i: (0, 0, 0)),
        ],
        out_specs=(
            pl.BlockSpec((1, width, context), lambda i: (i, 0, 0)),
            pl.BlockSpec((n_tp, items * steps * heads // n_tp, kv_rank), lambda i: (0, 0, 0)),
        ),
        scratch_shapes=[
            pltpu.VMEM((context, steps * heads), jnp.float32),
            pltpu.VMEM((kv_rank + 128, steps * heads), bf16),
        ],
        compiler_params=pltpu.CompilerParams(vmem_limit_bytes=40 * 2**20),
    )(my_lengths, arrived, arrived, queries.transpose(0, 1, 3, 2), new_latent[:, :, None, :kv_rank], new_tail)
    return flipped.transpose(0, 2, 1), latents


def dense_kernel(
    lat,
    value_up,
    hidden,
    gain,
    w_out,
    w_gate,
    w_up,
    w_down,
    out,
    vup_v,
    wout_v,
    wgate_v,
    wup_v,
    wdown_v,
    latr,
    perm,
    xbuf,
    s3,
    r3,
    after,
    ybuf,
    gu,
    pair_s,
    pair_r,
    ring_s,
    ring_r,
    hbuf,
    wsem,
    lat_ss,
    lat_rs,
    x_ss,
    x_rs,
    s3_ss,
    s3_rs,
    y_ss,
    y_rs,
    pair_ss,
    pair_rs,
    ring_ss,
    ring_rs,
    h_ss,
    h_rs,
    s7_ss,
    s7_rs,
    o_ss,
    o_rs,
):
    f32, bf16 = jnp.float32, jnp.bfloat16
    g = lax.axis_index("dp")
    c = lax.axis_index("tp")
    y, k = g // 2, lax.rem(g, 2)
    z, x = c // 4, lax.rem(c, 4)
    sib = g + 1 - 2 * k
    ff = wgate_v.shape[1]
    width = 2 * ff

    def block_of(column):
        down = column // 4
        return 4 * lax.rem(lax.rem(column, 4) - down + 4, 4) + down

    mine = block_of(c)

    loads = []
    for n, (src, dst) in enumerate(
        ((value_up, vup_v), (w_out, wout_v), (w_gate, wgate_v), (w_up, wup_v), (w_down, wdown_v))
    ):
        loads.append(pltpu.make_async_copy(src, dst, wsem.at[n]))
        loads[-1].start()

    def remote(src, dst, send_sem, recv_sem, dp, tp):
        return pltpu.make_async_remote_copy(
            src_ref=src, dst_ref=dst, send_sem=send_sem, recv_sem=recv_sem, device_id=(dp, tp), device_id_type=MESH
        )

    barrier = pltpu.get_barrier_semaphore()
    loop(1, 16, lambda i: pl.semaphore_signal(barrier, 1, device_id=(g, lax.rem(c + i, 16)), device_id_type=MESH))
    loop(1, 4, lambda i: pl.semaphore_signal(barrier, 1, device_id=(lax.rem(g + 2 * i, 8), c), device_id_type=MESH))
    pl.semaphore_signal(barrier, 1, device_id=(sib, c), device_id_type=MESH)
    pl.semaphore_wait(barrier, 19)

    def lat_copy(i, source):
        to = lax.rem(c + i, 16)
        return remote(lat.at[to], latr.at[source], lat_ss, lat_rs, g, to)

    lat_all = remote(lat.at[pl.ds(0, 15)], latr.at[pl.ds(0, 15)], lat_ss, lat_rs, g, lax.rem(c + 1, 16))
    loop(1, 16, lambda i: lat_copy(i, c).start())
    latr[c] = lat[c]
    row = lax.broadcasted_iota(jnp.int32, (512, 512), 0)
    col = lax.broadcasted_iota(jnp.int32, (512, 512), 1)
    wanted = ((row & 31) >> 1) * 32 + (row & 1) * 16 + ((row >> 5) & 1) * 8 + (row >> 6)
    perm[...] = jnp.where(col == wanted, 1.0, 0.0).astype(bf16)
    lat_all.wait_recv()
    ordered = jnp.dot(perm[...], latr[...].reshape(512, 512), preferred_element_type=f32).astype(bf16)
    loads[0].wait()
    for head in range(8):
        part = jnp.dot(ordered[64 * head : 64 * head + 64], vup_v[head], preferred_element_type=f32)
        xbuf[0, g, :, 128 * head : 128 * head + 128] = part[:32].astype(bf16)
        xbuf[1, g, :, 128 * head : 128 * head + 128] = part[32:].astype(bf16)

    def gather_ring(buf, ss, rs, s, i, source):
        to = lax.rem(g + 2 * i, 8)
        return remote(buf.at[s, g], buf.at[s, source], ss.at[s, i], rs.at[s, source], to, c)

    def gather_pair(buf, ss, rs, s, i, sent, got):
        return remote(buf.at[s, sent], buf.at[s, got], ss.at[s, 4 + i], rs.at[s, got], sib, c)

    def gather_start(buf, ss, rs, s):
        loop(1, 4, lambda i: gather_ring(buf, ss, rs, s, i, g).start())
        gather_pair(buf, ss, rs, s, 0, g, g).start()

    def gather_rest(buf, ss, rs, s):
        def forward(i):
            src = lax.rem(g + 8 - 2 * i, 8)
            gather_ring(buf, ss, rs, s, i, src).wait_recv()
            gather_pair(buf, ss, rs, s, i, src, src).start()

        loop(1, 4, forward)
        loop(0, 4, lambda i: gather_pair(buf, ss, rs, s, i, g, lax.rem(sib + 8 - 2 * i, 8)).wait_recv())

    def gather_end(buf, ss, rs, s):
        loop(1, 4, lambda i: gather_ring(buf, ss, rs, s, i, g).wait_send())
        loop(0, 4, lambda i: gather_pair(buf, ss, rs, s, i, g, g).wait_send())

    def scatter_copy(ss, rs, s, i, source):
        to = lax.rem(c + i, 16)
        return remote(s3.at[s, block_of(to)], r3.at[s, source], ss.at[s], rs.at[s], g, to)

    def scatter_all(ss, rs, s):
        part = pl.ds(0, 15)
        return remote(s3.at[s, part], r3.at[s, part], ss.at[s], rs.at[s], g, lax.rem(c + 1, 16))

    def scatter(value, ss, rs, s):
        s3[s] = value.reshape(16, 16, value.shape[1]).astype(bf16)
        loop(1, 16, lambda i: scatter_copy(ss, rs, s, i, c).start())

    def scatter_sum(ss, rs, s, first):
        r3[s, c] = s3[s, mine]
        scatter_all(ss, rs, s).wait_recv()
        total = first + jnp.sum(r3[s].astype(f32), axis=0)
        scatter_all(ss, rs, s).wait_send()
        return total

    def spread(buf, ss, rs, s, i, source):
        to = lax.rem(c + i, 16)
        return remote(buf.at[s, mine], buf.at[s, block_of(source)], ss.at[s], rs.at[s], g, to)

    def spread_all(buf, ss, rs, s):
        part = pl.ds(0, 15)
        return remote(buf.at[s, part], buf.at[s, part], ss.at[s], rs.at[s], g, lax.rem(c + 1, 16))

    def spread_start(buf, ss, rs, s):
        loop(1, 16, lambda i: spread(buf, ss, rs, s, i, c).start())

    def spread_wait(buf, ss, rs, s):
        spread_all(buf, ss, rs, s).wait_recv()

    def spread_end(buf, ss, rs, s):
        spread_all(buf, ss, rs, s).wait_send()

    loop(0, 2, lambda s: gather_start(xbuf, x_ss, x_rs, s))
    loads[1].wait()

    def out_stage(s):
        gather_rest(xbuf, x_ss, x_rs, s)
        rows = xbuf[s].reshape(256, xbuf.shape[3])
        scatter(jnp.dot(rows, wout_v[...], preferred_element_type=f32), s3_ss, s3_rs, s)

    loop(0, 2, out_stage)

    def after_stage(s):
        after[s] = scatter_sum(s3_ss, s3_rs, s, hidden[s, mine].astype(f32))
        ybuf[s, mine] = after[s].astype(bf16)
        spread_start(ybuf, y_ss, y_rs, s)

    loop(0, 2, after_stage)
    loads[2].wait()
    loads[3].wait()
    lane = lax.broadcasted_iota(jnp.int32, (32, 128), 1)

    def two_part(total):
        high = total.astype(bf16)
        low = (total - high.astype(f32)).astype(bf16)
        return jnp.where(lane < 64, high.astype(f32), low.astype(f32)).astype(bf16)

    def one_part(pair):
        return pair[:, 0:1].astype(f32) + pair[:, 64:65].astype(f32)

    def pair_copy(s, chunk):
        return remote(pair_s.at[s, chunk], pair_r.at[s, chunk], pair_ss.at[s, chunk], pair_rs.at[s, chunk], sib, c)

    def ring_copy(s, chunk, source):
        return remote(
            ring_s.at[s, chunk], ring_r.at[s, source], ring_ss.at[s, chunk], ring_rs.at[s, source], 2 * chunk + k, c
        )

    def gate_stage(s):
        spread_wait(ybuf, y_ss, y_rs, s)
        rows = ybuf[s].reshape(256, ybuf.shape[3]).astype(f32)
        squares = jnp.sum(rows * rows, axis=1, keepdims=True)
        scaled = (rows * gain[...]).astype(bf16)
        gu[s, :, :, :, width : width + 128] = jnp.broadcast_to(squares, (256, 128)).reshape(4, 2, 32, 128)
        gu[s, :, :, :, 0:ff] = jnp.dot(scaled, wgate_v[...], preferred_element_type=f32).reshape(4, 2, 32, ff)
        gu[s, :, :, :, ff:width] = jnp.dot(scaled, wup_v[...], preferred_element_type=f32).reshape(4, 2, 32, ff)

        def give(i):
            chunk = lax.rem(y + 1 + i, 4)
            pair_s[s, chunk, :, 0:width] = gu[s, chunk, 1 - k, :, 0:width].astype(bf16)
            pair_s[s, chunk, :, width : width + 128] = two_part(gu[s, chunk, 1 - k, :, width : width + 128])
            pair_copy(s, chunk).start()

        loop(0, 4, give)

        def merge(i):
            chunk = lax.rem(y + 1 + i, 4)
            pair_copy(s, chunk).wait_recv()
            total = gu[s, chunk, k, :, 0:width] + pair_r[s, chunk, :, 0:width].astype(f32)
            squares = gu[s, chunk, k, :, width : width + 128] + one_part(pair_r[s, chunk, :, width : width + 128])
            gu[s, chunk, k, :, 0:width] = total
            gu[s, chunk, k, :, width : width + 128] = squares

            @pl.when(chunk != y)
            def _():
                ring_s[s, chunk, :, 0:width] = total.astype(bf16)
                ring_s[s, chunk, :, width : width + 128] = two_part(squares)
                ring_copy(s, chunk, y).start()

        loop(0, 4, merge)

    loop(0, 2, gate_stage)

    def act_stage(s):
        def ring_add(i):
            source = lax.rem(y + i, 4)
            ring_copy(s, source, source).wait_recv()
            gu[s, y, k, :, 0:width] += ring_r[s, source, :, 0:width].astype(f32)
            gu[s, y, k, :, width : width + 128] += one_part(ring_r[s, source, :, width : width + 128])

        loop(1, 4, ring_add)
        scale = 1.0 / jnp.sqrt(gu[s, y, k, :, width : width + 1] / D + norm_eps)
        gate = gu[s, y, k, :, 0:ff] * scale
        up = gu[s, y, k, :, ff:width] * scale
        hbuf[s, g] = (jax.nn.silu(gate) * up).astype(bf16)
        gather_start(hbuf, h_ss, h_rs, s)

    loop(0, 2, act_stage)
    loads[4].wait()

    def down_stage(s):
        gather_rest(hbuf, h_ss, h_rs, s)
        rows = hbuf[s].reshape(256, ff)
        scatter(jnp.dot(rows, wdown_v[...], preferred_element_type=f32), s7_ss, s7_rs, s)

    loop(0, 2, down_stage)

    def result_stage(s):
        out[s, mine] = scatter_sum(s7_ss, s7_rs, s, after[s]).astype(bf16)
        spread_start(out, o_ss, o_rs, s)

    loop(0, 2, result_stage)
    lat_all.wait_send()

    def end_stage(s):
        gather_end(xbuf, x_ss, x_rs, s)
        spread_end(ybuf, y_ss, y_rs, s)
        loop(0, 4, lambda i: pair_copy(s, i).wait_send())
        loop(1, 4, lambda i: ring_copy(s, lax.rem(y + i, 4), y).wait_send())
        gather_end(hbuf, h_ss, h_rs, s)
        spread_end(out, o_ss, o_rs, s)
        spread_wait(out, o_ss, o_rs, s)

    loop(0, 2, end_stage)


def dense(lat, value_up, hidden, gain, w_out, w_gate, w_up, w_down):
    steps, total, cols = hidden.shape
    ff = w_gate.shape[1]
    bf16, f32 = jnp.bfloat16, jnp.float32
    vmem, sems = pltpu.VMEM, pltpu.SemaphoreType.DMA
    in_vmem, anywhere = pl.BlockSpec(memory_space=pltpu.VMEM), pl.BlockSpec(memory_space=pl.ANY)
    result = pl.pallas_call(
        dense_kernel,
        out_shape=jax.ShapeDtypeStruct((steps, 16, 16, cols), bf16),
        in_specs=[in_vmem, anywhere, in_vmem, in_vmem, anywhere, anywhere, anywhere, anywhere],
        out_specs=in_vmem,
        scratch_shapes=[
            vmem(value_up.shape, bf16),
            vmem(w_out.shape, bf16),
            vmem(w_gate.shape, bf16),
            vmem(w_up.shape, bf16),
            vmem(w_down.shape, bf16),
            vmem(lat.shape, bf16),
            vmem((512, 512), bf16),
            vmem((2, 8, 32, w_out.shape[0]), bf16),
            vmem((2, 16, 16, cols), bf16),
            vmem((2, 16, 16, cols), bf16),
            vmem((2, 16, cols), f32),
            vmem((2, 16, 16, cols), bf16),
            vmem((2, 4, 2, 32, 2 * ff + 128), f32),
            vmem((2, 4, 32, 2 * ff + 128), bf16),
            vmem((2, 4, 32, 2 * ff + 128), bf16),
            vmem((2, 4, 32, 2 * ff + 128), bf16),
            vmem((2, 4, 32, 2 * ff + 128), bf16),
            vmem((2, 8, 32, ff), bf16),
            sems((5,)),
            sems,
            sems,
            sems((2, 8)),
            sems((2, 8)),
            sems((2,)),
            sems((2,)),
            sems((2,)),
            sems((2,)),
            sems((2, 4)),
            sems((2, 4)),
            sems((2, 4)),
            sems((2, 4)),
            sems((2, 8)),
            sems((2, 8)),
            sems((2,)),
            sems((2,)),
            sems((2,)),
            sems((2,)),
        ],
        compiler_params=pltpu.CompilerParams(collective_id=1, has_side_effects=True, vmem_limit_bytes=52 * 2**20),
    )(lat, value_up, hidden.reshape(steps, 16, 16, cols), gain, w_out, w_gate, w_up, w_down)
    return result.reshape(steps, total, cols)


def shards(
    old_cache,
    lengths,
    new_slot,
    queries,
    new_latent,
    hidden,
    value_up_weight,
    w_out,
    norm_gain,
    w_gate,
    w_up,
    w_down,
):
    dp_count = lax.axis_size("dp")
    tp_count = lax.axis_size("tp")
    my_group = lax.axis_index("dp")
    my_column = lax.axis_index("tp")
    group_req = old_cache.shape[0]
    per_pair = group_req // dp_count
    req_dev = queries.shape[1]
    req_total = new_slot.shape[0]
    kv_rank = value_up_weight.shape[1]
    everyone = jnp.arange(req_total, dtype=jnp.int32)
    order = jnp.arange(group_req, dtype=jnp.int32)
    out_slots = order // per_pair * group_req + my_group * per_pair + order % per_pair
    picked = jnp.sum(
        jnp.where(new_slot[None, :] == out_slots[:, None], everyone[None, :] % group_req, 0), axis=1
    )
    arrived = move(picked, old_cache, dp_count, tp_count)
    my_slots = (my_group * tp_count + my_column) * req_dev + jnp.arange(req_dev, dtype=jnp.int32)
    my_lengths = jnp.sum(jnp.where(new_slot[None, :] == my_slots[:, None], lengths[None, :], 0), axis=1)
    new_cache, latents = attend(my_lengths, arrived, queries, new_latent, tp_count, kv_rank)
    gain = norm_gain.astype(jnp.float32)[None, :]
    layer_out = dense(latents, value_up_weight, hidden, gain, w_out, w_gate, w_up, w_down)
    return (new_cache, layer_out)


def solution(mesh):
    in_specs = (
        P("dp", "tp", None),
        P(),
        P(),
        P(None, ("dp", "tp"), None, None),
        P(None, ("dp", "tp"), None),
        P(None, None, "dp"),
        P("tp", None, None),
        P("tp", "dp"),
        P("dp"),
        P("dp", "tp"),
        P("dp", "tp"),
        P("tp", "dp"),
    )
    out_specs = (P(("dp", "tp"), None, None), P(None, None, "dp"))
    return jax.shard_map(shards, mesh=mesh, in_specs=in_specs, out_specs=out_specs, check_vma=False)
```
